32 devices in a mesh: layer: 8 (over z, x), dp: 4 (over y, core).
Axes of the slice: x: 2, y: 2, z: 4, core: 2. Of those that a mesh axis runs over, the one named last changes fastest.
Arguments:
- state_guess: float32 [8, 4, 32, 256], P('layer', 'dp'), may hold values from -6 to 6
- adjoint_guess: float32 [8, 4, 32, 256], P('layer', 'dp'), may hold values from -6 to 6
- conv_weight: bfloat16 [32, 32, 288], P('layer'), may hold values from -0.375 to 0.375
- conv_bias: float32 [32, 32], P('layer'), may hold values from -3 to 3
Outputs:
- state_fixed: float32 [8, 4, 32, 256], P('layer', 'dp')
- adjoint_fixed: float32 [8, 4, 32, 256], P('layer', 'dp')
- weight_grad: float32 [32, 32, 288], P('layer', 'dp')
- bias_grad: float32 [32, 32], P('layer', 'dp')
The draws below stay inside these ranges and needn't reach their ends.
All inputs are finite; a program needn't handle non-finite values.
Results may differ from the reference program's by a relative error of at most 0.0071.
Values sent between devices are 32-bit elements; how exact they have to be, the bound alone decides.
No kernel may reach another device: no remote copies, remote signals or barrier semaphores. Data moves between devices by JAX's collectives and lax.ppermute only.
A program may use at most 64 MiB of HBM per device.

```python
import jax
import jax.numpy as jnp
from jax import lax

C = 32
IMG = 16
L_DEV = 4
HW = 256
BATCH = 4
LAYERS = 32
N_LAYER = 8


def level_of(own_key, extent, split, smallest, top_value):
    loudness, own = 1.0, jax.random.fold_in(own_key, 6)
    for axis_at, shards_of in split:
        draws = jnp.exp(jax.random.uniform(jax.random.fold_in(own, axis_at), (shards_of,), jnp.float32, smallest / len(split), top_value / len(split)))
        loudness = loudness * jnp.repeat(draws, extent[axis_at] // shards_of).reshape([-1 if axis == axis_at else 1 for axis in range(len(extent))])
    return loudness


def scatter_about(key, dims, scale, bound, split=(), dtype=jnp.bfloat16):
    loudness = level_of(key, dims, split, -0.22, 0.18) if split else 1.0
    values = jax.random.normal(key, dims, jnp.float32) * scale * loudness
    return jnp.minimum(jnp.maximum(values, -bound), bound).astype(dtype)


def setup_inputs(seed: int = 0) -> dict:
    key_list = jax.random.split(jax.random.key(seed), 5)
    return {
        "state_guess": scatter_about(key_list[0], (N_LAYER, BATCH, C, HW), 1.0, 6.0, ((0, 8), (1, 4)), jnp.float32),
        "adjoint_guess": scatter_about(key_list[1], (N_LAYER, BATCH, C, HW), 1.0, 6.0, ((0, 8), (1, 4)), jnp.float32),
        "conv_weight": scatter_about(key_list[2], (LAYERS, C, 9 * C), (9 * C) ** -0.5, 0.375, ((0, 8),)),
        "conv_bias": scatter_about(key_list[3], (LAYERS, C), 0.5, 3.0, ((0, 8),), jnp.float32),
    }


step_size = 0.5


def gather_taps(values):
    count = values.shape[0]
    grid = values.reshape(count, C, IMG, IMG)
    padded = jnp.pad(grid, ((0, 0), (0, 0), (1, 1), (1, 1)))
    taps = [padded[:, :, row:row + IMG, col:col + IMG] for row in range(3) for col in range(3)]
    return jnp.stack(taps, axis=2).reshape(count, C * 9, IMG * IMG)


def spread_taps(grads):
    count = grads.shape[0]
    grid = grads.reshape(count, C, 9, IMG, IMG)
    total = jnp.zeros((count, C, IMG + 2, IMG + 2), jnp.float32)
    for tap in range(9):
        row, col = tap // 3, tap % 3
        total = total + jnp.pad(grid[:, :, tap], ((0, 0), (0, 0), (row, 2 - row), (col, 2 - col)))
    return total[:, :, 1:-1, 1:-1].reshape(count, C, IMG * IMG)


def forward_block(state, weights, biases):
    gain = jnp.ones(state.shape, jnp.float32)
    saved = []
    for layer in range(L_DEV):
        kernel = weights[layer]
        rounded = state.astype(jnp.bfloat16)
        patch = gather_taps(rounded)
        pre = jnp.einsum("ok,bkp->bop", kernel.astype(jnp.float32), patch.astype(jnp.float32)) + biases[layer][None, :, None]
        squash = jnp.tanh(pre)
        center = jnp.diagonal(kernel.reshape(C, C, 9)[:, :, 4]).astype(jnp.float32)
        gain = gain * (1.0 + step_size * (1.0 - squash * squash) * center[None, :, None])
        state = state + step_size * squash
        saved.append((rounded, squash))
    return state, gain, saved


def backward_block(adjoint, weights, saved):
    wgrads = []
    bgrads = []
    for layer in reversed(range(L_DEV)):
        rounded, squash = saved[layer]
        kernel = weights[layer]
        dz = step_size * adjoint * (1.0 - squash * squash)
        dzb = dz.astype(jnp.bfloat16)
        back = jnp.einsum("ok,bop->bkp", kernel.astype(jnp.float32), dzb.astype(jnp.float32))
        adjoint = adjoint + spread_taps(back)
        wgrads.append(jnp.einsum("bop,bkp->ok", dzb.astype(jnp.float32), gather_taps(rounded).astype(jnp.float32)))
        bgrads.append(jnp.sum(dz, axis=(0, 2)))
    return adjoint, jnp.stack(wgrads[::-1]), jnp.stack(bgrads[::-1])


def relax_pair(items):
    state, adjoint, weights, biases = items
    final, gain, saved = forward_block(state, weights, biases)
    back, wgrad, bgrad = backward_block(adjoint, weights, saved)
    return final, gain, back


def grad_pass(items):
    state, adjoint, weights, biases = items
    final, gain, saved = forward_block(state, weights, biases)
    back, wgrad, bgrad = backward_block(adjoint, weights, saved)
    return wgrad, bgrad


def reference(state_guess, adjoint_guess, conv_weight, conv_bias):
    weights = conv_weight.reshape(N_LAYER, L_DEV, C, 9 * C)
    biases = conv_bias.reshape(N_LAYER, L_DEV, C)
    final, gain, back = lax.map(relax_pair, (state_guess, adjoint_guess, weights, biases))

    def forward_link(carry, items):
        gain_prev, final_prev, guess = items
        fresh = gain_prev * carry + final_prev - guess
        return fresh, fresh

    zero = jnp.zeros(state_guess.shape[1:], jnp.float32)
    _, fwd_err = lax.scan(forward_link, zero, (gain[:-1], final[:-1], state_guess[1:]))
    state_fixed = jnp.concatenate([state_guess[:1], state_guess[1:] + fwd_err], axis=0)
    _, bwd_err = lax.scan(forward_link, zero, (gain[1:], back[1:], adjoint_guess[:-1]), reverse=True)
    adjoint_fixed = jnp.concatenate([adjoint_guess[:-1] + bwd_err, adjoint_guess[-1:]], axis=0)
    wgrad, bgrad = lax.map(grad_pass, (state_guess, adjoint_fixed, weights, biases))
    return state_fixed, adjoint_fixed, wgrad.reshape(LAYERS, C, 9 * C), bgrad.reshape(LAYERS, C)
```

```python
import functools

import jax
import jax.numpy as jnp
from jax import lax
from jax.experimental import pallas as pl
from jax.experimental.pallas import tpu as pltpu
from jax.sharding import PartitionSpec as P

IMG = 16
HW = IMG * IMG
HALF = 128
TAPS = 9
STEP = 0.5
LIMIT = 32 * 1024 * 1024

VMEM = pl.BlockSpec(memory_space=pltpu.VMEM)


def offset_of(tap):
    return (tap // 3 - 1) * IMG + (tap % 3 - 1)


def inside(shape, down, right):
    pixel = lax.broadcasted_iota(jnp.int32, shape, 1)
    col = lax.rem(pixel, IMG)
    ok = None
    for test in (
        (pixel >= IMG) if down < 0 else None,
        (pixel < HW - IMG) if down > 0 else None,
        (col >= 1) if right < 0 else None,
        (col < IMG - 1) if right > 0 else None,
    ):
        if test is not None:
            ok = test if ok is None else jnp.logical_and(ok, test)
    return ok


def taps_of(values):
    out = []
    for tap in range(TAPS):
        by = offset_of(tap)
        if by == 0:
            out.append(values)
            continue
        ok = inside(values.shape, tap // 3 - 1, tap % 3 - 1)
        out.append(jnp.where(ok, pltpu.roll(values, (-by) % HW, 1), 0.0))
    return out


def spread(rows, chans):
    total = None
    for tap in range(TAPS):
        by = offset_of(tap)
        part = rows[tap * chans : (tap + 1) * chans]
        if by != 0:
            ok = inside(part.shape, 1 - tap // 3, 1 - tap % 3)
            part = jnp.where(ok, pltpu.roll(part, by % HW, 1), 0.0)
        total = part if total is None else total + part
    return total


def permutation(chans):
    size = TAPS * chans
    src = lax.broadcasted_iota(jnp.int32, (size, size), 0)
    dst = lax.broadcasted_iota(jnp.int32, (size, size), 1)
    tap = lax.div(dst, chans)
    return jnp.where(src == (dst - tap * chans) * TAPS + tap, 1.0, 0.0).astype(jnp.bfloat16)


def dot(a, b, dims):
    return lax.dot_general(a, b, (dims, ((), ())), preferred_element_type=jnp.float32)


def relax_kernel(state_ref, adj_ref, w_ref, bias_ref, sent_ref, slope_ref, patch_ref, back_w_ref):
    depth, chans, width = w_ref.shape
    perm = permutation(chans)
    start = state_ref[0, 0]
    guess = adj_ref[0, 0]
    row = lax.broadcasted_iota(jnp.int32, (chans, width), 0)
    lane = lax.broadcasted_iota(jnp.int32, (chans, width), 1)
    center = lane == row * TAPS + TAPS // 2
    eye = lax.broadcasted_iota(jnp.int32, (chans, chans), 0) == lax.broadcasted_iota(
        jnp.int32, (chans, chans), 1
    )
    state = start
    gain = None
    slopes = []
    for n in range(depth):
        weight = w_ref[n]
        kc = jnp.sum(jnp.where(center, weight.astype(jnp.float32), 0.0), axis=1, keepdims=True)
        bias = jnp.sum(
            jnp.where(eye, jnp.broadcast_to(bias_ref[n : n + 1, :], (chans, chans)), 0.0),
            axis=1,
            keepdims=True,
        )
        by_tap = dot(weight, perm, ((1,), (0,))).astype(jnp.bfloat16)
        back_w_ref[n] = dot(perm, weight, ((0,), (1,))).astype(jnp.bfloat16)
        rounded = state.astype(jnp.bfloat16).astype(jnp.float32)
        patch = jnp.concatenate([t.astype(jnp.bfloat16) for t in taps_of(rounded)], axis=0)
        patch_ref[n] = dot(perm, patch, ((1,), (0,))).astype(jnp.bfloat16)
        squash = jnp.tanh(dot(by_tap, patch, ((1,), (0,))) + bias)
        slope = STEP * (1.0 - squash * squash)
        factor = 1.0 + slope * kc
        gain = factor if gain is None else gain * factor
        state = state + STEP * squash
        slope_ref[n] = slope
        slopes.append(slope)
    back = guess
    for n in reversed(range(depth)):
        dzb = (back * slopes[n]).astype(jnp.bfloat16)
        back = back + spread(dot(back_w_ref[n], dzb, ((1,), (0,))), chans)
    place = lax.axis_index("layer")
    first = jnp.where(place == 0, 0.0, start)
    last = jnp.where(place == lax.axis_size("layer") - 1, 0.0, guess)
    for k, value in enumerate((gain, back - gain * last, state - gain * first)):
        put_parts(sent_ref, k, value)


def put_parts(ref, k, value):
    chans = value.shape[0]
    for half in range(HW // HALF):
        piece = value[:, half * HALF : (half + 1) * HALF]
        if len(ref.shape) == 3:
            ref[k, half * chans : (half + 1) * chans, :] = piece
        else:
            for part in range(chans // 8):
                ref[half * (chans // 8) + part, k] = piece[part * 8 : part * 8 + 8]


def get_parts(ref, k, chans):
    if len(ref.shape) == 3:
        halves = [ref[k, h * chans : (h + 1) * chans, :] for h in range(HW // HALF)]
    else:
        parts = chans // 8
        halves = [
            jnp.concatenate([ref[h * parts + p, k] for p in range(parts)], axis=0)
            for h in range(HW // HALF)
        ]
    return jnp.concatenate(halves, axis=1)


def scan_kernel(ref, out_ref):
    count = ref.shape[0]
    out_ref[0, 1] = jnp.zeros(ref.shape[2:], jnp.float32)
    out_ref[count - 1, 0] = jnp.zeros(ref.shape[2:], jnp.float32)
    adj = ref[count - 1, 1]
    for j in reversed(range(count - 1)):
        out_ref[j, 0] = adj
        if j:
            adj = ref[j, 0] * adj + ref[j, 1]
    state = ref[0, 2]
    for j in range(1, count):
        out_ref[j, 1] = state
        state = ref[j, 0] * state + ref[j, 2]


def grad_kernel(
    shares,
    fixed_ref,
    guess_ref,
    start_ref,
    slope_ref,
    patch_ref,
    back_w_ref,
    adj_ref,
    state_ref,
    out_ref,
):
    depth, rows, _ = back_w_ref.shape
    chans = rows // TAPS
    own = chans // shares
    place = lax.axis_index("layer")
    last = place == lax.axis_size("layer") - 1
    adj = jnp.where(last, guess_ref[0, 0], get_parts(fixed_ref, 0, chans))
    adj_ref[0, 0] = adj
    state_ref[0, 0] = jnp.where(place == 0, start_ref[0, 0], get_parts(fixed_ref, 1, chans))
    pad = out_ref.shape[2] - rows
    for n in reversed(range(depth)):
        dz = adj * slope_ref[n]
        dzb = dz.astype(jnp.bfloat16)
        grad = dot(dzb, patch_ref[n], ((1,), (1,)))
        bias = jnp.broadcast_to(jnp.sum(dz, axis=1, keepdims=True), (chans, pad))
        for s in range(shares):
            out_ref[s, n * own : (n + 1) * own, :rows] = grad[s * own : (s + 1) * own]
            out_ref[s, n * own : (n + 1) * own, rows:] = bias[s * own : (s + 1) * own]
        if n:
            adj = adj + spread(dot(back_w_ref[n], dzb, ((1,), (0,))), chans)


def total_kernel(ref, grad_ref, bias_ref):
    depth, own, width = grad_ref.shape
    total = ref[0]
    for s in range(1, ref.shape[0]):
        total = total + ref[s]
    eye = lax.broadcasted_iota(jnp.int32, (own, own), 0) == lax.broadcasted_iota(
        jnp.int32, (own, own), 1
    )
    for n in range(depth):
        mine = total[n * own : (n + 1) * own]
        grad_ref[n] = mine[:, :width]
        column = jnp.broadcast_to(mine[:, width : width + 1], (own, own))
        bias_ref[n : n + 1, :] = jnp.sum(jnp.where(eye, column, 0.0), axis=0, keepdims=True)


def call(kernel, out_shape, args):
    many = isinstance(out_shape, (list, tuple))
    return pl.pallas_call(
        kernel,
        out_shape=out_shape,
        in_specs=[VMEM] * len(args),
        out_specs=[VMEM] * len(out_shape) if many else VMEM,
        compiler_params=pltpu.CompilerParams(vmem_limit_bytes=LIMIT),
    )(*args)


def f32(*shape):
    return jax.ShapeDtypeStruct(shape, jnp.float32)


def bf16(*shape):
    return jax.ShapeDtypeStruct(shape, jnp.bfloat16)


def swap(x, axis):
    return lax.all_to_all(x, axis, 0, 0, tiled=True)


def local(state_guess, adjoint_guess, conv_weight, conv_bias):
    depth, chans, width = conv_weight.shape
    blocks = lax.axis_size("layer")
    shares = lax.axis_size("dp")
    rows = HW // HALF * chans
    tiled = rows == 8 * blocks
    items = 3
    sent, slope, patch, back_w = call(
        relax_kernel,
        (
            f32(blocks, items, 8, HALF) if tiled else f32(items, rows, HALF),
            f32(depth, chans, HW),
            bf16(depth, width, HW),
            bf16(depth, width, chans),
        ),
        (state_guess, adjoint_guess, conv_weight, conv_bias),
    )
    if not tiled:
        sent = jnp.moveaxis(sent.reshape(items, blocks, 1, rows * HALF // blocks), 0, 1)
    got = swap(sent, "layer")
    fixed = call(scan_kernel, f32(blocks, 2, *got.shape[2:]), (got,))
    fixed = swap(fixed, "layer")
    if not tiled:
        fixed = jnp.moveaxis(fixed, 1, 0).reshape(2, rows, HALF)
    lanes = -(-(width + 1) // HALF) * HALF
    adjoint_fixed, state_fixed, parts = call(
        functools.partial(grad_kernel, shares),
        (
            f32(*adjoint_guess.shape),
            f32(*state_guess.shape),
            f32(shares, depth * chans // shares, lanes),
        ),
        (fixed, adjoint_guess, state_guess, slope, patch, back_w),
    )
    weight_grad, bias_grad = call(
        total_kernel,
        (f32(depth, chans // shares, width), f32(depth, chans // shares)),
        (swap(parts, "dp"),),
    )
    return (state_fixed, adjoint_fixed, weight_grad, bias_grad)


def solution(mesh):
    placed = (
        P("layer", "dp", None, None),
        P("layer", "dp", None, None),
        P("layer", None, None),
        P("layer", None),
    )
    return jax.shard_map(
        local,
        mesh=mesh,
        in_specs=placed,
        out_specs=(
            P("layer", "dp", None, None),
            P("layer", "dp", None, None),
            P("layer", "dp", None),
            P("layer", "dp"),
        ),
        check_vma=False,
    )
```

```python
import functools

import jax
import jax.numpy as jnp
from jax import lax
from jax.experimental import pallas as pl
from jax.experimental.pallas import tpu as pltpu
from jax.sharding import PartitionSpec as P

IMG = 16
HW = IMG * IMG
HALF = 128
TAPS = 9
STEP = 0.5
LIMIT = 32 * 1024 * 1024

VMEM = pl.BlockSpec(memory_space=pltpu.VMEM)
HBM = pl.BlockSpec(memory_space=pltpu.HBM)


def offset_of(tap):
    return (tap // 3 - 1) * IMG + (tap % 3 - 1)


def inside(shape, down, right):
    pixel = lax.broadcasted_iota(jnp.int32, shape, 1)
    col = lax.rem(pixel, IMG)
    ok = None
    for test in (
        (pixel >= IMG) if down < 0 else None,
        (pixel < HW - IMG) if down > 0 else None,
        (col >= 1) if right < 0 else None,
        (col < IMG - 1) if right > 0 else None,
    ):
        if test is not None:
            ok = test if ok is None else jnp.logical_and(ok, test)
    return ok


def taps_of(values):
    out = []
    for tap in range(TAPS):
        by = offset_of(tap)
        if by == 0:
            out.append(values)
            continue
        ok = inside(values.shape, tap // 3 - 1, tap % 3 - 1)
        out.append(jnp.where(ok, pltpu.roll(values, (-by) % HW, 1), 0.0))
    return out


def spread(rows, chans):
    total = None
    for tap in range(TAPS):
        by = offset_of(tap)
        part = rows[tap * chans : (tap + 1) * chans]
        if by != 0:
            ok = inside(part.shape, 1 - tap // 3, 1 - tap % 3)
            part = jnp.where(ok, pltpu.roll(part, by % HW, 1), 0.0)
        total = part if total is None else total + part
    return total


def permutation(chans):
    size = TAPS * chans
    src = lax.broadcasted_iota(jnp.int32, (size, size), 0)
    dst = lax.broadcasted_iota(jnp.int32, (size, size), 1)
    tap = lax.div(dst, chans)
    return jnp.where(src == (dst - tap * chans) * TAPS + tap, 1.0, 0.0).astype(jnp.bfloat16)


def dot(a, b, dims):
    return lax.dot_general(a, b, (dims, ((), ())), preferred_element_type=jnp.float32)


def relax_kernel(
    state_hbm,
    adj_hbm,
    w_hbm,
    bias_hbm,
    sent_ref,
    slope_ref,
    patch_ref,
    back_w_ref,
    state_ref,
    adj_ref,
    w_ref,
    bias_ref,
    sems,
):
    copies = [
        pltpu.make_async_copy(src, dst, sems.at[k])
        for k, (src, dst) in enumerate(
            ((w_hbm, w_ref), (state_hbm, state_ref), (bias_hbm, bias_ref), (adj_hbm, adj_ref))
        )
    ]
    for copy in copies:
        copy.start()
    depth, chans, width = w_ref.shape
    perm = permutation(chans)
    for copy in copies:
        copy.wait()
    start = state_ref[0, 0]
    guess = adj_ref[0, 0]
    row = lax.broadcasted_iota(jnp.int32, (chans, width), 0)
    lane = lax.broadcasted_iota(jnp.int32, (chans, width), 1)
    center = lane == row * TAPS + TAPS // 2
    eye = lax.broadcasted_iota(jnp.int32, (chans, chans), 0) == lax.broadcasted_iota(
        jnp.int32, (chans, chans), 1
    )
    state = start
    gain = None
    slopes = []
    for n in range(depth):
        weight = w_ref[n]
        kc = jnp.sum(jnp.where(center, weight.astype(jnp.float32), 0.0), axis=1, keepdims=True)
        bias = jnp.sum(
            jnp.where(eye, jnp.broadcast_to(bias_ref[n : n + 1, :], (chans, chans)), 0.0),
            axis=1,
            keepdims=True,
        )
        by_tap = dot(weight, perm, ((1,), (0,))).astype(jnp.bfloat16)
        back_w_ref[n] = dot(perm, weight, ((0,), (1,))).astype(jnp.bfloat16)
        rounded = state.astype(jnp.bfloat16).astype(jnp.float32)
        patch = jnp.concatenate([t.astype(jnp.bfloat16) for t in taps_of(rounded)], axis=0)
        patch_ref[n] = dot(perm, patch, ((1,), (0,))).astype(jnp.bfloat16)
        squash = jnp.tanh(dot(by_tap, patch, ((1,), (0,))) + bias)
        slope = STEP * (1.0 - squash * squash)
        factor = 1.0 + slope * kc
        gain = factor if gain is None else gain * factor
        state = state + STEP * squash
        slope_ref[n] = slope
        slopes.append(slope)
    back = guess
    for n in reversed(range(depth)):
        dzb = (back * slopes[n]).astype(jnp.bfloat16)
        back = back + spread(dot(back_w_ref[n], dzb, ((1,), (0,))), chans)
    place = lax.axis_index("layer")
    first = jnp.where(place == 0, 0.0, start)
    last = jnp.where(place == lax.axis_size("layer") - 1, 0.0, guess)
    sent_ref[0] = gain
    sent_ref[1] = state - gain * first
    sent_ref[2] = back - gain * last


def joined(bit, total, mine, got):
    gain, fwd, bwd = total
    pre_gain, pre, post_gain, post = mine
    got_gain, got_fwd, got_bwd = got
    total = (
        gain * got_gain,
        jnp.where(bit, gain * got_fwd + fwd, got_gain * fwd + got_fwd),
        jnp.where(bit, got_gain * bwd + got_bwd, gain * got_bwd + bwd),
    )
    mine = (
        jnp.where(bit, pre_gain * got_gain, pre_gain),
        jnp.where(bit, pre_gain * got_fwd + pre, pre),
        jnp.where(bit, post_gain, post_gain * got_gain),
        jnp.where(bit, post, post_gain * got_bwd + post),
    )
    return total, mine


def bit_of(axis, step):
    return lax.rem(lax.div(lax.axis_index(axis), 2**step), 2) == 1


def join_kernel(step, final, *refs):
    if step == 1:
        total_ref, got_ref, sent_ref, mine_out = refs
        one = jnp.ones(total_ref.shape[1:], jnp.float32)
        zero = jnp.zeros(total_ref.shape[1:], jnp.float32)
        mine = (one, zero, one, zero)
    else:
        total_ref, got_ref, mine_ref, sent_ref, mine_out = refs
        mine = tuple(mine_ref[k] for k in range(4))
    total = tuple(total_ref[k] for k in range(3))
    got = tuple(got_ref[k] for k in range(3))
    total, mine = joined(bit_of("layer", step - 1), total, mine, got)
    for k in range(4):
        mine_out[k] = mine[k]
    if final:
        sent_ref[...] = jnp.where(bit_of("layer", step), total[2], total[1])
    else:
        for k in range(3):
            sent_ref[k] = total[k]


def grad_kernel(
    steps,
    got_ref,
    mine_ref,
    guess_ref,
    start_ref,
    slope_ref,
    patch_ref,
    back_w_ref,
    adj_hbm,
    state_hbm,
    keep_ref,
    send_ref,
    adj_ref,
    state_ref,
    sems,
):
    depth, rows, _ = back_w_ref.shape
    chans = rows // TAPS
    shares = 2 * keep_ref.shape[0]
    own = chans // shares
    place = lax.axis_index("layer")
    upper = bit_of("layer", steps - 1)
    got = got_ref[...]
    fixed = jnp.where(upper, mine_ref[1] + mine_ref[0] * got, mine_ref[1])
    state_ref[0, 0] = jnp.where(place == 0, start_ref[0, 0], fixed)
    fixed = jnp.where(upper, mine_ref[3], mine_ref[3] + mine_ref[2] * got)
    adj = jnp.where(place == lax.axis_size("layer") - 1, guess_ref[0, 0], fixed)
    adj_ref[0, 0] = adj
    copies = [
        pltpu.make_async_copy(src, dst, sems.at[k])
        for k, (src, dst) in enumerate(((adj_ref, adj_hbm), (state_ref, state_hbm)))
    ]
    for copy in copies:
        copy.start()
    pad = keep_ref.shape[2] - rows
    odd = bit_of("dp", 0)
    for n in reversed(range(depth)):
        dz = adj * slope_ref[n]
        dzb = dz.astype(jnp.bfloat16)
        grad = dot(dzb, patch_ref[n], ((1,), (1,)))
        bias = jnp.broadcast_to(jnp.sum(dz, axis=1, keepdims=True), (chans, pad))
        both = jnp.concatenate([grad, bias], axis=1)
        for s in range(shares // 2):
            even_part = both[2 * s * own : (2 * s + 1) * own]
            odd_part = both[(2 * s + 1) * own : (2 * s + 2) * own]
            keep_ref[s, n * own : (n + 1) * own] = jnp.where(odd, odd_part, even_part)
            send_ref[s, n * own : (n + 1) * own] = jnp.where(odd, even_part, odd_part)
        if n:
            adj = adj + spread(dot(back_w_ref[n], dzb, ((1,), (0,))), chans)
    for copy in copies:
        copy.wait()


def halve_kernel(step, mine_ref, got_ref, keep_ref, send_ref):
    odd = bit_of("dp", step)
    for s in range(keep_ref.shape[0]):
        even_part = mine_ref[2 * s] + got_ref[2 * s]
        odd_part = mine_ref[2 * s + 1] + got_ref[2 * s + 1]
        keep_ref[s] = jnp.where(odd, odd_part, even_part)
        send_ref[s] = jnp.where(odd, even_part, odd_part)


def total_kernel(mine_ref, got_ref, grad_ref, bias_ref):
    depth, own, width = grad_ref.shape
    total = mine_ref[0] + got_ref[0]
    eye = lax.broadcasted_iota(jnp.int32, (own, own), 0) == lax.broadcasted_iota(
        jnp.int32, (own, own), 1
    )
    for n in range(depth):
        mine = total[n * own : (n + 1) * own]
        grad_ref[n] = mine[:, :width]
        column = jnp.broadcast_to(mine[:, width : width + 1], (own, own))
        bias_ref[n : n + 1, :] = jnp.sum(jnp.where(eye, column, 0.0), axis=0, keepdims=True)


def call(kernel, out_shape, args, hbm_in=(), hbm_out=(), scratch=()):
    return pl.pallas_call(
        kernel,
        out_shape=out_shape,
        in_specs=[HBM if k in hbm_in else VMEM for k in range(len(args))],
        out_specs=[HBM if k in hbm_out else VMEM for k in range(len(out_shape))],
        scratch_shapes=list(scratch),
        compiler_params=pltpu.CompilerParams(vmem_limit_bytes=LIMIT),
    )(*(pltpu.with_memory_space_constraint(a, pltpu.HBM) if k in hbm_in else a for k, a in enumerate(args)))


def f32(*shape):
    return jax.ShapeDtypeStruct(shape, jnp.float32)


def bf16(*shape):
    return jax.ShapeDtypeStruct(shape, jnp.bfloat16)


def exchange(x, axis, step):
    pairs = [(i, i ^ (1 << step)) for i in range(lax.axis_size(axis))]
    return lax.ppermute(x, axis, pairs)


def local(state_guess, adjoint_guess, conv_weight, conv_bias):
    depth, chans, width = conv_weight.shape
    shares = lax.axis_size("dp")
    steps = lax.axis_size("layer").bit_length() - 1
    args = (state_guess, adjoint_guess, conv_weight, conv_bias)
    total, slope, patch, back_w = call(
        relax_kernel,
        (
            f32(3, chans, HW),
            f32(depth, chans, HW),
            bf16(depth, width, HW),
            bf16(depth, width, chans),
        ),
        args,
        hbm_in=range(4),
        scratch=[pltpu.VMEM(a.shape, a.dtype) for a in args] + [pltpu.SemaphoreType.DMA((4,))],
    )
    mine = ()
    for step in range(1, steps):
        got = exchange(total, "layer", step - 1)
        final = step == steps - 1
        total, *mine = call(
            functools.partial(join_kernel, step, final),
            (f32(chans, HW) if final else f32(3, chans, HW), f32(4, chans, HW)),
            (total, got, *mine),
        )
    got = exchange(total, "layer", steps - 1)
    lanes = -(-(width + 1) // HALF) * HALF
    part = (depth * chans // shares, lanes)
    guess = pltpu.VMEM(adjoint_guess.shape, jnp.float32)
    adjoint_fixed, state_fixed, keep, send = call(
        functools.partial(grad_kernel, steps),
        (
            f32(*adjoint_guess.shape),
            f32(*state_guess.shape),
            f32(shares // 2, *part),
            f32(shares // 2, *part),
        ),
        (got, *mine, adjoint_guess, state_guess, slope, patch, back_w),
        hbm_out=(0, 1),
        scratch=[guess, guess, pltpu.SemaphoreType.DMA((2,))],
    )
    left = shares // 2
    step = 0
    while left > 1:
        left //= 2
        step += 1
        keep, send = call(
            functools.partial(halve_kernel, step),
            (f32(left, *part), f32(left, *part)),
            (keep, exchange(send, "dp", step - 1)),
        )
    weight_grad, bias_grad = call(
        total_kernel,
        (f32(depth, chans // shares, width), f32(depth, chans // shares)),
        (keep, exchange(send, "dp", step)),
    )
    return (state_fixed, adjoint_fixed, weight_grad, bias_grad)


def solution(mesh):
    placed = (
        P("layer", "dp", None, None),
        P("layer", "dp", None, None),
        P("layer", None, None),
        P("layer", None),
    )
    return jax.shard_map(
        local,
        mesh=mesh,
        in_specs=placed,
        out_specs=(
            P("layer", "dp", None, None),
            P("layer", "dp", None, None),
            P("layer", "dp", None),
            P("layer", "dp"),
        ),
        check_vma=False,
    )
```

```python
import functools

import jax
import jax.numpy as jnp
from jax import lax
from jax.experimental import pallas as pl
from jax.experimental.pallas import tpu as pltpu
from jax.sharding import PartitionSpec as P

IMG = 16
HW = IMG * IMG
HALF = 128
TAPS = 9
STEP = 0.5
LIMIT = 32 * 1024 * 1024

VMEM = pl.BlockSpec(memory_space=pltpu.VMEM)
HBM = pl.BlockSpec(memory_space=pltpu.HBM)


def taps_of(values):
    pixel = lax.broadcasted_iota(jnp.int16, values.shape, 1)
    col = pixel & (IMG - 1)
    rows = {-1: pixel >= IMG, 1: pixel < HW - IMG}
    cols = {-1: col >= 1, 1: col < IMG - 1}
    out = []
    for tap in range(TAPS):
        down, right = tap // 3 - 1, tap % 3 - 1
        part = values
        if down or right:
            part = pltpu.roll(values, -(down * IMG + right) % HW, 1)
            tests = [rows[down]] if down else []
            tests += [cols[right]] if right else []
            part = jnp.where(functools.reduce(jnp.logical_and, tests), part, jnp.zeros_like(part))
        out.append(part)
    return jnp.concatenate(out, axis=0)


def permutation(chans):
    size = TAPS * chans
    src = lax.broadcasted_iota(jnp.int32, (size, size), 0)
    dst = lax.broadcasted_iota(jnp.int32, (size, size), 1)
    tap = lax.div(dst, chans)
    return jnp.where(src == (dst - tap * chans) * TAPS + tap, 1.0, 0.0).astype(jnp.bfloat16)


def dot(a, b, dims):
    return lax.dot_general(a, b, (dims, ((), ())), preferred_element_type=jnp.float32)


def relax_kernel(
    state_hbm,
    adj_hbm,
    w_hbm,
    bias_hbm,
    sent_ref,
    slope_ref,
    rounded_ref,
    back_w_ref,
    state_ref,
    adj_ref,
    w_ref,
    bias_ref,
    sems,
):
    copies = [
        pltpu.make_async_copy(src, dst, sems.at[k])
        for k, (src, dst) in enumerate(
            ((w_hbm, w_ref), (state_hbm, state_ref), (bias_hbm, bias_ref), (adj_hbm, adj_ref))
        )
    ]
    for copy in copies:
        copy.start()
    depth, chans, width = w_ref.shape
    perm = permutation(chans)
    for copy in copies:
        copy.wait()
    start = state_ref[0, 0]
    guess = adj_ref[0, 0]
    row = lax.broadcasted_iota(jnp.int32, (chans, width), 0)
    lane = lax.broadcasted_iota(jnp.int32, (chans, width), 1)
    center = lane == row * TAPS + TAPS // 2
    eye = lax.broadcasted_iota(jnp.int32, (chans, chans), 0) == lax.broadcasted_iota(
        jnp.int32, (chans, chans), 1
    )
    state = start
    gain = None
    slopes = []
    for n in range(depth):
        weight = w_ref[n]
        kc = jnp.sum(jnp.where(center, weight.astype(jnp.float32), 0.0), axis=1, keepdims=True)
        bias = jnp.sum(
            jnp.where(eye, jnp.broadcast_to(bias_ref[n : n + 1, :], (chans, chans)), 0.0),
            axis=1,
            keepdims=True,
        )
        by_tap = dot(weight, perm, ((1,), (0,))).astype(jnp.bfloat16)
        turned = dot(perm, weight, ((0,), (1,))).astype(jnp.bfloat16)
        back_w_ref[n] = jnp.concatenate(
            [turned[t * chans : (t + 1) * chans] for t in reversed(range(TAPS))], axis=1
        )
        rounded = state.astype(jnp.bfloat16)
        rounded_ref[n] = rounded
        squash = jnp.tanh(dot(by_tap, taps_of(rounded), ((1,), (0,))) + bias)
        slope = STEP * (1.0 - squash * squash)
        factor = 1.0 + slope * kc
        gain = factor if gain is None else gain * factor
        state = state + STEP * squash
        slope_ref[n] = slope
        slopes.append(slope)
    back = guess
    for n in reversed(range(depth)):
        dzb = (back * slopes[n]).astype(jnp.bfloat16)
        back = back + dot(back_w_ref[n], taps_of(dzb), ((1,), (0,)))
    place = lax.axis_index("layer")
    first = jnp.where(place == 0, 0.0, start)
    last = jnp.where(place == lax.axis_size("layer") - 1, 0.0, guess)
    sent_ref[0] = gain
    sent_ref[1] = state - gain * first
    sent_ref[2] = back - gain * last


def patch_kernel(rounded_ref, patch_ref):
    depth, chans, _ = rounded_ref.shape
    perm = permutation(chans)
    for n in range(depth):
        patch_ref[n] = dot(perm, taps_of(rounded_ref[n]), ((1,), (0,))).astype(jnp.bfloat16)


def joined(bit, total, mine, got):
    gain, fwd, bwd = total
    pre_gain, pre, post_gain, post = mine
    got_gain, got_fwd, got_bwd = got
    total = (
        gain * got_gain,
        jnp.where(bit, gain * got_fwd + fwd, got_gain * fwd + got_fwd),
        jnp.where(bit, got_gain * bwd + got_bwd, gain * got_bwd + bwd),
    )
    mine = (
        jnp.where(bit, pre_gain * got_gain, pre_gain),
        jnp.where(bit, pre_gain * got_fwd + pre, pre),
        jnp.where(bit, post_gain, post_gain * got_gain),
        jnp.where(bit, post, post_gain * got_bwd + post),
    )
    return total, mine


def bit_of(axis, step):
    return lax.rem(lax.div(lax.axis_index(axis), 2**step), 2) == 1


def join_kernel(step, final, *refs):
    if step == 1:
        total_ref, got_ref, sent_ref, mine_out = refs
        one = jnp.ones(total_ref.shape[1:], jnp.float32)
        zero = jnp.zeros(total_ref.shape[1:], jnp.float32)
        mine = (one, zero, one, zero)
    else:
        total_ref, got_ref, mine_ref, sent_ref, mine_out = refs
        mine = tuple(mine_ref[k] for k in range(4))
    total = tuple(total_ref[k] for k in range(3))
    got = tuple(got_ref[k] for k in range(3))
    total, mine = joined(bit_of("layer", step - 1), total, mine, got)
    for k in range(4):
        mine_out[k] = mine[k]
    if final:
        sent_ref[...] = jnp.where(bit_of("layer", step), total[2], total[1])
    else:
        for k in range(3):
            sent_ref[k] = total[k]


def grad_kernel(
    steps,
    got_ref,
    mine_ref,
    guess_ref,
    start_ref,
    slope_ref,
    patch_ref,
    back_w_ref,
    adj_hbm,
    state_hbm,
    keep_ref,
    send_ref,
    adj_ref,
    state_ref,
    sems,
):
    depth, chans, rows = back_w_ref.shape
    shares = 2 * keep_ref.shape[0]
    own = chans // shares
    place = lax.axis_index("layer")
    upper = bit_of("layer", steps - 1)
    got = got_ref[...]
    fixed = jnp.where(upper, mine_ref[1] + mine_ref[0] * got, mine_ref[1])
    state_ref[0, 0] = jnp.where(place == 0, start_ref[0, 0], fixed)
    fixed = jnp.where(upper, mine_ref[3], mine_ref[3] + mine_ref[2] * got)
    adj = jnp.where(place == lax.axis_size("layer") - 1, guess_ref[0, 0], fixed)
    adj_ref[0, 0] = adj
    copies = [
        pltpu.make_async_copy(src, dst, sems.at[k])
        for k, (src, dst) in enumerate(((adj_ref, adj_hbm), (state_ref, state_hbm)))
    ]
    for copy in copies:
        copy.start()
    pad = keep_ref.shape[2] - rows
    odd = bit_of("dp", 0)
    for n in reversed(range(depth)):
        dz = adj * slope_ref[n]
        dzb = dz.astype(jnp.bfloat16)
        grad = dot(dzb, patch_ref[n], ((1,), (1,)))
        bias = jnp.broadcast_to(jnp.sum(dz, axis=1, keepdims=True), (chans, pad))
        both = jnp.concatenate([grad, bias], axis=1)
        for s in range(shares // 2):
            even_part = both[2 * s * own : (2 * s + 1) * own]
            odd_part = both[(2 * s + 1) * own : (2 * s + 2) * own]
            keep_ref[s, n * own : (n + 1) * own] = jnp.where(odd, odd_part, even_part)
            send_ref[s, n * own : (n + 1) * own] = jnp.where(odd, even_part, odd_part)
        if n:
            adj = adj + dot(back_w_ref[n], taps_of(dzb), ((1,), (0,)))
    for copy in copies:
        copy.wait()


def halve_kernel(step, mine_ref, got_ref, keep_ref, send_ref):
    odd = bit_of("dp", step)
    for s in range(keep_ref.shape[0]):
        even_part = mine_ref[2 * s] + got_ref[2 * s]
        odd_part = mine_ref[2 * s + 1] + got_ref[2 * s + 1]
        keep_ref[s] = jnp.where(odd, odd_part, even_part)
        send_ref[s] = jnp.where(odd, even_part, odd_part)


def total_kernel(mine_ref, got_ref, grad_ref, bias_ref):
    depth, own, width = grad_ref.shape
    total = mine_ref[0] + got_ref[0]
    eye = lax.broadcasted_iota(jnp.int32, (own, own), 0) == lax.broadcasted_iota(
        jnp.int32, (own, own), 1
    )
    for n in range(depth):
        mine = total[n * own : (n + 1) * own]
        grad_ref[n] = mine[:, :width]
        column = jnp.broadcast_to(mine[:, width : width + 1], (own, own))
        bias_ref[n : n + 1, :] = jnp.sum(jnp.where(eye, column, 0.0), axis=0, keepdims=True)


def call(kernel, out_shape, args, hbm_in=(), hbm_out=(), scratch=()):
    return pl.pallas_call(
        kernel,
        out_shape=out_shape,
        in_specs=[HBM if k in hbm_in else VMEM for k in range(len(args))],
        out_specs=[HBM if k in hbm_out else VMEM for k in range(len(out_shape))],
        scratch_shapes=list(scratch),
        compiler_params=pltpu.CompilerParams(vmem_limit_bytes=LIMIT),
        cost_estimate=pl.CostEstimate(flops=2**28, bytes_accessed=2**20, transcendentals=0),
    )(*(pltpu.with_memory_space_constraint(a, pltpu.HBM) if k in hbm_in else a for k, a in enumerate(args)))


def f32(*shape):
    return jax.ShapeDtypeStruct(shape, jnp.float32)


def bf16(*shape):
    return jax.ShapeDtypeStruct(shape, jnp.bfloat16)


def exchange(x, axis, step):
    pairs = [(i, i ^ (1 << step)) for i in range(lax.axis_size(axis))]
    return lax.ppermute(x, axis, pairs)


def local(state_guess, adjoint_guess, conv_weight, conv_bias):
    depth, chans, width = conv_weight.shape
    shares = lax.axis_size("dp")
    steps = lax.axis_size("layer").bit_length() - 1
    args = (state_guess, adjoint_guess, conv_weight, conv_bias)
    total, slope, rounded, back_w = call(
        relax_kernel,
        (
            f32(3, chans, HW),
            f32(depth, chans, HW),
            bf16(depth, chans, HW),
            bf16(depth, chans, width),
        ),
        args,
        hbm_in=range(4),
        scratch=[pltpu.VMEM(a.shape, a.dtype) for a in args] + [pltpu.SemaphoreType.DMA((4,))],
    )
    (patch,) = call(patch_kernel, (bf16(depth, width, HW),), (rounded,))
    mine = ()
    for step in range(1, steps):
        got = exchange(total, "layer", step - 1)
        final = step == steps - 1
        total, *mine = call(
            functools.partial(join_kernel, step, final),
            (f32(chans, HW) if final else f32(3, chans, HW), f32(4, chans, HW)),
            (total, got, *mine),
        )
    got = exchange(total, "layer", steps - 1)
    lanes = -(-(width + 1) // HALF) * HALF
    part = (depth * chans // shares, lanes)
    guess = pltpu.VMEM(adjoint_guess.shape, jnp.float32)
    adjoint_fixed, state_fixed, keep, send = call(
        functools.partial(grad_kernel, steps),
        (
            f32(*adjoint_guess.shape),
            f32(*state_guess.shape),
            f32(shares // 2, *part),
            f32(shares // 2, *part),
        ),
        (got, *mine, adjoint_guess, state_guess, slope, patch, back_w),
        hbm_out=(0, 1),
        scratch=[guess, guess, pltpu.SemaphoreType.DMA((2,))],
    )
    left = shares // 2
    step = 0
    while left > 1:
        left //= 2
        step += 1
        keep, send = call(
            functools.partial(halve_kernel, step),
            (f32(left, *part), f32(left, *part)),
            (keep, exchange(send, "dp", step - 1)),
        )
    weight_grad, bias_grad = call(
        total_kernel,
        (f32(depth, chans // shares, width), f32(depth, chans // shares)),
        (keep, exchange(send, "dp", step)),
    )
    return (state_fixed, adjoint_fixed, weight_grad, bias_grad)


def solution(mesh):
    placed = (
        P("layer", "dp", None, None),
        P("layer", "dp", None, None),
        P("layer", None, None),
        P("layer", None),
    )
    return jax.shard_map(
        local,
        mesh=mesh,
        in_specs=placed,
        out_specs=(
            P("layer", "dp", None, None),
            P("layer", "dp", None, None),
            P("layer", "dp", None),
            P("layer", "dp"),
        ),
        check_vma=False,
    )
```

```python
import functools

import jax
import jax.numpy as jnp
from jax import lax
from jax.experimental import pallas as pl
from jax.experimental.pallas import tpu as pltpu
from jax.sharding import PartitionSpec as P

IMG = 16
HW = IMG * IMG
HALF = 128
TAPS = 9
STEP = 0.5
LIMIT = 32 * 1024 * 1024

VMEM = pl.BlockSpec(memory_space=pltpu.VMEM)
HBM = pl.BlockSpec(memory_space=pltpu.HBM)


def shifts(values):
    pixel = lax.broadcasted_iota(jnp.int16, values.shape, 1)
    col = pixel & (IMG - 1)
    rows = {-1: pixel >= IMG, 1: pixel < HW - IMG}
    cols = {-1: col >= 1, 1: col < IMG - 1}
    out = []
    for tap in range(TAPS):
        down, right = tap // 3 - 1, tap % 3 - 1
        if not down and not right:
            continue
        part = pltpu.roll(values, -(down * IMG + right) % HW, 1)
        tests = [rows[down]] if down else []
        tests += [cols[right]] if right else []
        part = jnp.where(functools.reduce(jnp.logical_and, tests), part, jnp.zeros_like(part))
        out.append(part)
    return out


def permutation(chans):
    size = TAPS * chans
    row = lax.broadcasted_iota(jnp.int32, (size, size), 0)
    column = lax.broadcasted_iota(jnp.int32, (size, size), 1)
    block = lax.div(row, chans)
    chan = row - block * chans
    tap = jnp.where(block == TAPS - 1, TAPS // 2, block + jnp.where(block >= TAPS // 2, 1, 0))
    return jnp.where(column == chan * TAPS + tap, 1.0, 0.0).astype(jnp.bfloat16)


def dot(a, b, dims):
    return lax.dot_general(a, b, (dims, ((), ())), preferred_element_type=jnp.float32)


def convolve(weight, values):
    chans = values.shape[0]
    half = (TAPS // 2) * chans
    near = shifts(values)
    return (
        dot(weight[:, 2 * half :], values, ((1,), (0,)))
        + dot(weight[:, :half], jnp.concatenate(near[: TAPS // 2], axis=0), ((1,), (0,)))
        + dot(weight[:, half : 2 * half], jnp.concatenate(near[TAPS // 2 :], axis=0), ((1,), (0,)))
    )


def relax_kernel(
    state_hbm,
    adj_hbm,
    w_hbm,
    bias_hbm,
    sent_ref,
    slope_ref,
    rounded_ref,
    back_w_ref,
    state_ref,
    adj_ref,
    w_ref,
    bias_ref,
    sems,
):
    copies = [
        pltpu.make_async_copy(src, dst, sems.at[k])
        for k, (src, dst) in enumerate(
            ((w_hbm, w_ref), (state_hbm, state_ref), (bias_hbm, bias_ref), (adj_hbm, adj_ref))
        )
    ]
    for copy in copies:
        copy.start()
    depth, chans, width = w_ref.shape
    perm = permutation(chans)
    for copy in copies:
        copy.wait()
    start = state_ref[0, 0]
    guess = adj_ref[0, 0]
    row = lax.broadcasted_iota(jnp.int32, (chans, width), 0)
    lane = lax.broadcasted_iota(jnp.int32, (chans, width), 1)
    center = lane == row * TAPS + TAPS // 2
    eye = lax.broadcasted_iota(jnp.int32, (chans, chans), 0) == lax.broadcasted_iota(
        jnp.int32, (chans, chans), 1
    )
    weights = w_ref[...].reshape(depth * chans, width)
    by_tap = dot(weights, perm, ((1,), (1,))).astype(jnp.bfloat16)
    turned = dot(perm, weights, ((1,), (1,))).astype(jnp.bfloat16)
    state = start
    gain = None
    slopes = []
    backs = []
    for n in range(depth):
        mine = slice(n * chans, (n + 1) * chans)
        kc = jnp.sum(
            jnp.where(center, w_ref[n].astype(jnp.float32), 0.0), axis=1, keepdims=True
        )
        bias = jnp.sum(
            jnp.where(eye, jnp.broadcast_to(bias_ref[n : n + 1, :], (chans, chans)), 0.0),
            axis=1,
            keepdims=True,
        )
        order = list(reversed(range(TAPS - 1))) + [TAPS - 1]
        backs.append(
            jnp.concatenate([turned[t * chans : (t + 1) * chans, mine] for t in order], axis=1)
        )
        back_w_ref[n] = backs[n]
        rounded = state.astype(jnp.bfloat16)
        rounded_ref[n] = rounded
        squash = jnp.tanh(convolve(by_tap[mine], rounded) + bias)
        slope = STEP * (1.0 - squash * squash)
        factor = 1.0 + slope * kc
        gain = factor if gain is None else gain * factor
        state = state + STEP * squash
        slope_ref[n] = slope
        slopes.append(slope)
    back = guess
    for n in reversed(range(depth)):
        dzb = (back * slopes[n]).astype(jnp.bfloat16)
        back = back + convolve(backs[n], dzb)
    place = lax.axis_index("layer")
    first = jnp.where(place == 0, 0.0, start)
    last = jnp.where(place == lax.axis_size("layer") - 1, 0.0, guess)
    sent_ref[0] = gain
    sent_ref[1] = state - gain * first
    sent_ref[2] = back - gain * last


def patch_kernel(rounded_ref, patch_ref):
    depth, chans, _ = rounded_ref.shape
    perm = permutation(chans)
    for n in range(depth):
        rounded = rounded_ref[n]
        patch = jnp.concatenate(shifts(rounded) + [rounded], axis=0)
        patch_ref[n] = dot(perm, patch, ((0,), (0,))).astype(jnp.bfloat16)


def joined(bit, total, mine, got):
    gain, fwd, bwd = total
    pre_gain, pre, post_gain, post = mine
    got_gain, got_fwd, got_bwd = got
    total = (
        gain * got_gain,
        jnp.where(bit, gain * got_fwd + fwd, got_gain * fwd + got_fwd),
        jnp.where(bit, got_gain * bwd + got_bwd, gain * got_bwd + bwd),
    )
    mine = (
        jnp.where(bit, pre_gain * got_gain, pre_gain),
        jnp.where(bit, pre_gain * got_fwd + pre, pre),
        jnp.where(bit, post_gain, post_gain * got_gain),
        jnp.where(bit, post, post_gain * got_bwd + post),
    )
    return total, mine


def bit_of(axis, step):
    return lax.rem(lax.div(lax.axis_index(axis), 2**step), 2) == 1


def join_kernel(step, final, *refs):
    if step == 1:
        total_ref, got_ref, sent_ref, mine_out = refs
        one = jnp.ones(total_ref.shape[1:], jnp.float32)
        zero = jnp.zeros(total_ref.shape[1:], jnp.float32)
        mine = (one, zero, one, zero)
    else:
        total_ref, got_ref, mine_ref, sent_ref, mine_out = refs
        mine = tuple(mine_ref[k] for k in range(4))
    total = tuple(total_ref[k] for k in range(3))
    got = tuple(got_ref[k] for k in range(3))
    total, mine = joined(bit_of("layer", step - 1), total, mine, got)
    for k in range(4):
        mine_out[k] = mine[k]
    if final:
        sent_ref[...] = jnp.where(bit_of("layer", step), total[2], total[1])
    else:
        for k in range(3):
            sent_ref[k] = total[k]


def grad_kernel(
    steps,
    got_ref,
    mine_ref,
    guess_ref,
    start_ref,
    slope_ref,
    patch_ref,
    back_w_ref,
    adj_hbm,
    state_hbm,
    keep_ref,
    send_ref,
    adj_ref,
    state_ref,
    sems,
):
    depth, chans, rows = back_w_ref.shape
    shares = 2 * keep_ref.shape[0]
    own = chans // shares
    place = lax.axis_index("layer")
    upper = bit_of("layer", steps - 1)
    got = got_ref[...]
    fixed = jnp.where(upper, mine_ref[1] + mine_ref[0] * got, mine_ref[1])
    state_ref[0, 0] = jnp.where(place == 0, start_ref[0, 0], fixed)
    fixed = jnp.where(upper, mine_ref[3], mine_ref[3] + mine_ref[2] * got)
    adj = jnp.where(place == lax.axis_size("layer") - 1, guess_ref[0, 0], fixed)
    adj_ref[0, 0] = adj
    copies = [
        pltpu.make_async_copy(src, dst, sems.at[k])
        for k, (src, dst) in enumerate(((adj_ref, adj_hbm), (state_ref, state_hbm)))
    ]
    for copy in copies:
        copy.start()
    pad = keep_ref.shape[2] - rows
    odd, high = bit_of("dp", 0), bit_of("dp", 1)
    for n in reversed(range(depth)):
        dz = adj * slope_ref[n]
        dzb = dz.astype(jnp.bfloat16)
        grad = dot(dzb, patch_ref[n], ((1,), (1,)))
        bias = jnp.broadcast_to(jnp.sum(dz, axis=1, keepdims=True), (chans, pad))
        both = jnp.concatenate([grad, bias], axis=1)
        parts = [both[s * own : (s + 1) * own] for s in range(shares)]
        parts = [jnp.where(odd, parts[i ^ 1], parts[i]) for i in range(shares)]
        parts = [jnp.where(high, parts[i ^ 2], parts[i]) for i in range(shares)]
        where = slice(n * own, (n + 1) * own)
        keep_ref[0, where], keep_ref[1, where] = parts[0], parts[3]
        send_ref[0, where], send_ref[1, where] = parts[1], parts[2]
        if n:
            adj = adj + convolve(back_w_ref[n], dzb)
    for copy in copies:
        copy.wait()


def halve_kernel(mine_ref, got_ref, keep_ref, send_ref):
    keep_ref[...] = mine_ref[0] + got_ref[0]
    send_ref[...] = mine_ref[1] + got_ref[1]


def total_kernel(mine_ref, got_ref, grad_ref, bias_ref):
    depth, own, width = grad_ref.shape
    total = mine_ref[...] + got_ref[...]
    eye = lax.broadcasted_iota(jnp.int32, (own, own), 0) == lax.broadcasted_iota(
        jnp.int32, (own, own), 1
    )
    for n in range(depth):
        mine = total[n * own : (n + 1) * own]
        grad_ref[n] = mine[:, :width]
        column = jnp.broadcast_to(mine[:, width : width + 1], (own, own))
        bias_ref[n : n + 1, :] = jnp.sum(jnp.where(eye, column, 0.0), axis=0, keepdims=True)


def call(kernel, out_shape, args, hbm_in=(), hbm_out=(), scratch=()):
    return pl.pallas_call(
        kernel,
        out_shape=out_shape,
        in_specs=[HBM if k in hbm_in else VMEM for k in range(len(args))],
        out_specs=[HBM if k in hbm_out else VMEM for k in range(len(out_shape))],
        scratch_shapes=list(scratch),
        compiler_params=pltpu.CompilerParams(vmem_limit_bytes=LIMIT),
        cost_estimate=pl.CostEstimate(flops=2**28, bytes_accessed=2**20, transcendentals=0),
    )(*(pltpu.with_memory_space_constraint(a, pltpu.HBM) if k in hbm_in else a for k, a in enumerate(args)))


def f32(*shape):
    return jax.ShapeDtypeStruct(shape, jnp.float32)


def bf16(*shape):
    return jax.ShapeDtypeStruct(shape, jnp.bfloat16)


def exchange(x, axis, mask):
    return lax.ppermute(x, axis, [(i, i ^ mask) for i in range(lax.axis_size(axis))])


def local(state_guess, adjoint_guess, conv_weight, conv_bias):
    depth, chans, width = conv_weight.shape
    shares = lax.axis_size("dp")
    steps = lax.axis_size("layer").bit_length() - 1
    args = (state_guess, adjoint_guess, conv_weight, conv_bias)
    total, slope, rounded, back_w = call(
        relax_kernel,
        (
            f32(3, chans, HW),
            f32(depth, chans, HW),
            bf16(depth, chans, HW),
            bf16(depth, chans, width),
        ),
        args,
        hbm_in=range(4),
        scratch=[pltpu.VMEM(a.shape, a.dtype) for a in args] + [pltpu.SemaphoreType.DMA((4,))],
    )
    (patch,) = call(patch_kernel, (bf16(depth, width, HW),), (rounded,))
    mine = ()
    for step in range(1, steps):
        got = exchange(total, "layer", 1 << (step - 1))
        final = step == steps - 1
        total, *mine = call(
            functools.partial(join_kernel, step, final),
            (f32(chans, HW) if final else f32(3, chans, HW), f32(4, chans, HW)),
            (total, got, *mine),
        )
    got = exchange(total, "layer", 1 << (steps - 1))
    lanes = -(-(width + 1) // HALF) * HALF
    part = (depth * chans // shares, lanes)
    guess = pltpu.VMEM(adjoint_guess.shape, jnp.float32)
    adjoint_fixed, state_fixed, keep, send = call(
        functools.partial(grad_kernel, steps),
        (
            f32(*adjoint_guess.shape),
            f32(*state_guess.shape),
            f32(shares // 2, *part),
            f32(shares // 2, *part),
        ),
        (got, *mine, adjoint_guess, state_guess, slope, patch, back_w),
        hbm_out=(0, 1),
        scratch=[guess, guess, pltpu.SemaphoreType.DMA((2,))],
    )
    keep, send = call(halve_kernel, (f32(*part), f32(*part)), (keep, exchange(send, "dp", 1)))
    weight_grad, bias_grad = call(
        total_kernel,
        (f32(depth, chans // shares, width), f32(depth, chans // shares)),
        (keep, exchange(send, "dp", 3)),
    )
    return (state_fixed, adjoint_fixed, weight_grad, bias_grad)


def solution(mesh):
    placed = (
        P("layer", "dp", None, None),
        P("layer", "dp", None, None),
        P("layer", None, None),
        P("layer", None),
    )
    return jax.shard_map(
        local,
        mesh=mesh,
        in_specs=placed,
        out_specs=(
            P("layer", "dp", None, None),
            P("layer", "dp", None, None),
            P("layer", "dp", None),
            P("layer", "dp"),
        ),
        check_vma=False,
    )
```

```python
import functools

import jax
import jax.numpy as jnp
from jax import lax
from jax.experimental import pallas as pl
from jax.experimental.pallas import tpu as pltpu
from jax.sharding import PartitionSpec as P

IMG = 16
HW = IMG * IMG
HALF = 128
TAPS = 9
STEP = 0.5
LIMIT = 32 * 1024 * 1024

VMEM = pl.BlockSpec(memory_space=pltpu.VMEM)
HBM = pl.BlockSpec(memory_space=pltpu.HBM)


def moved(values, down, right):
    if not down and not right:
        return values
    kind = jnp.int16 if values.dtype == jnp.bfloat16 else jnp.int32
    pixel = lax.broadcasted_iota(kind, values.shape, 1)
    col = pixel & (IMG - 1)
    tests = {-1: [pixel >= IMG], 0: [], 1: [pixel < HW - IMG]}[down]
    tests = tests + {-1: [col >= 1], 0: [], 1: [col < IMG - 1]}[right]
    part = pltpu.roll(values, -(down * IMG + right) % HW, 1)
    return jnp.where(functools.reduce(jnp.logical_and, tests), part, jnp.zeros_like(part))


def permutation(chans):
    size = TAPS * chans
    row = lax.broadcasted_iota(jnp.int32, (size, size), 0)
    column = lax.broadcasted_iota(jnp.int32, (size, size), 1)
    tap = lax.div(row, chans)
    return jnp.where(column == (row - tap * chans) * TAPS + tap, 1.0, 0.0).astype(jnp.bfloat16)


def dot(a, b, dims):
    return lax.dot_general(a, b, (dims, ((), ())), preferred_element_type=jnp.float32)


def convolve(weight, values):
    chans = values.shape[0]
    columns = jnp.concatenate([moved(values, 0, right) for right in (-1, 0, 1)], axis=0)
    rows = dot(weight, columns, ((1,), (0,)))
    return (
        rows[chans : 2 * chans]
        + moved(rows[:chans], -1, 0)
        + moved(rows[2 * chans :], 1, 0)
    )


def relax_kernel(
    state_hbm,
    adj_hbm,
    w_hbm,
    bias_hbm,
    sent_ref,
    slope_ref,
    rounded_ref,
    back_w_ref,
    state_ref,
    adj_ref,
    w_ref,
    bias_ref,
    sems,
):
    copies = [
        pltpu.make_async_copy(src, dst, sems.at[k])
        for k, (src, dst) in enumerate(
            ((w_hbm, w_ref), (state_hbm, state_ref), (bias_hbm, bias_ref), (adj_hbm, adj_ref))
        )
    ]
    for copy in copies:
        copy.start()
    depth, chans, width = w_ref.shape
    perm = permutation(chans)
    for copy in copies:
        copy.wait()
    start = state_ref[0, 0]
    guess = adj_ref[0, 0]
    row = lax.broadcasted_iota(jnp.int32, (chans, width), 0)
    lane = lax.broadcasted_iota(jnp.int32, (chans, width), 1)
    center = lane == row * TAPS + TAPS // 2
    eye = lax.broadcasted_iota(jnp.int32, (chans, chans), 0) == lax.broadcasted_iota(
        jnp.int32, (chans, chans), 1
    )
    weights = w_ref[...].reshape(depth * chans, width)
    by_tap = dot(weights, perm, ((1,), (1,))).astype(jnp.bfloat16)
    turned = dot(perm, weights, ((1,), (1,))).astype(jnp.bfloat16)
    state = start
    gain = None
    slopes = []
    backs = []
    for n in range(depth):
        mine = slice(n * chans, (n + 1) * chans)
        kc = jnp.sum(
            jnp.where(center, w_ref[n].astype(jnp.float32), 0.0), axis=1, keepdims=True
        )
        bias = jnp.sum(
            jnp.where(eye, jnp.broadcast_to(bias_ref[n : n + 1, :], (chans, chans)), 0.0),
            axis=1,
            keepdims=True,
        )
        blocks = [turned[t * chans : (t + 1) * chans, mine] for t in reversed(range(TAPS))]
        backs.append(
            jnp.concatenate(
                [jnp.concatenate(blocks[3 * a : 3 * a + 3], axis=1) for a in range(3)], axis=0
            )
        )
        back_w_ref[n] = backs[n]
        span = 3 * chans
        ahead = jnp.concatenate(
            [by_tap[mine, a * span : (a + 1) * span] for a in range(3)], axis=0
        )
        rounded = state.astype(jnp.bfloat16)
        rounded_ref[n] = rounded
        squash = jnp.tanh(convolve(ahead, rounded) + bias)
        slope = STEP * (1.0 - squash * squash)
        factor = 1.0 + slope * kc
        gain = factor if gain is None else gain * factor
        state = state + STEP * squash
        slope_ref[n] = slope
        slopes.append(slope)
    back = guess
    for n in reversed(range(depth)):
        dzb = (back * slopes[n]).astype(jnp.bfloat16)
        back = back + convolve(backs[n], dzb)
    place = lax.axis_index("layer")
    first = jnp.where(place == 0, 0.0, start)
    last = jnp.where(place == lax.axis_size("layer") - 1, 0.0, guess)
    sent_ref[0] = gain
    sent_ref[1] = state - gain * first
    sent_ref[2] = back - gain * last


def patch_kernel(rounded_ref, patch_ref):
    depth, chans, _ = rounded_ref.shape
    perm = permutation(chans)
    for n in range(depth):
        rounded = rounded_ref[n]
        patch = jnp.concatenate(
            [moved(rounded, tap // 3 - 1, tap % 3 - 1) for tap in range(TAPS)], axis=0
        )
        patch_ref[n] = dot(perm, patch, ((0,), (0,))).astype(jnp.bfloat16)


def joined(bit, total, mine, got):
    gain, fwd, bwd = total
    pre_gain, pre, post_gain, post = mine
    got_gain, got_fwd, got_bwd = got
    total = (
        gain * got_gain,
        jnp.where(bit, gain * got_fwd + fwd, got_gain * fwd + got_fwd),
        jnp.where(bit, got_gain * bwd + got_bwd, gain * got_bwd + bwd),
    )
    mine = (
        jnp.where(bit, pre_gain * got_gain, pre_gain),
        jnp.where(bit, pre_gain * got_fwd + pre, pre),
        jnp.where(bit, post_gain, post_gain * got_gain),
        jnp.where(bit, post, post_gain * got_bwd + post),
    )
    return total, mine


def bit_of(axis, step):
    return lax.rem(lax.div(lax.axis_index(axis), 2**step), 2) == 1


def join_kernel(step, final, *refs):
    if step == 1:
        total_ref, got_ref, sent_ref, mine_out = refs
        one = jnp.ones(total_ref.shape[1:], jnp.float32)
        zero = jnp.zeros(total_ref.shape[1:], jnp.float32)
        mine = (one, zero, one, zero)
    else:
        total_ref, got_ref, mine_ref, sent_ref, mine_out = refs
        mine = tuple(mine_ref[k] for k in range(4))
    total = tuple(total_ref[k] for k in range(3))
    got = tuple(got_ref[k] for k in range(3))
    total, mine = joined(bit_of("layer", step - 1), total, mine, got)
    for k in range(4):
        mine_out[k] = mine[k]
    if final:
        sent_ref[...] = jnp.where(bit_of("layer", step), total[2], total[1])
    else:
        for k in range(3):
            sent_ref[k] = total[k]


def grad_kernel(
    steps,
    got_ref,
    mine_ref,
    guess_ref,
    start_ref,
    slope_ref,
    patch_ref,
    back_w_ref,
    adj_hbm,
    state_hbm,
    keep_ref,
    send_ref,
    adj_ref,
    state_ref,
    sems,
):
    depth, rows, _ = patch_ref.shape
    chans = rows // TAPS
    shares = 2 * keep_ref.shape[0]
    own = chans // shares
    place = lax.axis_index("layer")
    upper = bit_of("layer", steps - 1)
    got = got_ref[...]
    fixed = jnp.where(upper, mine_ref[1] + mine_ref[0] * got, mine_ref[1])
    state_ref[0, 0] = jnp.where(place == 0, start_ref[0, 0], fixed)
    fixed = jnp.where(upper, mine_ref[3], mine_ref[3] + mine_ref[2] * got)
    adj = jnp.where(place == lax.axis_size("layer") - 1, guess_ref[0, 0], fixed)
    adj_ref[0, 0] = adj
    copies = [
        pltpu.make_async_copy(src, dst, sems.at[k])
        for k, (src, dst) in enumerate(((adj_ref, adj_hbm), (state_ref, state_hbm)))
    ]
    for copy in copies:
        copy.start()
    pad = keep_ref.shape[2] - rows
    odd, high = bit_of("dp", 0), bit_of("dp", 1)
    for n in reversed(range(depth)):
        dz = adj * slope_ref[n]
        dzb = dz.astype(jnp.bfloat16)
        grad = dot(dzb, patch_ref[n], ((1,), (1,)))
        bias = jnp.broadcast_to(jnp.sum(dz, axis=1, keepdims=True), (chans, pad))
        both = jnp.concatenate([grad, bias], axis=1)
        parts = [both[s * own : (s + 1) * own] for s in range(shares)]
        parts = [jnp.where(odd, parts[i ^ 1], parts[i]) for i in range(shares)]
        parts = [jnp.where(high, parts[i ^ 2], parts[i]) for i in range(shares)]
        where = slice(n * own, (n + 1) * own)
        keep_ref[0, where], keep_ref[1, where] = parts[0], parts[3]
        send_ref[0, where], send_ref[1, where] = parts[1], parts[2]
        if n:
            adj = adj + convolve(back_w_ref[n], dzb)
    for copy in copies:
        copy.wait()


def halve_kernel(mine_ref, got_ref, keep_ref, send_ref):
    keep_ref[...] = mine_ref[0] + got_ref[0]
    send_ref[...] = mine_ref[1] + got_ref[1]


def total_kernel(mine_ref, got_ref, grad_ref, bias_ref):
    depth, own, width = grad_ref.shape
    total = mine_ref[...] + got_ref[...]
    eye = lax.broadcasted_iota(jnp.int32, (own, own), 0) == lax.broadcasted_iota(
        jnp.int32, (own, own), 1
    )
    for n in range(depth):
        mine = total[n * own : (n + 1) * own]
        grad_ref[n] = mine[:, :width]
        column = jnp.broadcast_to(mine[:, width : width + 1], (own, own))
        bias_ref[n : n + 1, :] = jnp.sum(jnp.where(eye, column, 0.0), axis=0, keepdims=True)


def call(kernel, out_shape, args, hbm_in=(), hbm_out=(), scratch=()):
    return pl.pallas_call(
        kernel,
        out_shape=out_shape,
        in_specs=[HBM if k in hbm_in else VMEM for k in range(len(args))],
        out_specs=[HBM if k in hbm_out else VMEM for k in range(len(out_shape))],
        scratch_shapes=list(scratch),
        compiler_params=pltpu.CompilerParams(vmem_limit_bytes=LIMIT),
        cost_estimate=pl.CostEstimate(flops=2**28, bytes_accessed=2**20, transcendentals=0),
    )(*(pltpu.with_memory_space_constraint(a, pltpu.HBM) if k in hbm_in else a for k, a in enumerate(args)))


def f32(*shape):
    return jax.ShapeDtypeStruct(shape, jnp.float32)


def bf16(*shape):
    return jax.ShapeDtypeStruct(shape, jnp.bfloat16)


def exchange(x, axis, mask):
    return lax.ppermute(x, axis, [(i, i ^ mask) for i in range(lax.axis_size(axis))])


def local(state_guess, adjoint_guess, conv_weight, conv_bias):
    depth, chans, width = conv_weight.shape
    shares = lax.axis_size("dp")
    steps = lax.axis_size("layer").bit_length() - 1
    args = (state_guess, adjoint_guess, conv_weight, conv_bias)
    total, slope, rounded, back_w = call(
        relax_kernel,
        (
            f32(3, chans, HW),
            f32(depth, chans, HW),
            bf16(depth, chans, HW),
            bf16(depth, 3 * chans, 3 * chans),
        ),
        args,
        hbm_in=range(4),
        scratch=[pltpu.VMEM(a.shape, a.dtype) for a in args] + [pltpu.SemaphoreType.DMA((4,))],
    )
    (patch,) = call(patch_kernel, (bf16(depth, width, HW),), (rounded,))
    mine = ()
    for step in range(1, steps):
        got = exchange(total, "layer", 1 << (step - 1))
        final = step == steps - 1
        total, *mine = call(
            functools.partial(join_kernel, step, final),
            (f32(chans, HW) if final else f32(3, chans, HW), f32(4, chans, HW)),
            (total, got, *mine),
        )
    got = exchange(total, "layer", 1 << (steps - 1))
    lanes = -(-(width + 1) // HALF) * HALF
    part = (depth * chans // shares, lanes)
    guess = pltpu.VMEM(adjoint_guess.shape, jnp.float32)
    adjoint_fixed, state_fixed, keep, send = call(
        functools.partial(grad_kernel, steps),
        (
            f32(*adjoint_guess.shape),
            f32(*state_guess.shape),
            f32(shares // 2, *part),
            f32(shares // 2, *part),
        ),
        (got, *mine, adjoint_guess, state_guess, slope, patch, back_w),
        hbm_out=(0, 1),
        scratch=[guess, guess, pltpu.SemaphoreType.DMA((2,))],
    )
    keep, send = call(halve_kernel, (f32(*part), f32(*part)), (keep, exchange(send, "dp", 1)))
    weight_grad, bias_grad = call(
        total_kernel,
        (f32(depth, chans // shares, width), f32(depth, chans // shares)),
        (keep, exchange(send, "dp", 3)),
    )
    return (state_fixed, adjoint_fixed, weight_grad, bias_grad)


def solution(mesh):
    placed = (
        P("layer", "dp", None, None),
        P("layer", "dp", None, None),
        P("layer", None, None),
        P("layer", None),
    )
    return jax.shard_map(
        local,
        mesh=mesh,
        in_specs=placed,
        out_specs=(
            P("layer", "dp", None, None),
            P("layer", "dp", None, None),
            P("layer", "dp", None),
            P("layer", "dp"),
        ),
        check_vma=False,
    )
```

```python
import functools

import jax
import jax.numpy as jnp
from jax import lax
from jax.experimental import pallas as pl
from jax.experimental.pallas import tpu as pltpu
from jax.sharding import PartitionSpec as P

IMG = 16
HW = IMG * IMG
HALF = 128
TAPS = 9
STEP = 0.5
LIMIT = 32 * 1024 * 1024

VMEM = pl.BlockSpec(memory_space=pltpu.VMEM)
HBM = pl.BlockSpec(memory_space=pltpu.HBM)


def taps_of(values):
    pixel = lax.broadcasted_iota(jnp.int16, values.shape, 1)
    col = pixel & (IMG - 1)
    rows = {-1: pixel >= IMG, 1: pixel < HW - IMG}
    cols = {-1: col >= 1, 1: col < IMG - 1}
    out = []
    for tap in range(TAPS):
        down, right = tap // 3 - 1, tap % 3 - 1
        part = values
        if down or right:
            part = pltpu.roll(values, -(down * IMG + right) % HW, 1)
            tests = [rows[down]] if down else []
            tests += [cols[right]] if right else []
            part = jnp.where(functools.reduce(jnp.logical_and, tests), part, jnp.zeros_like(part))
        out.append(part)
    return jnp.concatenate(out, axis=0)


def permutation(chans):
    size = TAPS * chans
    row = lax.broadcasted_iota(jnp.int32, (size, size), 0)
    column = lax.broadcasted_iota(jnp.int32, (size, size), 1)
    tap = lax.div(row, chans)
    return jnp.where(column == (row - tap * chans) * TAPS + tap, 1.0, 0.0).astype(jnp.bfloat16)


def dot(a, b, dims):
    return lax.dot_general(a, b, (dims, ((), ())), preferred_element_type=jnp.float32)


def convolve(weight, values):
    return dot(weight, taps_of(values), ((1,), (0,)))


def relax_kernel(
    state_hbm,
    adj_hbm,
    w_hbm,
    bias_hbm,
    sent_ref,
    slope_ref,
    rounded_ref,
    back_w_ref,
    state_ref,
    adj_ref,
    w_ref,
    bias_ref,
    perm_ref,
    by_tap_ref,
    column_ref,
    sems,
):
    copies = [
        pltpu.make_async_copy(src, dst, sems.at[k])
        for k, (src, dst) in enumerate(
            ((w_hbm, w_ref), (state_hbm, state_ref), (bias_hbm, bias_ref), (adj_hbm, adj_ref))
        )
    ]
    for copy in copies:
        copy.start()
    depth, chans, width = w_ref.shape
    perm_ref[...] = permutation(chans)
    row = lax.broadcasted_iota(jnp.int32, (chans, width), 0)
    lane = lax.broadcasted_iota(jnp.int32, (chans, width), 1)
    center = lane == row * TAPS + TAPS // 2
    eye = lax.broadcasted_iota(jnp.int32, (chans, chans), 0) == lax.broadcasted_iota(
        jnp.int32, (chans, chans), 1
    )
    for copy in copies:
        copy.wait()
    start = state_ref[0, 0]
    guess = adj_ref[0, 0]
    by_tap = dot(w_ref[...].reshape(depth * chans, width), perm_ref[...], ((1,), (1,)))
    by_tap_ref[...] = by_tap.astype(jnp.bfloat16).reshape(depth, chans, width)
    for n in range(depth):
        bias = jnp.broadcast_to(bias_ref[n : n + 1, :], (chans, chans))
        bias = jnp.sum(jnp.where(eye, bias, 0.0), axis=1, keepdims=True)
        column_ref[n] = jnp.broadcast_to(bias, (chans, HALF))

    def ahead(n, carry):
        state, gain = carry
        weight = w_ref[n]
        kc = jnp.sum(jnp.where(center, weight.astype(jnp.float32), 0.0), axis=1, keepdims=True)
        rounded = state.astype(jnp.bfloat16)
        rounded_ref[n] = rounded
        squash = jnp.tanh(convolve(by_tap_ref[n], rounded) + column_ref[n][:, :1])
        slope = STEP * (1.0 - squash * squash)
        slope_ref[n] = slope
        turned = dot(perm_ref[...], weight, ((1,), (1,))).astype(jnp.bfloat16)
        back_w_ref[n] = jnp.concatenate(
            [turned[t * chans : (t + 1) * chans] for t in reversed(range(TAPS))], axis=1
        )
        return state + STEP * squash, gain * (1.0 + slope * kc)

    state, gain = lax.fori_loop(0, depth, ahead, (start, jnp.ones_like(start)))

    def behind(i, back):
        n = depth - 1 - i
        return back + convolve(back_w_ref[n], (back * slope_ref[n]).astype(jnp.bfloat16))

    back = lax.fori_loop(0, depth, behind, guess)
    place = lax.axis_index("layer")
    first = jnp.where(place == 0, 0.0, start)
    last = jnp.where(place == lax.axis_size("layer") - 1, 0.0, guess)
    sent_ref[0] = gain
    sent_ref[1] = state - gain * first
    sent_ref[2] = back - gain * last


def patch_kernel(rounded_ref, patch_ref):
    depth, chans, _ = rounded_ref.shape
    perm = permutation(chans)
    for n in range(depth):
        rounded = rounded_ref[n]
        patch_ref[n] = dot(perm, taps_of(rounded), ((0,), (0,))).astype(jnp.bfloat16)


def joined(bit, total, mine, got):
    gain, fwd, bwd = total
    pre_gain, pre, post_gain, post = mine
    got_gain, got_fwd, got_bwd = got
    total = (
        gain * got_gain,
        jnp.where(bit, gain * got_fwd + fwd, got_gain * fwd + got_fwd),
        jnp.where(bit, got_gain * bwd + got_bwd, gain * got_bwd + bwd),
    )
    mine = (
        jnp.where(bit, pre_gain * got_gain, pre_gain),
        jnp.where(bit, pre_gain * got_fwd + pre, pre),
        jnp.where(bit, post_gain, post_gain * got_gain),
        jnp.where(bit, post, post_gain * got_bwd + post),
    )
    return total, mine


def bit_of(axis, step):
    return lax.rem(lax.div(lax.axis_index(axis), 2**step), 2) == 1


def join_kernel(step, final, *refs):
    if step == 1:
        total_ref, got_ref, sent_ref, mine_out = refs
        one = jnp.ones(total_ref.shape[1:], jnp.float32)
        zero = jnp.zeros(total_ref.shape[1:], jnp.float32)
        mine = (one, zero, one, zero)
    else:
        total_ref, got_ref, mine_ref, sent_ref, mine_out = refs
        mine = tuple(mine_ref[k] for k in range(4))
    total = tuple(total_ref[k] for k in range(3))
    got = tuple(got_ref[k] for k in range(3))
    total, mine = joined(bit_of("layer", step - 1), total, mine, got)
    for k in range(4):
        mine_out[k] = mine[k]
    if final:
        sent_ref[...] = jnp.where(bit_of("layer", step), total[2], total[1])
    else:
        for k in range(3):
            sent_ref[k] = total[k]


def grad_kernel(
    steps,
    got_ref,
    mine_ref,
    guess_ref,
    start_ref,
    slope_ref,
    patch_ref,
    back_w_ref,
    adj_hbm,
    state_hbm,
    keep_ref,
    send_ref,
    adj_ref,
    state_ref,
    sems,
):
    depth, chans, rows = back_w_ref.shape
    shares = 2 * keep_ref.shape[0]
    own = chans // shares
    place = lax.axis_index("layer")
    upper = bit_of("layer", steps - 1)
    got = got_ref[...]
    fixed = jnp.where(upper, mine_ref[1] + mine_ref[0] * got, mine_ref[1])
    state_ref[0, 0] = jnp.where(place == 0, start_ref[0, 0], fixed)
    fixed = jnp.where(upper, mine_ref[3], mine_ref[3] + mine_ref[2] * got)
    adj = jnp.where(place == lax.axis_size("layer") - 1, guess_ref[0, 0], fixed)
    adj_ref[0, 0] = adj
    copies = [
        pltpu.make_async_copy(src, dst, sems.at[k])
        for k, (src, dst) in enumerate(((adj_ref, adj_hbm), (state_ref, state_hbm)))
    ]
    for copy in copies:
        copy.start()
    pad = keep_ref.shape[2] - rows
    odd, high = bit_of("dp", 0), bit_of("dp", 1)

    def layer(n, adj):
        dz = adj * slope_ref[n]
        dzb = dz.astype(jnp.bfloat16)
        grad = dot(dzb, patch_ref[n], ((1,), (1,)))
        bias = jnp.broadcast_to(jnp.sum(dz, axis=1, keepdims=True), (chans, pad))
        both = jnp.concatenate([grad, bias], axis=1)
        parts = [both[s * own : (s + 1) * own] for s in range(shares)]
        parts = [jnp.where(odd, parts[i ^ 1], parts[i]) for i in range(shares)]
        parts = [jnp.where(high, parts[i ^ 2], parts[i]) for i in range(shares)]
        where = pl.ds(pl.multiple_of(n * own, own), own)
        keep_ref[0, where], keep_ref[1, where] = parts[0], parts[3]
        send_ref[0, where], send_ref[1, where] = parts[1], parts[2]
        return dzb

    def behind(i, adj):
        n = depth - 1 - i
        return adj + convolve(back_w_ref[n], layer(n, adj))

    layer(0, lax.fori_loop(0, depth - 1, behind, adj))
    for copy in copies:
        copy.wait()


def halve_kernel(mine_ref, got_ref, keep_ref, send_ref):
    keep_ref[...] = mine_ref[0] + got_ref[0]
    send_ref[...] = mine_ref[1] + got_ref[1]


def total_kernel(mine_ref, got_ref, grad_ref, bias_ref):
    depth, own, width = grad_ref.shape
    total = mine_ref[...] + got_ref[...]
    eye = lax.broadcasted_iota(jnp.int32, (own, own), 0) == lax.broadcasted_iota(
        jnp.int32, (own, own), 1
    )
    for n in range(depth):
        mine = total[n * own : (n + 1) * own]
        grad_ref[n] = mine[:, :width]
        column = jnp.broadcast_to(mine[:, width : width + 1], (own, own))
        bias_ref[n : n + 1, :] = jnp.sum(jnp.where(eye, column, 0.0), axis=0, keepdims=True)


def call(kernel, out_shape, args, hbm_in=(), hbm_out=(), scratch=()):
    return pl.pallas_call(
        kernel,
        out_shape=out_shape,
        in_specs=[HBM if k in hbm_in else VMEM for k in range(len(args))],
        out_specs=[HBM if k in hbm_out else VMEM for k in range(len(out_shape))],
        scratch_shapes=list(scratch),
        compiler_params=pltpu.CompilerParams(vmem_limit_bytes=LIMIT),
        cost_estimate=pl.CostEstimate(flops=2**28, bytes_accessed=2**20, transcendentals=0),
    )(*(pltpu.with_memory_space_constraint(a, pltpu.HBM) if k in hbm_in else a for k, a in enumerate(args)))


def f32(*shape):
    return jax.ShapeDtypeStruct(shape, jnp.float32)


def bf16(*shape):
    return jax.ShapeDtypeStruct(shape, jnp.bfloat16)


def exchange(x, axis, mask):
    return lax.ppermute(x, axis, [(i, i ^ mask) for i in range(lax.axis_size(axis))])


def local(state_guess, adjoint_guess, conv_weight, conv_bias):
    depth, chans, width = conv_weight.shape
    shares = lax.axis_size("dp")
    steps = lax.axis_size("layer").bit_length() - 1
    args = (state_guess, adjoint_guess, conv_weight, conv_bias)
    total, slope, rounded, back_w = call(
        relax_kernel,
        (
            f32(3, chans, HW),
            f32(depth, chans, HW),
            bf16(depth, chans, HW),
            bf16(depth, chans, width),
        ),
        args,
        hbm_in=range(4),
        scratch=[pltpu.VMEM(a.shape, a.dtype) for a in args]
        + [
            pltpu.VMEM((width, width), jnp.bfloat16),
            pltpu.VMEM((depth, chans, width), jnp.bfloat16),
            pltpu.VMEM((depth, chans, HALF), jnp.float32),
            pltpu.SemaphoreType.DMA((4,)),
        ],
    )
    (patch,) = call(patch_kernel, (bf16(depth, width, HW),), (rounded,))
    mine = ()
    for step in range(1, steps):
        got = exchange(total, "layer", 1 << (step - 1))
        final = step == steps - 1
        total, *mine = call(
            functools.partial(join_kernel, step, final),
            (f32(chans, HW) if final else f32(3, chans, HW), f32(4, chans, HW)),
            (total, got, *mine),
        )
    got = exchange(total, "layer", 1 << (steps - 1))
    lanes = -(-(width + 1) // HALF) * HALF
    part = (depth * chans // shares, lanes)
    guess = pltpu.VMEM(adjoint_guess.shape, jnp.float32)
    adjoint_fixed, state_fixed, keep, send = call(
        functools.partial(grad_kernel, steps),
        (
            f32(*adjoint_guess.shape),
            f32(*state_guess.shape),
            f32(shares // 2, *part),
            f32(shares // 2, *part),
        ),
        (got, *mine, adjoint_guess, state_guess, slope, patch, back_w),
        hbm_out=(0, 1),
        scratch=[guess, guess, pltpu.SemaphoreType.DMA((2,))],
    )
    keep, send = call(halve_kernel, (f32(*part), f32(*part)), (keep, exchange(send, "dp", 1)))
    weight_grad, bias_grad = call(
        total_kernel,
        (f32(depth, chans // shares, width), f32(depth, chans // shares)),
        (keep, exchange(send, "dp", 3)),
    )
    return (state_fixed, adjoint_fixed, weight_grad, bias_grad)


def solution(mesh):
    placed = (
        P("layer", "dp", None, None),
        P("layer", "dp", None, None),
        P("layer", None, None),
        P("layer", None),
    )
    return jax.shard_map(
        local,
        mesh=mesh,
        in_specs=placed,
        out_specs=(
            P("layer", "dp", None, None),
            P("layer", "dp", None, None),
            P("layer", "dp", None),
            P("layer", "dp"),
        ),
        check_vma=False,
    )
```

```python
import functools

import jax
import jax.numpy as jnp
from jax import lax
from jax.experimental import pallas as pl
from jax.experimental.pallas import tpu as pltpu
from jax.sharding import PartitionSpec as P

IMG = 16
HW = IMG * IMG
HALF = 128
TAPS = 9
STEP = 0.5
LIMIT = 32 * 1024 * 1024

VMEM = pl.BlockSpec(memory_space=pltpu.VMEM)
HBM = pl.BlockSpec(memory_space=pltpu.HBM)


def taps_of(values):
    pixel = lax.broadcasted_iota(jnp.int16, values.shape, 1)
    col = pixel & (IMG - 1)
    rows = {-1: pixel >= IMG, 1: pixel < HW - IMG}
    cols = {-1: col >= 1, 1: col < IMG - 1}
    out = []
    for tap in range(TAPS):
        down, right = tap // 3 - 1, tap % 3 - 1
        part = values
        if down or right:
            part = pltpu.roll(values, -(down * IMG + right) % HW, 1)
            tests = [rows[down]] if down else []
            tests += [cols[right]] if right else []
            part = jnp.where(functools.reduce(jnp.logical_and, tests), part, jnp.zeros_like(part))
        out.append(part)
    return jnp.concatenate(out, axis=0)


def permutation(chans):
    size = TAPS * chans
    row = lax.broadcasted_iota(jnp.int32, (size, size), 0)
    column = lax.broadcasted_iota(jnp.int32, (size, size), 1)
    tap = lax.div(row, chans)
    return jnp.where(column == (row - tap * chans) * TAPS + tap, 1.0, 0.0).astype(jnp.bfloat16)


def dot(a, b, dims):
    return lax.dot_general(a, b, (dims, ((), ())), preferred_element_type=jnp.float32)


def convolve(weight, values):
    return dot(weight, taps_of(values), ((1,), (0,)))


def relax_kernel(
    state_hbm,
    adj_hbm,
    w_hbm,
    bias_hbm,
    sent_ref,
    slope_ref,
    rounded_ref,
    back_w_ref,
    state_ref,
    adj_ref,
    w_ref,
    bias_ref,
    perm_ref,
    by_tap_ref,
    column_ref,
    sems,
):
    copies = [
        pltpu.make_async_copy(src, dst, sems.at[k])
        for k, (src, dst) in enumerate(
            ((w_hbm, w_ref), (state_hbm, state_ref), (bias_hbm, bias_ref), (adj_hbm, adj_ref))
        )
    ]
    for copy in copies:
        copy.start()
    depth, chans, width = w_ref.shape
    perm_ref[...] = permutation(chans)
    eye = lax.broadcasted_iota(jnp.int32, (chans, chans), 0) == lax.broadcasted_iota(
        jnp.int32, (chans, chans), 1
    )
    for copy in copies:
        copy.wait()
    weights = w_ref[...].reshape(depth * chans, width)
    by_tap = dot(weights, perm_ref[...], ((1,), (1,)))
    by_tap_ref[...] = by_tap.astype(jnp.bfloat16).reshape(depth, chans, width)
    turned = dot(perm_ref[...], weights, ((1,), (1,))).astype(jnp.bfloat16)
    middle = TAPS // 2 * chans
    for n in range(depth):
        mine = slice(n * chans, (n + 1) * chans)
        back_w_ref[n] = jnp.concatenate(
            [turned[t * chans : (t + 1) * chans, mine] for t in reversed(range(TAPS))], axis=1
        )
        bias = jnp.broadcast_to(bias_ref[n : n + 1, :], (chans, chans))
        for k, square in enumerate((bias, by_tap[mine, middle : middle + chans])):
            column = jnp.sum(jnp.where(eye, square, 0.0), axis=1, keepdims=True)
            column_ref[n, k] = jnp.broadcast_to(column, (chans, HALF))
    start = state_ref[0, 0]
    guess = adj_ref[0, 0]

    def ahead(n, carry):
        state, gain = carry
        bias, kc = (jnp.concatenate([column_ref[n, k]] * (HW // HALF), axis=1) for k in range(2))
        rounded = state.astype(jnp.bfloat16)
        rounded_ref[n] = rounded
        squash = jnp.tanh(convolve(by_tap_ref[n], rounded) + bias)
        slope = STEP * (1.0 - squash * squash)
        slope_ref[n] = slope
        return state + STEP * squash, gain * (1.0 + slope * kc)

    state, gain = lax.fori_loop(0, depth, ahead, (start, jnp.ones_like(start)))

    def behind(i, back):
        n = depth - 1 - i
        return back + convolve(back_w_ref[n], (back * slope_ref[n]).astype(jnp.bfloat16))

    back = lax.fori_loop(0, depth, behind, guess)
    place = lax.axis_index("layer")
    first = jnp.where(place == 0, 0.0, start)
    last = jnp.where(place == lax.axis_size("layer") - 1, 0.0, guess)
    sent_ref[0] = gain
    sent_ref[1] = state - gain * first
    sent_ref[2] = back - gain * last


def patch_kernel(rounded_ref, patch_ref, perm_ref):
    depth, chans, _ = rounded_ref.shape
    perm_ref[...] = permutation(chans)

    @pl.loop(0, depth)
    def _(n):
        patch = taps_of(rounded_ref[n])
        patch_ref[n] = dot(perm_ref[...], patch, ((0,), (0,))).astype(jnp.bfloat16)


def joined(bit, total, mine, got):
    gain, fwd, bwd = total
    pre_gain, pre, post_gain, post = mine
    got_gain, got_fwd, got_bwd = got
    total = (
        gain * got_gain,
        jnp.where(bit, gain * got_fwd + fwd, got_gain * fwd + got_fwd),
        jnp.where(bit, got_gain * bwd + got_bwd, gain * got_bwd + bwd),
    )
    mine = (
        jnp.where(bit, pre_gain * got_gain, pre_gain),
        jnp.where(bit, pre_gain * got_fwd + pre, pre),
        jnp.where(bit, post_gain, post_gain * got_gain),
        jnp.where(bit, post, post_gain * got_bwd + post),
    )
    return total, mine


def bit_of(axis, step):
    return lax.rem(lax.div(lax.axis_index(axis), 2**step), 2) == 1


def join_kernel(step, final, *refs):
    if step == 1:
        total_ref, got_ref, sent_ref, mine_out = refs
        one = jnp.ones(total_ref.shape[1:], jnp.float32)
        zero = jnp.zeros(total_ref.shape[1:], jnp.float32)
        mine = (one, zero, one, zero)
    else:
        total_ref, got_ref, mine_ref, sent_ref, mine_out = refs
        mine = tuple(mine_ref[k] for k in range(4))
    total = tuple(total_ref[k] for k in range(3))
    got = tuple(got_ref[k] for k in range(3))
    total, mine = joined(bit_of("layer", step - 1), total, mine, got)
    for k in range(4):
        mine_out[k] = mine[k]
    if final:
        sent_ref[...] = jnp.where(bit_of("layer", step), total[2], total[1])
    else:
        for k in range(3):
            sent_ref[k] = total[k]


def grad_kernel(
    steps,
    got_ref,
    mine_ref,
    guess_ref,
    start_ref,
    slope_ref,
    patch_ref,
    back_w_ref,
    adj_hbm,
    state_hbm,
    keep_ref,
    send_ref,
    adj_ref,
    state_ref,
    sems,
):
    depth, chans, rows = back_w_ref.shape
    shares = 2 * keep_ref.shape[0]
    own = chans // shares
    place = lax.axis_index("layer")
    upper = bit_of("layer", steps - 1)
    got = got_ref[...]
    fixed = jnp.where(upper, mine_ref[1] + mine_ref[0] * got, mine_ref[1])
    state_ref[0, 0] = jnp.where(place == 0, start_ref[0, 0], fixed)
    fixed = jnp.where(upper, mine_ref[3], mine_ref[3] + mine_ref[2] * got)
    adj = jnp.where(place == lax.axis_size("layer") - 1, guess_ref[0, 0], fixed)
    adj_ref[0, 0] = adj
    copies = [
        pltpu.make_async_copy(src, dst, sems.at[k])
        for k, (src, dst) in enumerate(((adj_ref, adj_hbm), (state_ref, state_hbm)))
    ]
    for copy in copies:
        copy.start()
    pad = keep_ref.shape[2] - rows
    odd, high = bit_of("dp", 0), bit_of("dp", 1)

    def layer(n, adj):
        dz = adj * slope_ref[n]
        dzb = dz.astype(jnp.bfloat16)
        grad = dot(dzb, patch_ref[n], ((1,), (1,)))
        bias = jnp.broadcast_to(jnp.sum(dz, axis=1, keepdims=True), (chans, pad))
        both = jnp.concatenate([grad, bias], axis=1)
        parts = [both[s * own : (s + 1) * own] for s in range(shares)]
        parts = [jnp.where(odd, parts[i ^ 1], parts[i]) for i in range(shares)]
        parts = [jnp.where(high, parts[i ^ 2], parts[i]) for i in range(shares)]
        where = pl.ds(pl.multiple_of(n * own, own), own)
        keep_ref[0, where], keep_ref[1, where] = parts[0], parts[3]
        send_ref[0, where], send_ref[1, where] = parts[1], parts[2]
        return dzb

    def behind(i, adj):
        n = depth - 1 - i
        return adj + convolve(back_w_ref[n], layer(n, adj))

    layer(0, lax.fori_loop(0, depth - 1, behind, adj))
    for copy in copies:
        copy.wait()


def halve_kernel(mine_ref, got_ref, keep_ref, send_ref):
    keep_ref[...] = mine_ref[0] + got_ref[0]
    send_ref[...] = mine_ref[1] + got_ref[1]


def total_kernel(mine_ref, got_ref, grad_ref, bias_ref):
    depth, own, width = grad_ref.shape
    total = mine_ref[...] + got_ref[...]
    eye = lax.broadcasted_iota(jnp.int32, (own, own), 0) == lax.broadcasted_iota(
        jnp.int32, (own, own), 1
    )
    for n in range(depth):
        mine = total[n * own : (n + 1) * own]
        grad_ref[n] = mine[:, :width]
        column = jnp.broadcast_to(mine[:, width : width + 1], (own, own))
        bias_ref[n : n + 1, :] = jnp.sum(jnp.where(eye, column, 0.0), axis=0, keepdims=True)


def call(kernel, out_shape, args, hbm_in=(), hbm_out=(), scratch=()):
    return pl.pallas_call(
        kernel,
        out_shape=out_shape,
        in_specs=[HBM if k in hbm_in else VMEM for k in range(len(args))],
        out_specs=[HBM if k in hbm_out else VMEM for k in range(len(out_shape))],
        scratch_shapes=list(scratch),
        compiler_params=pltpu.CompilerParams(vmem_limit_bytes=LIMIT),
        cost_estimate=pl.CostEstimate(flops=2**28, bytes_accessed=2**20, transcendentals=0),
    )(*(pltpu.with_memory_space_constraint(a, pltpu.HBM) if k in hbm_in else a for k, a in enumerate(args)))


def f32(*shape):
    return jax.ShapeDtypeStruct(shape, jnp.float32)


def bf16(*shape):
    return jax.ShapeDtypeStruct(shape, jnp.bfloat16)


def exchange(x, axis, mask):
    return lax.ppermute(x, axis, [(i, i ^ mask) for i in range(lax.axis_size(axis))])


def local(state_guess, adjoint_guess, conv_weight, conv_bias):
    depth, chans, width = conv_weight.shape
    shares = lax.axis_size("dp")
    steps = lax.axis_size("layer").bit_length() - 1
    args = (state_guess, adjoint_guess, conv_weight, conv_bias)
    total, slope, rounded, back_w = call(
        relax_kernel,
        (
            f32(3, chans, HW),
            f32(depth, chans, HW),
            bf16(depth, chans, HW),
            bf16(depth, chans, width),
        ),
        args,
        hbm_in=range(4),
        scratch=[pltpu.VMEM(a.shape, a.dtype) for a in args]
        + [
            pltpu.VMEM((width, width), jnp.bfloat16),
            pltpu.VMEM((depth, chans, width), jnp.bfloat16),
            pltpu.VMEM((depth, 2, chans, HALF), jnp.float32),
            pltpu.SemaphoreType.DMA((4,)),
        ],
    )
    (patch,) = call(
        patch_kernel,
        (bf16(depth, width, HW),),
        (rounded,),
        scratch=[pltpu.VMEM((width, width), jnp.bfloat16)],
    )
    mine = ()
    for step in range(1, steps):
        got = exchange(total, "layer", 1 << (step - 1))
        final = step == steps - 1
        total, *mine = call(
            functools.partial(join_kernel, step, final),
            (f32(chans, HW) if final else f32(3, chans, HW), f32(4, chans, HW)),
            (total, got, *mine),
        )
    got = exchange(total, "layer", 1 << (steps - 1))
    lanes = -(-(width + 1) // HALF) * HALF
    part = (depth * chans // shares, lanes)
    guess = pltpu.VMEM(adjoint_guess.shape, jnp.float32)
    adjoint_fixed, state_fixed, keep, send = call(
        functools.partial(grad_kernel, steps),
        (
            f32(*adjoint_guess.shape),
            f32(*state_guess.shape),
            f32(shares // 2, *part),
            f32(shares // 2, *part),
        ),
        (got, *mine, adjoint_guess, state_guess, slope, patch, back_w),
        hbm_out=(0, 1),
        scratch=[guess, guess, pltpu.SemaphoreType.DMA((2,))],
    )
    keep, send = call(halve_kernel, (f32(*part), f32(*part)), (keep, exchange(send, "dp", 1)))
    weight_grad, bias_grad = call(
        total_kernel,
        (f32(depth, chans // shares, width), f32(depth, chans // shares)),
        (keep, exchange(send, "dp", 3)),
    )
    return (state_fixed, adjoint_fixed, weight_grad, bias_grad)


def solution(mesh):
    placed = (
        P("layer", "dp", None, None),
        P("layer", "dp", None, None),
        P("layer", None, None),
        P("layer", None),
    )
    return jax.shard_map(
        local,
        mesh=mesh,
        in_specs=placed,
        out_specs=(
            P("layer", "dp", None, None),
            P("layer", "dp", None, None),
            P("layer", "dp", None),
            P("layer", "dp"),
        ),
        check_vma=False,
    )
```

```python
import functools

import jax
import jax.numpy as jnp
from jax import lax
from jax.experimental import pallas as pl
from jax.experimental.pallas import tpu as pltpu
from jax.sharding import PartitionSpec as P

IMG = 16
HW = IMG * IMG
HALF = 128
TAPS = 9
STEP = 0.5
LIMIT = 32 * 1024 * 1024

VMEM = pl.BlockSpec(memory_space=pltpu.VMEM)
HBM = pl.BlockSpec(memory_space=pltpu.HBM)


def taps_of(values):
    pixel = lax.broadcasted_iota(jnp.int16, values.shape, 1)
    col = pixel & (IMG - 1)
    rows = {-1: pixel >= IMG, 1: pixel < HW - IMG}
    cols = {-1: col >= 1, 1: col < IMG - 1}
    out = []
    for tap in range(TAPS):
        down, right = tap // 3 - 1, tap % 3 - 1
        part = values
        if down or right:
            part = pltpu.roll(values, -(down * IMG + right) % HW, 1)
            tests = [rows[down]] if down else []
            tests += [cols[right]] if right else []
            part = jnp.where(functools.reduce(jnp.logical_and, tests), part, jnp.zeros_like(part))
        out.append(part)
    return jnp.concatenate(out, axis=0)


def permutation(chans):
    size = TAPS * chans
    row = lax.broadcasted_iota(jnp.int32, (size, size), 0)
    column = lax.broadcasted_iota(jnp.int32, (size, size), 1)
    tap = lax.div(row, chans)
    return jnp.where(column == (row - tap * chans) * TAPS + tap, 1.0, 0.0).astype(jnp.bfloat16)


def dot(a, b, dims):
    return lax.dot_general(a, b, (dims, ((), ())), preferred_element_type=jnp.float32)


def convolve(weight, values):
    return dot(weight, taps_of(values), ((1,), (0,)))


def relax_kernel(
    state_hbm,
    adj_hbm,
    w_hbm,
    bias_hbm,
    sent_ref,
    slope_ref,
    rounded_ref,
    back_w_ref,
    state_ref,
    adj_ref,
    w_ref,
    bias_ref,
    sems,
):
    copies = [
        pltpu.make_async_copy(src, dst, sems.at[k])
        for k, (src, dst) in enumerate(
            ((w_hbm, w_ref), (state_hbm, state_ref), (bias_hbm, bias_ref), (adj_hbm, adj_ref))
        )
    ]
    for copy in copies:
        copy.start()
    depth, chans, width = w_ref.shape
    perm = permutation(chans)
    eye = lax.broadcasted_iota(jnp.int32, (chans, chans), 0) == lax.broadcasted_iota(
        jnp.int32, (chans, chans), 1
    )
    for copy in copies:
        copy.wait()
    weights = w_ref[...].reshape(depth * chans, width)
    by_tap = dot(weights, perm, ((1,), (1,)))
    turned = dot(perm, weights, ((1,), (1,))).astype(jnp.bfloat16)
    middle = TAPS // 2 * chans
    start = state_ref[0, 0]
    guess = adj_ref[0, 0]
    state = start
    gain = None
    slopes = []
    backs = []
    for n in range(depth):
        mine = slice(n * chans, (n + 1) * chans)
        bias = jnp.broadcast_to(bias_ref[n : n + 1, :], (chans, chans))
        bias, kc = (
            jnp.sum(jnp.where(eye, square, 0.0), axis=1, keepdims=True)
            for square in (bias, by_tap[mine, middle : middle + chans])
        )
        rounded = state.astype(jnp.bfloat16)
        rounded_ref[n] = rounded
        squash = jnp.tanh(convolve(by_tap[mine].astype(jnp.bfloat16), rounded) + bias)
        slope = STEP * (1.0 - squash * squash)
        slope_ref[n] = slope
        slopes.append(slope)
        state = state + STEP * squash
        factor = 1.0 + slope * kc
        gain = factor if gain is None else gain * factor
        back_w = jnp.concatenate(
            [turned[t * chans : (t + 1) * chans, mine] for t in reversed(range(TAPS))], axis=1
        )
        back_w_ref[n] = back_w
        backs.append(back_w)
    back = guess
    for n in reversed(range(depth)):
        back = back + convolve(backs[n], (back * slopes[n]).astype(jnp.bfloat16))
    place = lax.axis_index("layer")
    first = jnp.where(place == 0, 0.0, start)
    last = jnp.where(place == lax.axis_size("layer") - 1, 0.0, guess)
    sent_ref[0] = gain
    sent_ref[1] = state - gain * first
    sent_ref[2] = back - gain * last


def patch_kernel(rounded_ref, patch_ref):
    depth, chans, _ = rounded_ref.shape
    perm = permutation(chans)
    for n in range(depth):
        patch = taps_of(rounded_ref[n])
        patch_ref[n] = dot(perm, patch, ((0,), (0,))).astype(jnp.bfloat16)


def joined(bit, total, mine, got):
    gain, fwd, bwd = total
    pre_gain, pre, post_gain, post = mine
    got_gain, got_fwd, got_bwd = got
    total = (
        gain * got_gain,
        jnp.where(bit, gain * got_fwd + fwd, got_gain * fwd + got_fwd),
        jnp.where(bit, got_gain * bwd + got_bwd, gain * got_bwd + bwd),
    )
    mine = (
        jnp.where(bit, pre_gain * got_gain, pre_gain),
        jnp.where(bit, pre_gain * got_fwd + pre, pre),
        jnp.where(bit, post_gain, post_gain * got_gain),
        jnp.where(bit, post, post_gain * got_bwd + post),
    )
    return total, mine


def bit_of(axis, step):
    return lax.rem(lax.div(lax.axis_index(axis), 2**step), 2) == 1


def join_kernel(step, final, *refs):
    if step == 1:
        total_ref, got_ref, sent_ref, mine_out = refs
        one = jnp.ones(total_ref.shape[1:], jnp.float32)
        zero = jnp.zeros(total_ref.shape[1:], jnp.float32)
        mine = (one, zero, one, zero)
    else:
        total_ref, got_ref, mine_ref, sent_ref, mine_out = refs
        mine = tuple(mine_ref[k] for k in range(4))
    total = tuple(total_ref[k] for k in range(3))
    got = tuple(got_ref[k] for k in range(3))
    total, mine = joined(bit_of("layer", step - 1), total, mine, got)
    for k in range(4):
        mine_out[k] = mine[k]
    if final:
        sent_ref[...] = jnp.where(bit_of("layer", step), total[2], total[1])
    else:
        for k in range(3):
            sent_ref[k] = total[k]


def grad_kernel(
    steps,
    got_ref,
    mine_ref,
    guess_ref,
    start_ref,
    slope_ref,
    patch_ref,
    back_w_ref,
    adj_hbm,
    state_hbm,
    keep_ref,
    send_ref,
    adj_ref,
    state_ref,
    sems,
):
    depth, chans, rows = back_w_ref.shape
    shares = 2 * keep_ref.shape[0]
    own = chans // shares
    place = lax.axis_index("layer")
    upper = bit_of("layer", steps - 1)
    got = got_ref[...]
    fixed = jnp.where(upper, mine_ref[1] + mine_ref[0] * got, mine_ref[1])
    state_ref[0, 0] = jnp.where(place == 0, start_ref[0, 0], fixed)
    fixed = jnp.where(upper, mine_ref[3], mine_ref[3] + mine_ref[2] * got)
    adj = jnp.where(place == lax.axis_size("layer") - 1, guess_ref[0, 0], fixed)
    adj_ref[0, 0] = adj
    copies = [
        pltpu.make_async_copy(src, dst, sems.at[k])
        for k, (src, dst) in enumerate(((adj_ref, adj_hbm), (state_ref, state_hbm)))
    ]
    for copy in copies:
        copy.start()
    pad = keep_ref.shape[2] - rows
    odd, high = bit_of("dp", 0), bit_of("dp", 1)

    def layer(n, adj):
        dz = adj * slope_ref[n]
        dzb = dz.astype(jnp.bfloat16)
        grad = dot(dzb, patch_ref[n], ((1,), (1,)))
        bias = jnp.broadcast_to(jnp.sum(dz, axis=1, keepdims=True), (chans, pad))
        both = jnp.concatenate([grad, bias], axis=1)
        parts = [both[s * own : (s + 1) * own] for s in range(shares)]
        parts = [jnp.where(odd, parts[i ^ 1], parts[i]) for i in range(shares)]
        parts = [jnp.where(high, parts[i ^ 2], parts[i]) for i in range(shares)]
        where = pl.ds(pl.multiple_of(n * own, own), own)
        keep_ref[0, where], keep_ref[1, where] = parts[0], parts[3]
        send_ref[0, where], send_ref[1, where] = parts[1], parts[2]
        return dzb

    def behind(i, adj):
        n = depth - 1 - i
        return adj + convolve(back_w_ref[n], layer(n, adj))

    layer(0, lax.fori_loop(0, depth - 1, behind, adj))
    for copy in copies:
        copy.wait()


def halve_kernel(mine_ref, got_ref, keep_ref, send_ref):
    keep_ref[...] = mine_ref[0] + got_ref[0]
    send_ref[...] = mine_ref[1] + got_ref[1]


def total_kernel(mine_ref, got_ref, grad_ref, bias_ref):
    depth, own, width = grad_ref.shape
    total = mine_ref[...] + got_ref[...]
    eye = lax.broadcasted_iota(jnp.int32, (own, own), 0) == lax.broadcasted_iota(
        jnp.int32, (own, own), 1
    )
    for n in range(depth):
        mine = total[n * own : (n + 1) * own]
        grad_ref[n] = mine[:, :width]
        column = jnp.broadcast_to(mine[:, width : width + 1], (own, own))
        bias_ref[n : n + 1, :] = jnp.sum(jnp.where(eye, column, 0.0), axis=0, keepdims=True)


def call(kernel, out_shape, args, hbm_in=(), hbm_out=(), scratch=()):
    return pl.pallas_call(
        kernel,
        out_shape=out_shape,
        in_specs=[HBM if k in hbm_in else VMEM for k in range(len(args))],
        out_specs=[HBM if k in hbm_out else VMEM for k in range(len(out_shape))],
        scratch_shapes=list(scratch),
        compiler_params=pltpu.CompilerParams(vmem_limit_bytes=LIMIT),
        cost_estimate=pl.CostEstimate(flops=2**28, bytes_accessed=2**20, transcendentals=0),
    )(*(pltpu.with_memory_space_constraint(a, pltpu.HBM) if k in hbm_in else a for k, a in enumerate(args)))


def f32(*shape):
    return jax.ShapeDtypeStruct(shape, jnp.float32)


def bf16(*shape):
    return jax.ShapeDtypeStruct(shape, jnp.bfloat16)


def exchange(x, axis, mask):
    return lax.ppermute(x, axis, [(i, i ^ mask) for i in range(lax.axis_size(axis))])


def local(state_guess, adjoint_guess, conv_weight, conv_bias):
    depth, chans, width = conv_weight.shape
    shares = lax.axis_size("dp")
    steps = lax.axis_size("layer").bit_length() - 1
    args = (state_guess, adjoint_guess, conv_weight, conv_bias)
    total, slope, rounded, back_w = call(
        relax_kernel,
        (
            f32(3, chans, HW),
            f32(depth, chans, HW),
            bf16(depth, chans, HW),
            bf16(depth, chans, width),
        ),
        args,
        hbm_in=range(4),
        scratch=[pltpu.VMEM(a.shape, a.dtype) for a in args] + [pltpu.SemaphoreType.DMA((4,))],
    )
    (patch,) = call(patch_kernel, (bf16(depth, width, HW),), (rounded,))
    mine = ()
    for step in range(1, steps):
        got = exchange(total, "layer", 1 << (step - 1))
        final = step == steps - 1
        total, *mine = call(
            functools.partial(join_kernel, step, final),
            (f32(chans, HW) if final else f32(3, chans, HW), f32(4, chans, HW)),
            (total, got, *mine),
        )
    got = exchange(total, "layer", 1 << (steps - 1))
    lanes = -(-(width + 1) // HALF) * HALF
    part = (depth * chans // shares, lanes)
    guess = pltpu.VMEM(adjoint_guess.shape, jnp.float32)
    adjoint_fixed, state_fixed, keep, send = call(
        functools.partial(grad_kernel, steps),
        (
            f32(*adjoint_guess.shape),
            f32(*state_guess.shape),
            f32(shares // 2, *part),
            f32(shares // 2, *part),
        ),
        (got, *mine, adjoint_guess, state_guess, slope, patch, back_w),
        hbm_out=(0, 1),
        scratch=[guess, guess, pltpu.SemaphoreType.DMA((2,))],
    )
    keep, send = call(halve_kernel, (f32(*part), f32(*part)), (keep, exchange(send, "dp", 1)))
    weight_grad, bias_grad = call(
        total_kernel,
        (f32(depth, chans // shares, width), f32(depth, chans // shares)),
        (keep, exchange(send, "dp", 3)),
    )
    return (state_fixed, adjoint_fixed, weight_grad, bias_grad)


def solution(mesh):
    placed = (
        P("layer", "dp", None, None),
        P("layer", "dp", None, None),
        P("layer", None, None),
        P("layer", None),
    )
    return jax.shard_map(
        local,
        mesh=mesh,
        in_specs=placed,
        out_specs=(
            P("layer", "dp", None, None),
            P("layer", "dp", None, None),
            P("layer", "dp", None),
            P("layer", "dp"),
        ),
        check_vma=False,
    )
```

```python
import functools

import jax
import jax.numpy as jnp
from jax import lax
from jax.experimental import pallas as pl
from jax.experimental.pallas import tpu as pltpu
from jax.sharding import PartitionSpec as P

IMG = 16
HW = IMG * IMG
HALF = 128
TAPS = 9
STEP = 0.5
LIMIT = 32 * 1024 * 1024

VMEM = pl.BlockSpec(memory_space=pltpu.VMEM)
HBM = pl.BlockSpec(memory_space=pltpu.HBM)


def taps_of(values):
    pixel = lax.broadcasted_iota(jnp.int16, values.shape, 1)
    col = pixel & (IMG - 1)
    rows = {-1: pixel >= IMG, 1: pixel < HW - IMG}
    cols = {-1: col >= 1, 1: col < IMG - 1}
    out = []
    for tap in range(TAPS):
        down, right = tap // 3 - 1, tap % 3 - 1
        part = values
        if down or right:
            part = pltpu.roll(values, -(down * IMG + right) % HW, 1)
            tests = [rows[down]] if down else []
            tests += [cols[right]] if right else []
            part = jnp.where(functools.reduce(jnp.logical_and, tests), part, jnp.zeros_like(part))
        out.append(part)
    return jnp.concatenate(out, axis=0)


def permutation(chans):
    size = TAPS * chans
    row = lax.broadcasted_iota(jnp.int32, (size, size), 0)
    column = lax.broadcasted_iota(jnp.int32, (size, size), 1)
    tap = lax.div(row, chans)
    return jnp.where(column == (row - tap * chans) * TAPS + tap, 1.0, 0.0).astype(jnp.bfloat16)


def dot(a, b, dims):
    return lax.dot_general(a, b, (dims, ((), ())), preferred_element_type=jnp.float32)


def convolve(weight, values):
    return dot(weight, taps_of(values), ((1,), (0,)))


def weight_kernel(w_hbm, bias_hbm, by_tap_ref, back_w_ref, column_ref, w_ref, bias_ref, sems):
    copies = [
        pltpu.make_async_copy(src, dst, sems.at[k])
        for k, (src, dst) in enumerate(((w_hbm, w_ref), (bias_hbm, bias_ref)))
    ]
    for copy in copies:
        copy.start()
    depth, chans, width = w_ref.shape
    perm = permutation(chans)
    eye = lax.broadcasted_iota(jnp.int32, (chans, chans), 0) == lax.broadcasted_iota(
        jnp.int32, (chans, chans), 1
    )
    for copy in copies:
        copy.wait()
    weights = w_ref[...].reshape(depth * chans, width)
    by_tap = dot(weights, perm, ((1,), (1,)))
    turned = dot(perm, weights, ((1,), (1,))).astype(jnp.bfloat16)
    by_tap_ref[...] = by_tap.astype(jnp.bfloat16).reshape(depth, chans, width)
    middle = TAPS // 2 * chans
    for n in range(depth):
        mine = slice(n * chans, (n + 1) * chans)
        back_w_ref[n] = jnp.concatenate(
            [turned[t * chans : (t + 1) * chans, mine] for t in reversed(range(TAPS))], axis=1
        )
        bias = jnp.broadcast_to(bias_ref[n : n + 1, :], (chans, chans))
        for k, square in enumerate((bias, by_tap[mine, middle : middle + chans])):
            column = jnp.sum(jnp.where(eye, square, 0.0), axis=1, keepdims=True)
            column_ref[n, k] = jnp.broadcast_to(column, (chans, HALF))


def relax_kernel(
    state_ref, adj_ref, by_tap_ref, back_w_ref, column_ref, sent_ref, slope_ref, rounded_ref
):
    depth = by_tap_ref.shape[0]
    start = state_ref[0, 0]
    guess = adj_ref[0, 0]
    state = start
    gain = None
    slopes = []
    for n in range(depth):
        bias, kc = (jnp.concatenate([column_ref[n, k]] * (HW // HALF), axis=1) for k in range(2))
        rounded = state.astype(jnp.bfloat16)
        rounded_ref[n] = rounded
        squash = jnp.tanh(convolve(by_tap_ref[n], rounded) + bias)
        slope = STEP * (1.0 - squash * squash)
        slope_ref[n] = slope
        slopes.append(slope)
        state = state + STEP * squash
        factor = 1.0 + slope * kc
        gain = factor if gain is None else gain * factor
    back = guess
    for n in reversed(range(depth)):
        back = back + convolve(back_w_ref[n], (back * slopes[n]).astype(jnp.bfloat16))
    place = lax.axis_index("layer")
    first = jnp.where(place == 0, 0.0, start)
    last = jnp.where(place == lax.axis_size("layer") - 1, 0.0, guess)
    sent_ref[0] = gain
    sent_ref[1] = state - gain * first
    sent_ref[2] = back - gain * last


def patch_kernel(rounded_ref, patch_ref):
    depth, chans, _ = rounded_ref.shape
    perm = permutation(chans)
    for n in range(depth):
        patch = taps_of(rounded_ref[n])
        patch_ref[n] = dot(perm, patch, ((0,), (0,))).astype(jnp.bfloat16)


def joined(bit, total, mine, got):
    gain, fwd, bwd = total
    pre_gain, pre, post_gain, post = mine
    got_gain, got_fwd, got_bwd = got
    total = (
        gain * got_gain,
        jnp.where(bit, gain * got_fwd + fwd, got_gain * fwd + got_fwd),
        jnp.where(bit, got_gain * bwd + got_bwd, gain * got_bwd + bwd),
    )
    mine = (
        jnp.where(bit, pre_gain * got_gain, pre_gain),
        jnp.where(bit, pre_gain * got_fwd + pre, pre),
        jnp.where(bit, post_gain, post_gain * got_gain),
        jnp.where(bit, post, post_gain * got_bwd + post),
    )
    return total, mine


def bit_of(axis, step):
    return lax.rem(lax.div(lax.axis_index(axis), 2**step), 2) == 1


def join_kernel(step, final, *refs):
    if step == 1:
        total_ref, got_ref, sent_ref, mine_out = refs
        one = jnp.ones(total_ref.shape[1:], jnp.float32)
        zero = jnp.zeros(total_ref.shape[1:], jnp.float32)
        mine = (one, zero, one, zero)
    else:
        total_ref, got_ref, mine_ref, sent_ref, mine_out = refs
        mine = tuple(mine_ref[k] for k in range(4))
    total = tuple(total_ref[k] for k in range(3))
    got = tuple(got_ref[k] for k in range(3))
    total, mine = joined(bit_of("layer", step - 1), total, mine, got)
    for k in range(4):
        mine_out[k] = mine[k]
    if final:
        sent_ref[...] = jnp.where(bit_of("layer", step), total[2], total[1])
    else:
        for k in range(3):
            sent_ref[k] = total[k]


def grad_kernel(
    steps,
    got_ref,
    mine_ref,
    guess_ref,
    start_ref,
    slope_ref,
    patch_ref,
    back_w_ref,
    adj_ref,
    state_ref,
    keep_ref,
    send_ref,
):
    depth, chans, rows = back_w_ref.shape
    shares = 2 * keep_ref.shape[0]
    own = chans // shares
    place = lax.axis_index("layer")
    upper = bit_of("layer", steps - 1)
    got = got_ref[...]
    fixed = jnp.where(upper, mine_ref[1] + mine_ref[0] * got, mine_ref[1])
    state_ref[0, 0] = jnp.where(place == 0, start_ref[0, 0], fixed)
    fixed = jnp.where(upper, mine_ref[3], mine_ref[3] + mine_ref[2] * got)
    adj = jnp.where(place == lax.axis_size("layer") - 1, guess_ref[0, 0], fixed)
    adj_ref[0, 0] = adj
    pad = keep_ref.shape[2] - rows
    odd, high = bit_of("dp", 0), bit_of("dp", 1)

    def layer(n, adj):
        dz = adj * slope_ref[n]
        dzb = dz.astype(jnp.bfloat16)
        grad = dot(dzb, patch_ref[n], ((1,), (1,)))
        bias = jnp.broadcast_to(jnp.sum(dz, axis=1, keepdims=True), (chans, pad))
        both = jnp.concatenate([grad, bias], axis=1)
        parts = [both[s * own : (s + 1) * own] for s in range(shares)]
        parts = [jnp.where(odd, parts[i ^ 1], parts[i]) for i in range(shares)]
        parts = [jnp.where(high, parts[i ^ 2], parts[i]) for i in range(shares)]
        where = pl.ds(pl.multiple_of(n * own, own), own)
        keep_ref[0, where], keep_ref[1, where] = parts[0], parts[3]
        send_ref[0, where], send_ref[1, where] = parts[1], parts[2]
        return dzb

    def behind(i, adj):
        n = depth - 1 - i
        return adj + convolve(back_w_ref[n], layer(n, adj))

    layer(0, lax.fori_loop(0, depth - 1, behind, adj))


def halve_kernel(mine_ref, got_ref, adj_ref, state_ref, keep_ref, send_ref, adj_out, state_out):
    keep_ref[...] = mine_ref[0] + got_ref[0]
    send_ref[...] = mine_ref[1] + got_ref[1]
    adj_out[...] = adj_ref[...]
    state_out[...] = state_ref[...]


def total_kernel(
    mine_ref, got_ref, adj_ref, state_ref, grad_ref, bias_ref, adj_hbm, state_hbm, sems
):
    copies = [
        pltpu.make_async_copy(src, dst, sems.at[k])
        for k, (src, dst) in enumerate(((adj_ref, adj_hbm), (state_ref, state_hbm)))
    ]
    for copy in copies:
        copy.start()
    depth, own, width = grad_ref.shape
    total = mine_ref[...] + got_ref[...]
    eye = lax.broadcasted_iota(jnp.int32, (own, own), 0) == lax.broadcasted_iota(
        jnp.int32, (own, own), 1
    )
    for n in range(depth):
        mine = total[n * own : (n + 1) * own]
        grad_ref[n] = mine[:, :width]
        column = jnp.broadcast_to(mine[:, width : width + 1], (own, own))
        bias_ref[n : n + 1, :] = jnp.sum(jnp.where(eye, column, 0.0), axis=0, keepdims=True)
    for copy in copies:
        copy.wait()


def call(kernel, out_shape, args, hbm_in=(), hbm_out=(), scratch=()):
    return pl.pallas_call(
        kernel,
        out_shape=out_shape,
        in_specs=[HBM if k in hbm_in else VMEM for k in range(len(args))],
        out_specs=[HBM if k in hbm_out else VMEM for k in range(len(out_shape))],
        scratch_shapes=list(scratch),
        compiler_params=pltpu.CompilerParams(vmem_limit_bytes=LIMIT),
        cost_estimate=pl.CostEstimate(flops=2**28, bytes_accessed=2**20, transcendentals=0),
    )(*(pltpu.with_memory_space_constraint(a, pltpu.HBM) if k in hbm_in else a for k, a in enumerate(args)))


def f32(*shape):
    return jax.ShapeDtypeStruct(shape, jnp.float32)


def bf16(*shape):
    return jax.ShapeDtypeStruct(shape, jnp.bfloat16)


def exchange(x, partner):
    blocks, shares = lax.axis_size("layer"), lax.axis_size("dp")
    pairs = []
    for layer in range(blocks):
        for dp in range(shares):
            to = partner(layer, dp)
            pairs.append((layer * shares + dp, to[0] * shares + to[1]))
    return lax.ppermute(x, ("layer", "dp"), pairs)


def across(x, step):
    return exchange(x, lambda layer, dp: (layer ^ (1 << step), dp ^ 1))


def image_swap(x):
    return exchange(x, lambda layer, dp: (layer, dp ^ (layer.bit_count() % 2)))


def local(state_guess, adjoint_guess, conv_weight, conv_bias):
    depth, chans, width = conv_weight.shape
    shares = lax.axis_size("dp")
    steps = lax.axis_size("layer").bit_length() - 1
    state_guess = image_swap(state_guess)
    adjoint_guess = image_swap(adjoint_guess)
    by_tap, back_w, columns = call(
        weight_kernel,
        (bf16(depth, chans, width), bf16(depth, chans, width), f32(depth, 2, chans, HALF)),
        (conv_weight, conv_bias),
        hbm_in=(0, 1),
        scratch=[
            pltpu.VMEM(conv_weight.shape, conv_weight.dtype),
            pltpu.VMEM(conv_bias.shape, conv_bias.dtype),
            pltpu.SemaphoreType.DMA((2,)),
        ],
    )
    total, slope, rounded = call(
        relax_kernel,
        (f32(3, chans, HW), f32(depth, chans, HW), bf16(depth, chans, HW)),
        (state_guess, adjoint_guess, by_tap, back_w, columns),
    )
    (patch,) = call(patch_kernel, (bf16(depth, width, HW),), (rounded,))
    mine = ()
    for step in range(1, steps):
        got = across(total, step - 1)
        final = step == steps - 1
        total, *mine = call(
            functools.partial(join_kernel, step, final),
            (f32(chans, HW) if final else f32(3, chans, HW), f32(4, chans, HW)),
            (total, got, *mine),
        )
    got = across(total, steps - 1)
    lanes = -(-(width + 1) // HALF) * HALF
    part = (depth * chans // shares, lanes)
    one = f32(*state_guess.shape)
    adjoint_fixed, state_fixed, keep, send = call(
        functools.partial(grad_kernel, steps),
        (one, one, f32(shares // 2, *part), f32(shares // 2, *part)),
        (got, *mine, adjoint_guess, state_guess, slope, patch, back_w),
    )
    got = exchange(send, lambda layer, dp: (layer, dp ^ 1))
    keep, send, adjoint_fixed, state_fixed = call(
        halve_kernel,
        (f32(*part), f32(*part), one, one),
        (keep, got, adjoint_fixed, state_fixed),
    )
    got = exchange(send, lambda layer, dp: (layer, dp ^ 3))
    weight_grad, bias_grad, adjoint_fixed, state_fixed = call(
        total_kernel,
        (f32(depth, chans // shares, width), f32(depth, chans // shares), one, one),
        (keep, got, image_swap(adjoint_fixed), image_swap(state_fixed)),
        hbm_out=(2, 3),
        scratch=[pltpu.SemaphoreType.DMA((2,))],
    )
    return (state_fixed, adjoint_fixed, weight_grad, bias_grad)


def solution(mesh):
    placed = (
        P("layer", "dp", None, None),
        P("layer", "dp", None, None),
        P("layer", None, None),
        P("layer", None),
    )
    return jax.shard_map(
        local,
        mesh=mesh,
        in_specs=placed,
        out_specs=(
            P("layer", "dp", None, None),
            P("layer", "dp", None, None),
            P("layer", "dp", None),
            P("layer", "dp"),
        ),
        check_vma=False,
    )
```

```python
import functools

import jax
import jax.numpy as jnp
from jax import lax
from jax.experimental import pallas as pl
from jax.experimental.pallas import tpu as pltpu
from jax.sharding import PartitionSpec as P

IMG = 16
HW = IMG * IMG
HALF = 128
TAPS = 9
STEP = 0.5
LIMIT = 32 * 1024 * 1024

VMEM = pl.BlockSpec(memory_space=pltpu.VMEM)
HBM = pl.BlockSpec(memory_space=pltpu.HBM)


def picked(low, high, source, from_high):
    return jnp.where(
        from_high,
        jnp.take_along_axis(high, source, axis=1, mode="promise_in_bounds"),
        jnp.take_along_axis(low, source, axis=1, mode="promise_in_bounds"),
    )


def lanes_of(values):
    lane = lax.broadcasted_iota(jnp.int32, (values.shape[0], HALF), 1)
    return lane // IMG, lane % IMG


def by_parity(values):
    line, col = lanes_of(values)
    low, high = values[:, :HALF], values[:, HALF:]
    half = IMG // 4
    return jnp.concatenate(
        [
            picked(low, high, (2 * (line % half) + odd) * IMG + col, line >= half)
            for odd in range(2)
        ],
        axis=1,
    )


def in_order(values):
    line, col = lanes_of(values)
    even, odd = values[:, :HALF], values[:, HALF:]
    return jnp.concatenate(
        [
            picked(even, odd, (half * (IMG // 4) + line // 2) * IMG + col, line % 2 == 1)
            for half in range(2)
        ],
        axis=1,
    )


def taps_of(values):
    even, odd = values[:, :HALF], values[:, HALF:]
    lane = lax.broadcasted_iota(jnp.int16, even.shape, 1)
    col = lane & (IMG - 1)
    cols = {-1: [col >= 1], 0: [], 1: [col < IMG - 1]}

    def turned(half, lines, right):
        by = lines * IMG + right
        if not by:
            return half
        tests = cols[right] + {-1: [lane >= IMG], 0: [], 1: [lane < HALF - IMG]}[lines]
        part = pltpu.roll(half, -by % HALF, 1)
        return jnp.where(functools.reduce(jnp.logical_and, tests), part, jnp.zeros_like(part))

    above, here, below = [], [], []
    for right in (-1, 0, 1):
        same = turned(even, 0, right), turned(odd, 0, right)
        above.append((turned(odd, -1, right), same[0]))
        here.append(same)
        below.append((same[1], turned(even, 1, right)))
    return jnp.concatenate(
        [jnp.concatenate(pair, axis=1) for pair in above + here + below], axis=0
    )


def permutation(chans):
    size = TAPS * chans
    row = lax.broadcasted_iota(jnp.int32, (size, size), 0)
    column = lax.broadcasted_iota(jnp.int32, (size, size), 1)
    tap = lax.div(row, chans)
    return jnp.where(column == (row - tap * chans) * TAPS + tap, 1.0, 0.0).astype(jnp.bfloat16)


def dot(a, b, dims):
    return lax.dot_general(a, b, (dims, ((), ())), preferred_element_type=jnp.float32)


def convolve(weight, values):
    return dot(weight, taps_of(values), ((1,), (0,)))


def relax_kernel(
    state_hbm,
    adj_hbm,
    w_hbm,
    bias_hbm,
    guess_ref,
    sent_ref,
    slope_ref,
    rounded_ref,
    back_w_ref,
    state_ref,
    adj_ref,
    w_ref,
    bias_ref,
    sems,
):
    copies = [
        pltpu.make_async_copy(src, dst, sems.at[k])
        for k, (src, dst) in enumerate(
            ((w_hbm, w_ref), (state_hbm, state_ref), (bias_hbm, bias_ref), (adj_hbm, adj_ref))
        )
    ]
    for copy in copies:
        copy.start()
    depth, chans, width = w_ref.shape
    perm = permutation(chans)
    eye = lax.broadcasted_iota(jnp.int32, (chans, chans), 0) == lax.broadcasted_iota(
        jnp.int32, (chans, chans), 1
    )
    for copy in copies:
        copy.wait()
    weights = w_ref[...].reshape(depth * chans, width)
    by_tap = dot(weights, perm, ((1,), (1,)))
    turned = dot(perm, weights, ((1,), (1,))).astype(jnp.bfloat16)
    middle = TAPS // 2 * chans
    start = by_parity(state_ref[0, 0])
    guess = by_parity(adj_ref[0, 0])
    guess_ref[...] = guess
    state = start
    gain = None
    slopes = []
    backs = []
    for n in range(depth):
        mine = slice(n * chans, (n + 1) * chans)
        bias = jnp.broadcast_to(bias_ref[n : n + 1, :], (chans, chans))
        bias, kc = (
            jnp.sum(jnp.where(eye, square, 0.0), axis=1, keepdims=True)
            for square in (bias, by_tap[mine, middle : middle + chans])
        )
        rounded = state.astype(jnp.bfloat16)
        rounded_ref[n] = rounded
        squash = jnp.tanh(convolve(by_tap[mine].astype(jnp.bfloat16), rounded) + bias)
        slope = STEP * (1.0 - squash * squash)
        slope_ref[n] = slope
        slopes.append(slope)
        state = state + STEP * squash
        factor = 1.0 + slope * kc
        gain = factor if gain is None else gain * factor
        back_w = jnp.concatenate(
            [turned[t * chans : (t + 1) * chans, mine] for t in reversed(range(TAPS))], axis=1
        )
        back_w_ref[n] = back_w
        backs.append(back_w)
    back = guess
    for n in reversed(range(depth)):
        back = back + convolve(backs[n], (back * slopes[n]).astype(jnp.bfloat16))
    place = lax.axis_index("layer")
    first = jnp.where(place == 0, 0.0, start)
    last = jnp.where(place == lax.axis_size("layer") - 1, 0.0, guess)
    sent_ref[0] = gain
    sent_ref[1] = state - gain * first
    sent_ref[2] = back - gain * last


def patch_kernel(rounded_ref, patch_ref):
    depth, chans, _ = rounded_ref.shape
    perm = permutation(chans)
    for n in range(depth):
        patch = taps_of(rounded_ref[n])
        patch_ref[n] = dot(perm, patch, ((0,), (0,))).astype(jnp.bfloat16)


def joined(bit, total, mine, got):
    gain, fwd, bwd = total
    pre_gain, pre, post_gain, post = mine
    got_gain, got_fwd, got_bwd = got
    total = (
        gain * got_gain,
        jnp.where(bit, gain * got_fwd + fwd, got_gain * fwd + got_fwd),
        jnp.where(bit, got_gain * bwd + got_bwd, gain * got_bwd + bwd),
    )
    mine = (
        jnp.where(bit, pre_gain * got_gain, pre_gain),
        jnp.where(bit, pre_gain * got_fwd + pre, pre),
        jnp.where(bit, post_gain, post_gain * got_gain),
        jnp.where(bit, post, post_gain * got_bwd + post),
    )
    return total, mine


def bit_of(axis, step):
    return lax.rem(lax.div(lax.axis_index(axis), 2**step), 2) == 1


def join_kernel(step, final, *refs):
    if step == 1:
        total_ref, got_ref, sent_ref, mine_out = refs
        one = jnp.ones(total_ref.shape[1:], jnp.float32)
        zero = jnp.zeros(total_ref.shape[1:], jnp.float32)
        mine = (one, zero, one, zero)
    else:
        total_ref, got_ref, mine_ref, sent_ref, mine_out = refs
        mine = tuple(mine_ref[k] for k in range(4))
    total = tuple(total_ref[k] for k in range(3))
    got = tuple(got_ref[k] for k in range(3))
    total, mine = joined(bit_of("layer", step - 1), total, mine, got)
    for k in range(4):
        mine_out[k] = mine[k]
    if final:
        sent_ref[...] = jnp.where(bit_of("layer", step), total[2], total[1])
    else:
        for k in range(3):
            sent_ref[k] = total[k]


def later_fixed(steps, got_ref, mine_ref):
    got = jnp.where(bit_of("layer", steps - 1), 0.0, mine_ref[2] * got_ref[...])
    return mine_ref[3] + got


def fixed_kernel(steps, _, got_ref, mine_ref, guess_ref, start_ref, adj_ref, state_ref):
    place = lax.axis_index("layer")
    adj = in_order(later_fixed(steps, got_ref, mine_ref))
    got = jnp.where(bit_of("layer", steps - 1), mine_ref[0] * got_ref[...], 0.0)
    state = in_order(mine_ref[1] + got)
    adj_ref[0, 0] = jnp.where(place == lax.axis_size("layer") - 1, guess_ref[0, 0], adj)
    state_ref[0, 0] = jnp.where(place == 0, start_ref[0, 0], state)


def grad_kernel(
    steps,
    got_ref,
    mine_ref,
    guess_ref,
    slope_ref,
    patch_ref,
    back_w_ref,
    keep_ref,
    send_ref,
):
    depth, chans, rows = back_w_ref.shape
    shares = 2 * keep_ref.shape[0]
    own = chans // shares
    last = lax.axis_index("layer") == lax.axis_size("layer") - 1
    adj = jnp.where(last, guess_ref[...], later_fixed(steps, got_ref, mine_ref))
    pad = keep_ref.shape[2] - rows
    odd, high = bit_of("dp", 0), bit_of("dp", 1)

    def layer(n, adj):
        dz = adj * slope_ref[n]
        dzb = dz.astype(jnp.bfloat16)
        grad = dot(dzb, patch_ref[n], ((1,), (1,)))
        bias = jnp.broadcast_to(jnp.sum(dz, axis=1, keepdims=True), (chans, pad))
        both = jnp.concatenate([grad, bias], axis=1)
        parts = [both[s * own : (s + 1) * own] for s in range(shares)]
        parts = [jnp.where(odd, parts[i ^ 1], parts[i]) for i in range(shares)]
        parts = [jnp.where(high, parts[i ^ 2], parts[i]) for i in range(shares)]
        where = pl.ds(pl.multiple_of(n * own, own), own)
        keep_ref[0, where], keep_ref[1, where] = parts[0], parts[3]
        send_ref[0, where], send_ref[1, where] = parts[1], parts[2]
        return dzb

    def behind(i, adj):
        n = depth - 1 - i
        return adj + convolve(back_w_ref[n], layer(n, adj))

    layer(0, lax.fori_loop(0, depth - 1, behind, adj))


def halve_kernel(mine_ref, got_ref, keep_ref, send_ref):
    keep_ref[...] = mine_ref[0] + got_ref[0]
    send_ref[...] = mine_ref[1] + got_ref[1]


def total_kernel(mine_ref, got_ref, grad_ref, bias_ref):
    depth, own, width = grad_ref.shape
    total = mine_ref[...] + got_ref[...]
    eye = lax.broadcasted_iota(jnp.int32, (own, own), 0) == lax.broadcasted_iota(
        jnp.int32, (own, own), 1
    )
    for n in range(depth):
        mine = total[n * own : (n + 1) * own]
        grad_ref[n] = mine[:, :width]
        column = jnp.broadcast_to(mine[:, width : width + 1], (own, own))
        bias_ref[n : n + 1, :] = jnp.sum(jnp.where(eye, column, 0.0), axis=0, keepdims=True)


def call(kernel, out_shape, args, hbm_in=(), hbm_out=(), scratch=()):
    return pl.pallas_call(
        kernel,
        out_shape=out_shape,
        in_specs=[HBM if k in hbm_in else VMEM for k in range(len(args))],
        out_specs=[HBM if k in hbm_out else VMEM for k in range(len(out_shape))],
        scratch_shapes=list(scratch),
        compiler_params=pltpu.CompilerParams(vmem_limit_bytes=LIMIT),
        cost_estimate=pl.CostEstimate(flops=2**28, bytes_accessed=2**20, transcendentals=0),
    )(*(pltpu.with_memory_space_constraint(a, pltpu.HBM) if k in hbm_in else a for k, a in enumerate(args)))


def f32(*shape):
    return jax.ShapeDtypeStruct(shape, jnp.float32)


def bf16(*shape):
    return jax.ShapeDtypeStruct(shape, jnp.bfloat16)


def exchange(x, axis, mask):
    return lax.ppermute(x, axis, [(i, i ^ mask) for i in range(lax.axis_size(axis))])


def local(state_guess, adjoint_guess, conv_weight, conv_bias):
    depth, chans, width = conv_weight.shape
    shares = lax.axis_size("dp")
    steps = lax.axis_size("layer").bit_length() - 1
    args = (state_guess, adjoint_guess, conv_weight, conv_bias)
    guess, total, slope, rounded, back_w = call(
        relax_kernel,
        (
            f32(chans, HW),
            f32(3, chans, HW),
            f32(depth, chans, HW),
            bf16(depth, chans, HW),
            bf16(depth, chans, width),
        ),
        args,
        hbm_in=range(4),
        scratch=[pltpu.VMEM(a.shape, a.dtype) for a in args] + [pltpu.SemaphoreType.DMA((4,))],
    )
    (patch,) = call(patch_kernel, (bf16(depth, width, HW),), (rounded,))
    mine = ()
    for step in range(1, steps):
        got = exchange(total, "layer", 1 << (step - 1))
        final = step == steps - 1
        total, *mine = call(
            functools.partial(join_kernel, step, final),
            (f32(chans, HW) if final else f32(3, chans, HW), f32(4, chans, HW)),
            (total, got, *mine),
        )
    got = exchange(total, "layer", 1 << (steps - 1))
    lanes = -(-(width + 1) // HALF) * HALF
    part = (depth * chans // shares, lanes)
    keep, send = call(
        functools.partial(grad_kernel, steps),
        (f32(shares // 2, *part), f32(shares // 2, *part)),
        (got, *mine, guess, slope, patch, back_w),
    )
    adjoint_fixed, state_fixed = call(
        functools.partial(fixed_kernel, steps),
        (f32(*adjoint_guess.shape), f32(*state_guess.shape)),
        (keep, got, *mine, adjoint_guess, state_guess),
    )
    keep, send = call(halve_kernel, (f32(*part), f32(*part)), (keep, exchange(send, "dp", 1)))
    weight_grad, bias_grad = call(
        total_kernel,
        (f32(depth, chans // shares, width), f32(depth, chans // shares)),
        (keep, exchange(send, "dp", 3)),
    )
    return (state_fixed, adjoint_fixed, weight_grad, bias_grad)


def solution(mesh):
    placed = (
        P("layer", "dp", None, None),
        P("layer", "dp", None, None),
        P("layer", None, None),
        P("layer", None),
    )
    return jax.shard_map(
        local,
        mesh=mesh,
        in_specs=placed,
        out_specs=(
            P("layer", "dp", None, None),
            P("layer", "dp", None, None),
            P("layer", "dp", None),
            P("layer", "dp"),
        ),
        check_vma=False,
    )
```

```python
import functools

import jax
import jax.numpy as jnp
from jax import lax
from jax.experimental import pallas as pl
from jax.experimental.pallas import tpu as pltpu
from jax.sharding import PartitionSpec as P

IMG = 16
HW = IMG * IMG
HALF = 128
TAPS = 9
STEP = 0.5
LIMIT = 32 * 1024 * 1024

VMEM = pl.BlockSpec(memory_space=pltpu.VMEM)
HBM = pl.BlockSpec(memory_space=pltpu.HBM)


def picked(low, high, source, from_high):
    return jnp.where(
        from_high,
        jnp.take_along_axis(high, source, axis=1, mode="promise_in_bounds"),
        jnp.take_along_axis(low, source, axis=1, mode="promise_in_bounds"),
    )


def lanes_of(values):
    lane = lax.broadcasted_iota(jnp.int32, (values.shape[0], HALF), 1)
    return lane // IMG, lane % IMG


def by_parity(values):
    line, col = lanes_of(values)
    low, high = values[:, :HALF], values[:, HALF:]
    half = IMG // 4
    return jnp.concatenate(
        [
            picked(low, high, (2 * (line % half) + odd) * IMG + col, line >= half)
            for odd in range(2)
        ],
        axis=1,
    )


def in_order(values):
    line, col = lanes_of(values)
    even, odd = values[:, :HALF], values[:, HALF:]
    return jnp.concatenate(
        [
            picked(even, odd, (half * (IMG // 4) + line // 2) * IMG + col, line % 2 == 1)
            for half in range(2)
        ],
        axis=1,
    )


def taps_of(values):
    even, odd = values[:, :HALF], values[:, HALF:]
    lane = lax.broadcasted_iota(jnp.int16, even.shape, 1)
    col = lane & (IMG - 1)
    cols = {-1: [col >= 1], 0: [], 1: [col < IMG - 1]}

    def turned(half, lines, right):
        by = lines * IMG + right
        if not by:
            return half
        tests = cols[right] + {-1: [lane >= IMG], 0: [], 1: [lane < HALF - IMG]}[lines]
        part = pltpu.roll(half, -by % HALF, 1)
        return jnp.where(functools.reduce(jnp.logical_and, tests), part, jnp.zeros_like(part))

    above, here, below = [], [], []
    for right in (-1, 0, 1):
        same = turned(even, 0, right), turned(odd, 0, right)
        above.append((turned(odd, -1, right), same[0]))
        here.append(same)
        below.append((same[1], turned(even, 1, right)))
    return jnp.concatenate(
        [jnp.concatenate(pair, axis=1) for pair in above + here + below], axis=0
    )


def permutation(chans):
    size = TAPS * chans
    row = lax.broadcasted_iota(jnp.int32, (size, size), 0)
    column = lax.broadcasted_iota(jnp.int32, (size, size), 1)
    tap = lax.div(row, chans)
    return jnp.where(column == (row - tap * chans) * TAPS + tap, 1.0, 0.0).astype(jnp.bfloat16)


def dot(a, b, dims):
    return lax.dot_general(a, b, (dims, ((), ())), preferred_element_type=jnp.float32)


def convolve(weight, values):
    return dot(weight, taps_of(values), ((1,), (0,)))


def relax_kernel(
    state_hbm,
    adj_hbm,
    w_hbm,
    bias_hbm,
    guess_ref,
    sent_ref,
    slope_ref,
    rounded_ref,
    back_w_ref,
    state_ref,
    adj_ref,
    w_ref,
    bias_ref,
    sems,
):
    copies = [
        pltpu.make_async_copy(src, dst, sems.at[k])
        for k, (src, dst) in enumerate(
            ((w_hbm, w_ref), (state_hbm, state_ref), (bias_hbm, bias_ref), (adj_hbm, adj_ref))
        )
    ]
    for copy in copies:
        copy.start()
    depth, chans, width = w_ref.shape
    perm = permutation(chans)
    eye = lax.broadcasted_iota(jnp.int32, (chans, chans), 0) == lax.broadcasted_iota(
        jnp.int32, (chans, chans), 1
    )
    for copy in copies:
        copy.wait()
    weights = w_ref[...].reshape(depth * chans, width)
    by_tap = dot(weights, perm, ((1,), (1,)))
    turned = dot(perm, weights, ((1,), (1,))).astype(jnp.bfloat16)
    middle = TAPS // 2 * chans
    start = by_parity(state_ref[0, 0])
    guess = by_parity(adj_ref[0, 0])
    guess_ref[...] = guess
    state = start
    gain = None
    slopes = []
    backs = []
    for n in range(depth):
        mine = slice(n * chans, (n + 1) * chans)
        bias = jnp.broadcast_to(bias_ref[n : n + 1, :], (chans, chans))
        bias, kc = (
            jnp.sum(jnp.where(eye, square, 0.0), axis=1, keepdims=True)
            for square in (bias, by_tap[mine, middle : middle + chans])
        )
        rounded = state.astype(jnp.bfloat16)
        rounded_ref[n] = rounded
        squash = jnp.tanh(convolve(by_tap[mine].astype(jnp.bfloat16), rounded) + bias)
        slope = STEP * (1.0 - squash * squash)
        slope_ref[n] = slope
        slopes.append(slope)
        state = state + STEP * squash
        factor = 1.0 + slope * kc
        gain = factor if gain is None else gain * factor
        back_w = jnp.concatenate(
            [turned[t * chans : (t + 1) * chans, mine] for t in reversed(range(TAPS))], axis=1
        )
        back_w_ref[n] = back_w
        backs.append(back_w)
    back = guess
    for n in reversed(range(depth)):
        back = back + convolve(backs[n], (back * slopes[n]).astype(jnp.bfloat16))
    place = lax.axis_index("layer")
    first = jnp.where(place == 0, 0.0, start)
    last = jnp.where(place == lax.axis_size("layer") - 1, 0.0, guess)
    sent_ref[0] = gain
    sent_ref[1] = state - gain * first
    sent_ref[2] = back - gain * last


def patch_kernel(rounded_ref, patch_ref):
    depth, chans, _ = rounded_ref.shape
    perm = permutation(chans)
    for n in range(depth):
        patch = taps_of(rounded_ref[n])
        patch_ref[n] = dot(perm, patch, ((0,), (0,))).astype(jnp.bfloat16)


def joined(bit, total, mine, got):
    gain, fwd, bwd = total
    pre_gain, pre, post_gain, post = mine
    got_gain, got_fwd, got_bwd = got
    total = (
        gain * got_gain,
        jnp.where(bit, gain * got_fwd + fwd, got_gain * fwd + got_fwd),
        jnp.where(bit, got_gain * bwd + got_bwd, gain * got_bwd + bwd),
    )
    mine = (
        jnp.where(bit, pre_gain * got_gain, pre_gain),
        jnp.where(bit, pre_gain * got_fwd + pre, pre),
        jnp.where(bit, post_gain, post_gain * got_gain),
        jnp.where(bit, post, post_gain * got_bwd + post),
    )
    return total, mine


def bit_of(axis, step):
    return lax.rem(lax.div(lax.axis_index(axis), 2**step), 2) == 1


def join_kernel(step, narrow, *refs):
    if step == 1:
        total_ref, got_ref, sent_ref, fwd_out, mine_out = refs
        one = jnp.ones(total_ref.shape[1:], jnp.float32)
        zero = jnp.zeros(total_ref.shape[1:], jnp.float32)
        mine = (one, zero, one, zero)
    else:
        total_ref, got_ref, mine_ref, sent_ref, fwd_out, mine_out = refs
        mine = tuple(mine_ref[k] for k in range(4))
    total = tuple(total_ref[k] for k in range(3))
    got = tuple(got_ref[k] for k in range(3))
    (gain, fwd, bwd), mine = joined(bit_of("layer", step - 1), total, mine, got)
    for k in range(4):
        mine_out[k] = mine[k]
    fwd_out[...] = fwd
    sent_ref[0] = gain
    if narrow:
        first = jnp.logical_not(jnp.logical_or(bit_of("layer", step), bit_of("layer", step + 1)))
        sent_ref[1] = jnp.where(first, fwd, bwd)
    else:
        sent_ref[1] = fwd
        sent_ref[2] = bwd


def quarters_kernel(steps, total_ref, fwd_ref, got_ref, mine_ref, sent_ref, late_ref, mine_out):
    odd, upper = bit_of("layer", steps - 2), bit_of("layer", steps - 1)
    gain, bwd, fwd = total_ref[0], total_ref[1], fwd_ref[...]
    got_gain, got = got_ref[0], got_ref[1]
    pre_gain, pre, post_gain, post = (mine_ref[k] for k in range(4))
    low_fwd = gain * got + fwd
    up_bwd = jnp.where(odd, got_gain * bwd + got, gain * got + bwd)
    sent_ref[...] = jnp.where(upper, up_bwd, low_fwd)
    late_ref[...] = jnp.where(upper, fwd, low_fwd)
    second = jnp.logical_and(odd, jnp.logical_not(upper))
    mine_out[0] = pre_gain
    mine_out[1] = jnp.where(second, pre_gain * got + pre, pre)
    mine_out[2] = jnp.where(odd, post_gain, post_gain * got_gain)
    mine_out[3] = jnp.where(odd, post, post_gain * got + post)
    mine_out[4] = got_gain


def later_fixed(steps, got_ref, mine_ref):
    got = jnp.where(bit_of("layer", steps - 1), 0.0, mine_ref[2] * got_ref[...])
    return mine_ref[3] + got


def fixed_kernel(steps, _, got_ref, late_ref, mine_ref, guess_ref, start_ref, adj_ref, state_ref):
    odd, upper = bit_of("layer", steps - 2), bit_of("layer", steps - 1)
    place = lax.axis_index("layer")
    adj = in_order(later_fixed(steps, got_ref, mine_ref))
    late = late_ref[...]
    came = jnp.where(odd, mine_ref[4] * got_ref[...] + late, late)
    state = in_order(mine_ref[1] + jnp.where(upper, mine_ref[0] * came, 0.0))
    adj_ref[0, 0] = jnp.where(place == lax.axis_size("layer") - 1, guess_ref[0, 0], adj)
    state_ref[0, 0] = jnp.where(place == 0, start_ref[0, 0], state)


def grad_kernel(
    steps,
    got_ref,
    mine_ref,
    guess_ref,
    slope_ref,
    patch_ref,
    back_w_ref,
    parts_ref,
):
    depth, chans, rows = back_w_ref.shape
    shares = parts_ref.shape[0]
    own = chans // shares
    last = lax.axis_index("layer") == lax.axis_size("layer") - 1
    adj = jnp.where(last, guess_ref[...], later_fixed(steps, got_ref, mine_ref))
    pad = parts_ref.shape[2] - rows

    def layer(n, adj):
        dz = adj * slope_ref[n]
        dzb = dz.astype(jnp.bfloat16)
        grad = dot(dzb, patch_ref[n], ((1,), (1,)))
        bias = jnp.broadcast_to(jnp.sum(dz, axis=1, keepdims=True), (chans, pad))
        both = jnp.concatenate([grad, bias], axis=1)
        where = pl.ds(pl.multiple_of(n * own, own), own)
        for k in range(shares):
            parts_ref[k, where] = both[k * own : (k + 1) * own]
        return dzb

    def behind(i, adj):
        n = depth - 1 - i
        return adj + convolve(back_w_ref[n], layer(n, adj))

    layer(0, lax.fori_loop(0, depth - 1, behind, adj))


def deal_kernel(_, parts_ref, keep_ref, send_ref):
    odd, high = bit_of("dp", 0), bit_of("dp", 1)
    parts = [parts_ref[i] for i in range(parts_ref.shape[0])]
    parts = [jnp.where(odd, parts[i ^ 1], parts[i]) for i in range(len(parts))]
    parts = [jnp.where(high, parts[i ^ 2], parts[i]) for i in range(len(parts))]
    keep_ref[0], keep_ref[1] = parts[0], parts[3]
    send_ref[0], send_ref[1] = parts[1], parts[2]


def halve_kernel(mine_ref, got_ref, keep_ref, send_ref):
    keep_ref[...] = mine_ref[0] + got_ref[0]
    send_ref[...] = mine_ref[1] + got_ref[1]


def total_kernel(mine_ref, got_ref, grad_ref, bias_ref):
    depth, own, width = grad_ref.shape
    total = mine_ref[...] + got_ref[...]
    eye = lax.broadcasted_iota(jnp.int32, (own, own), 0) == lax.broadcasted_iota(
        jnp.int32, (own, own), 1
    )
    for n in range(depth):
        mine = total[n * own : (n + 1) * own]
        grad_ref[n] = mine[:, :width]
        column = jnp.broadcast_to(mine[:, width : width + 1], (own, own))
        bias_ref[n : n + 1, :] = jnp.sum(jnp.where(eye, column, 0.0), axis=0, keepdims=True)


def call(kernel, out_shape, args, hbm_in=(), hbm_out=(), scratch=(), work=2**28):
    return pl.pallas_call(
        kernel,
        out_shape=out_shape,
        in_specs=[HBM if k in hbm_in else VMEM for k in range(len(args))],
        out_specs=[HBM if k in hbm_out else VMEM for k in range(len(out_shape))],
        scratch_shapes=list(scratch),
        compiler_params=pltpu.CompilerParams(vmem_limit_bytes=LIMIT),
        cost_estimate=pl.CostEstimate(flops=work, bytes_accessed=work // 256, transcendentals=0),
    )(*(pltpu.with_memory_space_constraint(a, pltpu.HBM) if k in hbm_in else a for k, a in enumerate(args)))


def f32(*shape):
    return jax.ShapeDtypeStruct(shape, jnp.float32)


def bf16(*shape):
    return jax.ShapeDtypeStruct(shape, jnp.bfloat16)


def exchange(x, axis, mask):
    return lax.ppermute(x, axis, [(i, i ^ mask) for i in range(lax.axis_size(axis))])


def local(state_guess, adjoint_guess, conv_weight, conv_bias):
    depth, chans, width = conv_weight.shape
    shares = lax.axis_size("dp")
    steps = lax.axis_size("layer").bit_length() - 1
    args = (state_guess, adjoint_guess, conv_weight, conv_bias)
    guess, total, slope, rounded, back_w = call(
        relax_kernel,
        (
            f32(chans, HW),
            f32(3, chans, HW),
            f32(depth, chans, HW),
            bf16(depth, chans, HW),
            bf16(depth, chans, width),
        ),
        args,
        hbm_in=range(4),
        scratch=[pltpu.VMEM(a.shape, a.dtype) for a in args] + [pltpu.SemaphoreType.DMA((4,))],
    )
    (patch,) = call(patch_kernel, (bf16(depth, width, HW),), (rounded,))
    mine = ()
    one = f32(chans, HW)
    for step in range(1, steps - 1):
        got = exchange(total, "layer", 1 << (step - 1))
        narrow = step == steps - 2
        total, fwd, *mine = call(
            functools.partial(join_kernel, step, narrow),
            (f32(2 if narrow else 3, chans, HW), one, f32(4, chans, HW)),
            (total, got, *mine),
        )
    got = exchange(total, "layer", 1 << (steps - 2))
    total, late, *mine = call(
        functools.partial(quarters_kernel, steps),
        (one, one, f32(5, chans, HW)),
        (total, fwd, got, *mine),
    )
    got = exchange(total, "layer", 1 << (steps - 1))
    quarter = 1 << (steps - 2)
    late = lax.ppermute(late, "layer", [(i, i + quarter) for i in range(quarter, 3 * quarter)])
    lanes = -(-(width + 1) // HALF) * HALF
    part = (depth * chans // shares, lanes)
    (parts,) = call(
        functools.partial(grad_kernel, steps),
        (f32(shares, *part),),
        (got, *mine, guess, slope, patch, back_w),
        work=0,
    )
    keep, send = call(
        deal_kernel,
        (f32(shares // 2, *part), f32(shares // 2, *part)),
        (late, parts),
        work=0,
    )
    adjoint_fixed, state_fixed = call(
        functools.partial(fixed_kernel, steps),
        (f32(*adjoint_guess.shape), f32(*state_guess.shape)),
        (keep, got, late, *mine, adjoint_guess, state_guess),
    )
    keep, send = call(halve_kernel, (f32(*part), f32(*part)), (keep, exchange(send, "dp", 1)))
    weight_grad, bias_grad = call(
        total_kernel,
        (f32(depth, chans // shares, width), f32(depth, chans // shares)),
        (keep, exchange(send, "dp", 3)),
    )
    return (state_fixed, adjoint_fixed, weight_grad, bias_grad)


def solution(mesh):
    placed = (
        P("layer", "dp", None, None),
        P("layer", "dp", None, None),
        P("layer", None, None),
        P("layer", None),
    )
    return jax.shard_map(
        local,
        mesh=mesh,
        in_specs=placed,
        out_specs=(
            P("layer", "dp", None, None),
            P("layer", "dp", None, None),
            P("layer", "dp", None),
            P("layer", "dp"),
        ),
        check_vma=False,
    )
```

```python
import functools

import jax
import jax.numpy as jnp
from jax import lax
from jax.experimental import pallas as pl
from jax.experimental.pallas import tpu as pltpu
from jax.sharding import PartitionSpec as P

IMG = 16
HW = IMG * IMG
HALF = 128
TAPS = 9
STEP = 0.5
LIMIT = 32 * 1024 * 1024

VMEM = pl.BlockSpec(memory_space=pltpu.VMEM)
HBM = pl.BlockSpec(memory_space=pltpu.HBM)


def picked(low, high, source, from_high):
    return jnp.where(
        from_high,
        jnp.take_along_axis(high, source, axis=1, mode="promise_in_bounds"),
        jnp.take_along_axis(low, source, axis=1, mode="promise_in_bounds"),
    )


def lanes_of(values):
    lane = lax.broadcasted_iota(jnp.int32, (values.shape[0], HALF), 1)
    return lane // IMG, lane % IMG


def by_parity(values):
    line, col = lanes_of(values)
    low, high = values[:, :HALF], values[:, HALF:]
    half = IMG // 4
    return jnp.concatenate(
        [
            picked(low, high, (2 * (line % half) + odd) * IMG + col, line >= half)
            for odd in range(2)
        ],
        axis=1,
    )


def in_order(values):
    line, col = lanes_of(values)
    even, odd = values[:, :HALF], values[:, HALF:]
    return jnp.concatenate(
        [
            picked(even, odd, (half * (IMG // 4) + line // 2) * IMG + col, line % 2 == 1)
            for half in range(2)
        ],
        axis=1,
    )


def taps_of(values):
    even, odd = values[:, :HALF], values[:, HALF:]
    lane = lax.broadcasted_iota(jnp.int16, even.shape, 1)
    col = lane & (IMG - 1)
    cols = {-1: [col >= 1], 0: [], 1: [col < IMG - 1]}

    def turned(half, lines, right):
        by = lines * IMG + right
        if not by:
            return half
        tests = cols[right] + {-1: [lane >= IMG], 0: [], 1: [lane < HALF - IMG]}[lines]
        part = pltpu.roll(half, -by % HALF, 1)
        return jnp.where(functools.reduce(jnp.logical_and, tests), part, jnp.zeros_like(part))

    above, here, below = [], [], []
    for right in (-1, 0, 1):
        same = turned(even, 0, right), turned(odd, 0, right)
        above.append((turned(odd, -1, right), same[0]))
        here.append(same)
        below.append((same[1], turned(even, 1, right)))
    pairs = above + here + below
    return [jnp.concatenate([pair[half] for pair in pairs], axis=0) for half in range(2)]


def permutation(chans):
    size = TAPS * chans
    row = lax.broadcasted_iota(jnp.int32, (size, size), 0)
    column = lax.broadcasted_iota(jnp.int32, (size, size), 1)
    tap = lax.div(row, chans)
    return jnp.where(column == (row - tap * chans) * TAPS + tap, 1.0, 0.0).astype(jnp.bfloat16)


def dot(a, b, dims):
    return lax.dot_general(a, b, (dims, ((), ())), preferred_element_type=jnp.float32)


def convolve(weight, values):
    return jnp.concatenate([dot(weight, half, ((1,), (0,))) for half in taps_of(values)], axis=1)


def relax_kernel(
    state_hbm,
    adj_hbm,
    w_hbm,
    bias_hbm,
    guess_ref,
    sent_ref,
    slope_ref,
    rounded_ref,
    back_w_ref,
    state_ref,
    adj_ref,
    w_ref,
    bias_ref,
    sems,
):
    copies = [
        pltpu.make_async_copy(src, dst, sems.at[k])
        for k, (src, dst) in enumerate(
            ((w_hbm, w_ref), (state_hbm, state_ref), (bias_hbm, bias_ref), (adj_hbm, adj_ref))
        )
    ]
    for copy in copies:
        copy.start()
    depth, chans, width = w_ref.shape
    perm = permutation(chans)
    eye = lax.broadcasted_iota(jnp.int32, (chans, chans), 0) == lax.broadcasted_iota(
        jnp.int32, (chans, chans), 1
    )
    for copy in copies[:-1]:
        copy.wait()
    weights = w_ref[...].reshape(depth * chans, width)
    by_tap = dot(weights, perm, ((1,), (1,)))
    turned = dot(perm, weights, ((1,), (1,))).astype(jnp.bfloat16)
    middle = TAPS // 2 * chans
    start = by_parity(state_ref[0, 0])
    state = start
    gain = None
    slopes = []
    backs = []
    for n in range(depth):
        mine = slice(n * chans, (n + 1) * chans)
        bias = jnp.broadcast_to(bias_ref[n : n + 1, :], (chans, chans))
        bias, kc = (
            jnp.sum(jnp.where(eye, square, 0.0), axis=1, keepdims=True)
            for square in (bias, by_tap[mine, middle : middle + chans])
        )
        rounded = state.astype(jnp.bfloat16)
        rounded_ref[n] = rounded
        squash = jnp.tanh(convolve(by_tap[mine].astype(jnp.bfloat16), rounded) + bias)
        slope = STEP * (1.0 - squash * squash)
        slope_ref[n] = slope
        slopes.append(slope)
        state = state + STEP * squash
        factor = 1.0 + slope * kc
        gain = factor if gain is None else gain * factor
        back_w = jnp.concatenate(
            [turned[t * chans : (t + 1) * chans, mine] for t in reversed(range(TAPS))], axis=1
        )
        back_w_ref[n] = back_w
        backs.append(back_w)
    copies[-1].wait()
    guess = by_parity(adj_ref[0, 0])
    guess_ref[...] = guess
    back = guess
    for n in reversed(range(depth)):
        back = back + convolve(backs[n], (back * slopes[n]).astype(jnp.bfloat16))
    place = lax.axis_index("layer")
    first = jnp.where(place == 0, 0.0, start)
    last = jnp.where(place == lax.axis_size("layer") - 1, 0.0, guess)
    sent_ref[0] = gain
    sent_ref[1] = state - gain * first
    sent_ref[2] = back - gain * last


def patch_kernel(rounded_ref, patch_ref):
    depth, chans, _ = rounded_ref.shape
    perm = permutation(chans)
    for n in range(depth):
        for k, half in enumerate(taps_of(rounded_ref[n])):
            patch = dot(half, perm, ((0,), (0,))).astype(jnp.bfloat16)
            patch_ref[n, k * HALF : (k + 1) * HALF] = patch


def joined(bit, total, mine, got):
    gain, fwd, bwd = total
    pre_gain, pre, post_gain, post = mine
    got_gain, got_fwd, got_bwd = got
    total = (
        gain * got_gain,
        jnp.where(bit, gain * got_fwd + fwd, got_gain * fwd + got_fwd),
        jnp.where(bit, got_gain * bwd + got_bwd, gain * got_bwd + bwd),
    )
    mine = (
        jnp.where(bit, pre_gain * got_gain, pre_gain),
        jnp.where(bit, pre_gain * got_fwd + pre, pre),
        jnp.where(bit, post_gain, post_gain * got_gain),
        jnp.where(bit, post, post_gain * got_bwd + post),
    )
    return total, mine


def bit_of(axis, step):
    return lax.rem(lax.div(lax.axis_index(axis), 2**step), 2) == 1


def join_kernel(step, narrow, *refs):
    if step == 1:
        total_ref, got_ref, sent_ref, fwd_out, mine_out = refs
        one = jnp.ones(total_ref.shape[1:], jnp.float32)
        zero = jnp.zeros(total_ref.shape[1:], jnp.float32)
        mine = (one, zero, one, zero)
    else:
        total_ref, got_ref, mine_ref, sent_ref, fwd_out, mine_out = refs
        mine = tuple(mine_ref[k] for k in range(4))
    total = tuple(total_ref[k] for k in range(3))
    got = tuple(got_ref[k] for k in range(3))
    (gain, fwd, bwd), mine = joined(bit_of("layer", step - 1), total, mine, got)
    for k in range(4):
        mine_out[k] = mine[k]
    fwd_out[...] = fwd
    sent_ref[0] = gain
    if narrow:
        first = jnp.logical_not(jnp.logical_or(bit_of("layer", step), bit_of("layer", step + 1)))
        sent_ref[1] = jnp.where(first, fwd, bwd)
    else:
        sent_ref[1] = fwd
        sent_ref[2] = bwd


def quarters_kernel(steps, total_ref, fwd_ref, got_ref, mine_ref, sent_ref, late_ref, mine_out):
    odd, upper = bit_of("layer", steps - 2), bit_of("layer", steps - 1)
    gain, bwd, fwd = total_ref[0], total_ref[1], fwd_ref[...]
    got_gain, got = got_ref[0], got_ref[1]
    pre_gain, pre, post_gain, post = (mine_ref[k] for k in range(4))
    low_fwd = gain * got + fwd
    up_bwd = jnp.where(odd, got_gain * bwd + got, gain * got + bwd)
    sent_ref[...] = jnp.where(upper, up_bwd, low_fwd)
    late_ref[...] = jnp.where(upper, fwd, low_fwd)
    second = jnp.logical_and(odd, jnp.logical_not(upper))
    mine_out[0] = pre_gain
    mine_out[1] = jnp.where(second, pre_gain * got + pre, pre)
    mine_out[2] = jnp.where(odd, post_gain, post_gain * got_gain)
    mine_out[3] = jnp.where(odd, post, post_gain * got + post)
    mine_out[4] = got_gain


def later_fixed(steps, got_ref, mine_ref):
    got = jnp.where(bit_of("layer", steps - 1), 0.0, mine_ref[2] * got_ref[...])
    return mine_ref[3] + got


def fixed_kernel(steps, _, got_ref, late_ref, mine_ref, guess_ref, start_ref, adj_ref, state_ref):
    odd, upper = bit_of("layer", steps - 2), bit_of("layer", steps - 1)
    place = lax.axis_index("layer")
    adj = in_order(later_fixed(steps, got_ref, mine_ref))
    late = late_ref[...]
    came = jnp.where(odd, mine_ref[4] * got_ref[...] + late, late)
    state = in_order(mine_ref[1] + jnp.where(upper, mine_ref[0] * came, 0.0))
    adj_ref[0, 0] = jnp.where(place == lax.axis_size("layer") - 1, guess_ref[0, 0], adj)
    state_ref[0, 0] = jnp.where(place == 0, start_ref[0, 0], state)


def grad_kernel(
    steps,
    got_ref,
    mine_ref,
    guess_ref,
    slope_ref,
    patch_ref,
    back_w_ref,
    parts_ref,
):
    depth, chans, rows = back_w_ref.shape
    shares = parts_ref.shape[0]
    own = chans // shares
    last = lax.axis_index("layer") == lax.axis_size("layer") - 1
    adj = jnp.where(last, guess_ref[...], later_fixed(steps, got_ref, mine_ref))
    pad = parts_ref.shape[2] - rows

    def layer(n, adj):
        dz = adj * slope_ref[n]
        dzb = dz.astype(jnp.bfloat16)
        grad = dot(dzb, patch_ref[n], ((1,), (0,)))
        bias = jnp.broadcast_to(jnp.sum(dz, axis=1, keepdims=True), (chans, pad))
        both = jnp.concatenate([grad, bias], axis=1)
        where = pl.ds(pl.multiple_of(n * own, own), own)
        for k in range(shares):
            parts_ref[k, where] = both[k * own : (k + 1) * own]
        return dzb

    def behind(i, adj):
        n = depth - 1 - i
        return adj + convolve(back_w_ref[n], layer(n, adj))

    layer(0, lax.fori_loop(0, depth - 1, behind, adj))


def deal_kernel(_, parts_ref, keep_ref, send_ref):
    odd, high = bit_of("dp", 0), bit_of("dp", 1)
    parts = [parts_ref[i] for i in range(parts_ref.shape[0])]
    parts = [jnp.where(odd, parts[i ^ 1], parts[i]) for i in range(len(parts))]
    parts = [jnp.where(high, parts[i ^ 2], parts[i]) for i in range(len(parts))]
    keep_ref[0], keep_ref[1] = parts[0], parts[3]
    send_ref[0], send_ref[1] = parts[1], parts[2]


def halve_kernel(mine_ref, got_ref, keep_ref, send_ref):
    keep_ref[...] = mine_ref[0] + got_ref[0]
    send_ref[...] = mine_ref[1] + got_ref[1]


def total_kernel(mine_ref, got_ref, grad_ref, bias_ref):
    depth, own, width = grad_ref.shape
    total = mine_ref[...] + got_ref[...]
    eye = lax.broadcasted_iota(jnp.int32, (own, own), 0) == lax.broadcasted_iota(
        jnp.int32, (own, own), 1
    )
    for n in range(depth):
        mine = total[n * own : (n + 1) * own]
        grad_ref[n] = mine[:, :width]
        column = jnp.broadcast_to(mine[:, width : width + 1], (own, own))
        bias_ref[n : n + 1, :] = jnp.sum(jnp.where(eye, column, 0.0), axis=0, keepdims=True)


def call(kernel, out_shape, args, hbm_in=(), hbm_out=(), scratch=(), work=2**28):
    return pl.pallas_call(
        kernel,
        out_shape=out_shape,
        in_specs=[HBM if k in hbm_in else VMEM for k in range(len(args))],
        out_specs=[HBM if k in hbm_out else VMEM for k in range(len(out_shape))],
        scratch_shapes=list(scratch),
        compiler_params=pltpu.CompilerParams(vmem_limit_bytes=LIMIT),
        cost_estimate=pl.CostEstimate(flops=work, bytes_accessed=work // 256, transcendentals=0),
    )(*(pltpu.with_memory_space_constraint(a, pltpu.HBM) if k in hbm_in else a for k, a in enumerate(args)))


def f32(*shape):
    return jax.ShapeDtypeStruct(shape, jnp.float32)


def bf16(*shape):
    return jax.ShapeDtypeStruct(shape, jnp.bfloat16)


def exchange(x, axis, mask):
    return lax.ppermute(x, axis, [(i, i ^ mask) for i in range(lax.axis_size(axis))])


def local(state_guess, adjoint_guess, conv_weight, conv_bias):
    depth, chans, width = conv_weight.shape
    shares = lax.axis_size("dp")
    steps = lax.axis_size("layer").bit_length() - 1
    args = (state_guess, adjoint_guess, conv_weight, conv_bias)
    guess, total, slope, rounded, back_w = call(
        relax_kernel,
        (
            f32(chans, HW),
            f32(3, chans, HW),
            f32(depth, chans, HW),
            bf16(depth, chans, HW),
            bf16(depth, chans, width),
        ),
        args,
        hbm_in=range(4),
        scratch=[pltpu.VMEM(a.shape, a.dtype) for a in args] + [pltpu.SemaphoreType.DMA((4,))],
    )
    (patch,) = call(patch_kernel, (bf16(depth, HW, width),), (rounded,))
    mine = ()
    one = f32(chans, HW)
    for step in range(1, steps - 1):
        got = exchange(total, "layer", 1 << (step - 1))
        narrow = step == steps - 2
        total, fwd, *mine = call(
            functools.partial(join_kernel, step, narrow),
            (f32(2 if narrow else 3, chans, HW), one, f32(4, chans, HW)),
            (total, got, *mine),
        )
    got = exchange(total, "layer", 1 << (steps - 2))
    total, late, *mine = call(
        functools.partial(quarters_kernel, steps),
        (one, one, f32(5, chans, HW)),
        (total, fwd, got, *mine),
    )
    got = exchange(total, "layer", 1 << (steps - 1))
    quarter = 1 << (steps - 2)
    late = lax.ppermute(late, "layer", [(i, i + quarter) for i in range(quarter, 3 * quarter)])
    lanes = -(-(width + 1) // HALF) * HALF
    part = (depth * chans // shares, lanes)
    (parts,) = call(
        functools.partial(grad_kernel, steps),
        (f32(shares, *part),),
        (got, *mine, guess, slope, patch, back_w),
        work=0,
    )
    keep, send = call(
        deal_kernel,
        (f32(shares // 2, *part), f32(shares // 2, *part)),
        (late, parts),
        work=0,
    )
    adjoint_fixed, state_fixed = call(
        functools.partial(fixed_kernel, steps),
        (f32(*adjoint_guess.shape), f32(*state_guess.shape)),
        (keep, got, late, *mine, adjoint_guess, state_guess),
    )
    keep, send = call(halve_kernel, (f32(*part), f32(*part)), (keep, exchange(send, "dp", 1)))
    weight_grad, bias_grad = call(
        total_kernel,
        (f32(depth, chans // shares, width), f32(depth, chans // shares)),
        (keep, exchange(send, "dp", 3)),
    )
    return (state_fixed, adjoint_fixed, weight_grad, bias_grad)


def solution(mesh):
    placed = (
        P("layer", "dp", None, None),
        P("layer", "dp", None, None),
        P("layer", None, None),
        P("layer", None),
    )
    return jax.shard_map(
        local,
        mesh=mesh,
        in_specs=placed,
        out_specs=(
            P("layer", "dp", None, None),
            P("layer", "dp", None, None),
            P("layer", "dp", None),
            P("layer", "dp"),
        ),
        check_vma=False,
    )
```

```python
import functools

import jax
import jax.numpy as jnp
from jax import lax
from jax.experimental import pallas as pl
from jax.experimental.pallas import tpu as pltpu
from jax.sharding import PartitionSpec as P

IMG = 16
HW = IMG * IMG
HALF = 128
TAPS = 9
STEP = 0.5
LIMIT = 32 * 1024 * 1024

VMEM = pl.BlockSpec(memory_space=pltpu.VMEM)
HBM = pl.BlockSpec(memory_space=pltpu.HBM)


def picked(low, high, source, from_high):
    return jnp.where(
        from_high,
        jnp.take_along_axis(high, source, axis=1, mode="promise_in_bounds"),
        jnp.take_along_axis(low, source, axis=1, mode="promise_in_bounds"),
    )


def lanes_of(values):
    lane = lax.broadcasted_iota(jnp.int32, (values.shape[0], HALF), 1)
    return lane // IMG, lane % IMG


def by_parity(values):
    line, col = lanes_of(values)
    low, high = values[:, :HALF], values[:, HALF:]
    half = IMG // 4
    return jnp.concatenate(
        [
            picked(low, high, (2 * (line % half) + odd) * IMG + col, line >= half)
            for odd in range(2)
        ],
        axis=1,
    )


def in_order(values):
    line, col = lanes_of(values)
    even, odd = values[:, :HALF], values[:, HALF:]
    return jnp.concatenate(
        [
            picked(even, odd, (half * (IMG // 4) + line // 2) * IMG + col, line % 2 == 1)
            for half in range(2)
        ],
        axis=1,
    )


def taps_of(values):
    even, odd = values[:, :HALF], values[:, HALF:]
    lane = lax.broadcasted_iota(jnp.int16, even.shape, 1)
    col = lane & (IMG - 1)
    cols = {-1: [col >= 1], 0: [], 1: [col < IMG - 1]}

    def turned(half, lines, right):
        by = lines * IMG + right
        if not by:
            return half
        tests = cols[right] + {-1: [lane >= IMG], 0: [], 1: [lane < HALF - IMG]}[lines]
        part = pltpu.roll(half, -by % HALF, 1)
        return jnp.where(functools.reduce(jnp.logical_and, tests), part, jnp.zeros_like(part))

    above, here, below = [], [], []
    for right in (-1, 0, 1):
        same = turned(even, 0, right), turned(odd, 0, right)
        above.append((turned(odd, -1, right), same[0]))
        here.append(same)
        below.append((same[1], turned(even, 1, right)))
    return jnp.concatenate(
        [jnp.concatenate(pair, axis=1) for pair in above + here + below], axis=0
    )


def permutation(chans):
    size = TAPS * chans
    row = lax.broadcasted_iota(jnp.int32, (size, size), 0)
    column = lax.broadcasted_iota(jnp.int32, (size, size), 1)
    tap = lax.div(row, chans)
    return jnp.where(column == (row - tap * chans) * TAPS + tap, 1.0, 0.0).astype(jnp.bfloat16)


def dot(a, b, dims):
    return lax.dot_general(a, b, (dims, ((), ())), preferred_element_type=jnp.float32)


def convolve(weight, values):
    return dot(weight, taps_of(values), ((1,), (0,)))


def relax_kernel(
    state_hbm,
    adj_hbm,
    w_hbm,
    bias_hbm,
    guess_ref,
    sent_ref,
    slope_ref,
    rounded_ref,
    back_w_ref,
    state_ref,
    adj_ref,
    w_ref,
    bias_ref,
    sems,
):
    copies = [
        pltpu.make_async_copy(src, dst, sems.at[k])
        for k, (src, dst) in enumerate(
            ((w_hbm, w_ref), (state_hbm, state_ref), (bias_hbm, bias_ref), (adj_hbm, adj_ref))
        )
    ]
    for copy in copies:
        copy.start()
    depth, chans, width = w_ref.shape
    perm = permutation(chans)
    eye = lax.broadcasted_iota(jnp.int32, (chans, chans), 0) == lax.broadcasted_iota(
        jnp.int32, (chans, chans), 1
    )
    for copy in copies:
        copy.wait()
    weights = w_ref[...].reshape(depth * chans, width)
    by_tap = dot(weights, perm, ((1,), (1,)))
    turned = dot(perm, weights, ((1,), (1,))).astype(jnp.bfloat16)
    middle = TAPS // 2 * chans
    start = by_parity(state_ref[0, 0])
    guess = by_parity(adj_ref[0, 0])
    guess_ref[...] = guess
    state = start
    gain = None
    slopes = []
    backs = []
    for n in range(depth):
        mine = slice(n * chans, (n + 1) * chans)
        bias = jnp.broadcast_to(bias_ref[n : n + 1, :], (chans, chans))
        bias, kc = (
            jnp.sum(jnp.where(eye, square, 0.0), axis=1, keepdims=True)
            for square in (bias, by_tap[mine, middle : middle + chans])
        )
        rounded = state.astype(jnp.bfloat16)
        rounded_ref[n] = rounded
        squash = jnp.tanh(convolve(by_tap[mine].astype(jnp.bfloat16), rounded) + bias)
        slope = STEP * (1.0 - squash * squash)
        slope_ref[n] = slope
        slopes.append(slope)
        state = state + STEP * squash
        factor = 1.0 + slope * kc
        gain = factor if gain is None else gain * factor
        back_w = jnp.concatenate(
            [turned[t * chans : (t + 1) * chans, mine] for t in reversed(range(TAPS))], axis=1
        )
        back_w_ref[n] = back_w
        backs.append(back_w)
    back = guess
    for n in reversed(range(depth)):
        back = back + convolve(backs[n], (back * slopes[n]).astype(jnp.bfloat16))
    place = lax.axis_index("layer")
    first = jnp.where(place == 0, 0.0, start)
    last = jnp.where(place == lax.axis_size("layer") - 1, 0.0, guess)
    sent_ref[0] = gain
    sent_ref[1] = state - gain * first
    sent_ref[2] = back - gain * last


def patch_kernel(rounded_ref, patch_ref):
    depth, chans, _ = rounded_ref.shape
    perm = permutation(chans)
    for n in range(depth):
        patch = taps_of(rounded_ref[n])
        patch_ref[n] = dot(perm, patch, ((0,), (0,))).astype(jnp.bfloat16)


def joined(bit, total, mine, got):
    gain, fwd, bwd = total
    pre_gain, pre, post_gain, post = mine
    got_gain, got_fwd, got_bwd = got
    total = (
        gain * got_gain,
        jnp.where(bit, gain * got_fwd + fwd, got_gain * fwd + got_fwd),
        jnp.where(bit, got_gain * bwd + got_bwd, gain * got_bwd + bwd),
    )
    mine = (
        jnp.where(bit, pre_gain * got_gain, pre_gain),
        jnp.where(bit, pre_gain * got_fwd + pre, pre),
        jnp.where(bit, post_gain, post_gain * got_gain),
        jnp.where(bit, post, post_gain * got_bwd + post),
    )
    return total, mine


def bit_of(axis, step):
    return lax.rem(lax.div(lax.axis_index(axis), 2**step), 2) == 1


def join_kernel(step, narrow, *refs):
    if step == 1:
        total_ref, got_ref, sent_ref, fwd_out, mine_out = refs
        one = jnp.ones(total_ref.shape[1:], jnp.float32)
        zero = jnp.zeros(total_ref.shape[1:], jnp.float32)
        mine = (one, zero, one, zero)
    else:
        total_ref, got_ref, mine_ref, sent_ref, fwd_out, mine_out = refs
        mine = tuple(mine_ref[k] for k in range(4))
    total = tuple(total_ref[k] for k in range(3))
    got = tuple(got_ref[k] for k in range(3))
    (gain, fwd, bwd), mine = joined(bit_of("layer", step - 1), total, mine, got)
    for k in range(4):
        mine_out[k] = mine[k]
    fwd_out[...] = fwd
    sent_ref[0] = gain
    if narrow:
        first = jnp.logical_not(jnp.logical_or(bit_of("layer", step), bit_of("layer", step + 1)))
        sent_ref[1] = jnp.where(first, fwd, bwd)
    else:
        sent_ref[1] = fwd
        sent_ref[2] = bwd


def quarters_kernel(steps, total_ref, fwd_ref, got_ref, mine_ref, sent_ref, late_ref, mine_out):
    odd, upper = bit_of("layer", steps - 2), bit_of("layer", steps - 1)
    gain, bwd, fwd = total_ref[0], total_ref[1], fwd_ref[...]
    got_gain, got = got_ref[0], got_ref[1]
    pre_gain, pre, post_gain, post = (mine_ref[k] for k in range(4))
    low_fwd = gain * got + fwd
    up_bwd = jnp.where(odd, got_gain * bwd + got, gain * got + bwd)
    sent_ref[...] = jnp.where(upper, up_bwd, low_fwd)
    late_ref[...] = jnp.where(upper, fwd, low_fwd)
    second = jnp.logical_and(odd, jnp.logical_not(upper))
    mine_out[0] = pre_gain
    mine_out[1] = jnp.where(second, pre_gain * got + pre, pre)
    mine_out[2] = jnp.where(odd, post_gain, post_gain * got_gain)
    mine_out[3] = jnp.where(odd, post, post_gain * got + post)
    mine_out[4] = got_gain


def later_fixed(steps, got_ref, mine_ref):
    got = jnp.where(bit_of("layer", steps - 1), 0.0, mine_ref[2] * got_ref[...])
    return mine_ref[3] + got


def fixed_kernel(steps, _, got_ref, late_ref, mine_ref, guess_ref, start_ref, adj_ref, state_ref):
    odd, upper = bit_of("layer", steps - 2), bit_of("layer", steps - 1)
    place = lax.axis_index("layer")
    adj = in_order(later_fixed(steps, got_ref, mine_ref))
    late = late_ref[...]
    came = jnp.where(odd, mine_ref[4] * got_ref[...] + late, late)
    state = in_order(mine_ref[1] + jnp.where(upper, mine_ref[0] * came, 0.0))
    adj_ref[0, 0] = jnp.where(place == lax.axis_size("layer") - 1, guess_ref[0, 0], adj)
    state_ref[0, 0] = jnp.where(place == 0, start_ref[0, 0], state)


def grad_kernel(
    steps,
    got_ref,
    mine_ref,
    guess_ref,
    slope_ref,
    patch_ref,
    back_w_ref,
    parts_ref,
):
    depth, chans, rows = back_w_ref.shape
    shares = parts_ref.shape[0]
    own = chans // shares
    last = lax.axis_index("layer") == lax.axis_size("layer") - 1
    adj = jnp.where(last, guess_ref[...], later_fixed(steps, got_ref, mine_ref))
    pad = parts_ref.shape[2] - rows

    def layer(n, adj):
        dz = adj * slope_ref[n]
        dzb = dz.astype(jnp.bfloat16)
        grad = dot(dzb, patch_ref[n], ((1,), (1,)))
        bias = jnp.broadcast_to(jnp.sum(dz, axis=1, keepdims=True), (chans, pad))
        both = jnp.concatenate([grad, bias], axis=1)
        where = pl.ds(pl.multiple_of(n * own, own), own)
        for k in range(shares):
            parts_ref[k, where] = both[k * own : (k + 1) * own]
        return dzb

    def behind(i, adj):
        n = depth - 1 - i
        return adj + convolve(back_w_ref[n], layer(n, adj))

    layer(0, lax.fori_loop(0, depth - 1, behind, adj))


def deal_kernel(_, parts_ref, *outs):
    odd, high = bit_of("dp", 0), bit_of("dp", 1)
    parts = [parts_ref[i] for i in range(parts_ref.shape[0])]
    parts = [jnp.where(odd, parts[i ^ 1], parts[i]) for i in range(len(parts))]
    parts = [jnp.where(high, parts[i ^ 2], parts[i]) for i in range(len(parts))]
    for part, out in zip(parts, outs):
        out[...] = part


def total_kernel(mine_ref, both_ref, chip_ref, core_ref, grad_ref, bias_ref):
    depth, own, width = grad_ref.shape
    total = (mine_ref[...] + core_ref[...]) + (chip_ref[...] + both_ref[...])
    eye = lax.broadcasted_iota(jnp.int32, (own, own), 0) == lax.broadcasted_iota(
        jnp.int32, (own, own), 1
    )
    for n in range(depth):
        mine = total[n * own : (n + 1) * own]
        grad_ref[n] = mine[:, :width]
        column = jnp.broadcast_to(mine[:, width : width + 1], (own, own))
        bias_ref[n : n + 1, :] = jnp.sum(jnp.where(eye, column, 0.0), axis=0, keepdims=True)


def call(kernel, out_shape, args, hbm_in=(), hbm_out=(), scratch=(), work=2**28):
    return pl.pallas_call(
        kernel,
        out_shape=out_shape,
        in_specs=[HBM if k in hbm_in else VMEM for k in range(len(args))],
        out_specs=[HBM if k in hbm_out else VMEM for k in range(len(out_shape))],
        scratch_shapes=list(scratch),
        compiler_params=pltpu.CompilerParams(vmem_limit_bytes=LIMIT),
        cost_estimate=pl.CostEstimate(flops=work, bytes_accessed=work // 256, transcendentals=0),
    )(*(pltpu.with_memory_space_constraint(a, pltpu.HBM) if k in hbm_in else a for k, a in enumerate(args)))


def f32(*shape):
    return jax.ShapeDtypeStruct(shape, jnp.float32)


def bf16(*shape):
    return jax.ShapeDtypeStruct(shape, jnp.bfloat16)


def exchange(x, axis, mask):
    return lax.ppermute(x, axis, [(i, i ^ mask) for i in range(lax.axis_size(axis))])


def local(state_guess, adjoint_guess, conv_weight, conv_bias):
    depth, chans, width = conv_weight.shape
    shares = lax.axis_size("dp")
    steps = lax.axis_size("layer").bit_length() - 1
    args = (state_guess, adjoint_guess, conv_weight, conv_bias)
    guess, total, slope, rounded, back_w = call(
        relax_kernel,
        (
            f32(chans, HW),
            f32(3, chans, HW),
            f32(depth, chans, HW),
            bf16(depth, chans, HW),
            bf16(depth, chans, width),
        ),
        args,
        hbm_in=range(4),
        scratch=[pltpu.VMEM(a.shape, a.dtype) for a in args] + [pltpu.SemaphoreType.DMA((4,))],
    )
    (patch,) = call(patch_kernel, (bf16(depth, width, HW),), (rounded,))
    mine = ()
    one = f32(chans, HW)
    for step in range(1, steps - 1):
        got = exchange(total, "layer", 1 << (step - 1))
        narrow = step == steps - 2
        total, fwd, *mine = call(
            functools.partial(join_kernel, step, narrow),
            (f32(2 if narrow else 3, chans, HW), one, f32(4, chans, HW)),
            (total, got, *mine),
        )
    got = exchange(total, "layer", 1 << (steps - 2))
    total, late, *mine = call(
        functools.partial(quarters_kernel, steps),
        (one, one, f32(5, chans, HW)),
        (total, fwd, got, *mine),
    )
    got = exchange(total, "layer", 1 << (steps - 1))
    quarter = 1 << (steps - 2)
    late = lax.ppermute(late, "layer", [(i, i + quarter) for i in range(quarter, 3 * quarter)])
    lanes = -(-(width + 1) // HALF) * HALF
    part = (depth * chans // shares, lanes)
    (parts,) = call(
        functools.partial(grad_kernel, steps),
        (f32(shares, *part),),
        (got, *mine, guess, slope, patch, back_w),
        work=0,
    )
    keep, *sends = call(deal_kernel, (f32(*part),) * shares, (late, parts), work=0)
    adjoint_fixed, state_fixed = call(
        functools.partial(fixed_kernel, steps),
        (f32(*adjoint_guess.shape), f32(*state_guess.shape)),
        (keep, got, late, *mine, adjoint_guess, state_guess),
    )
    both = exchange(sends[2], "dp", 3)
    chip = exchange(sends[1], "dp", 2)
    core = exchange(sends[0], "dp", 1)
    weight_grad, bias_grad = call(
        total_kernel,
        (f32(depth, chans // shares, width), f32(depth, chans // shares)),
        (keep, both, chip, core),
    )
    return (state_fixed, adjoint_fixed, weight_grad, bias_grad)


def solution(mesh):
    placed = (
        P("layer", "dp", None, None),
        P("layer", "dp", None, None),
        P("layer", None, None),
        P("layer", None),
    )
    return jax.shard_map(
        local,
        mesh=mesh,
        in_specs=placed,
        out_specs=(
            P("layer", "dp", None, None),
            P("layer", "dp", None, None),
            P("layer", "dp", None),
            P("layer", "dp"),
        ),
        check_vma=False,
    )
```

```python
import functools

import jax
import jax.numpy as jnp
from jax import lax
from jax.experimental import pallas as pl
from jax.experimental.pallas import tpu as pltpu
from jax.sharding import PartitionSpec as P

IMG = 16
HW = IMG * IMG
HALF = 128
TAPS = 9
STEP = 0.5
LIMIT = 32 * 1024 * 1024

VMEM = pl.BlockSpec(memory_space=pltpu.VMEM)
HBM = pl.BlockSpec(memory_space=pltpu.HBM)


def picked(low, high, source, from_high):
    return jnp.where(
        from_high,
        jnp.take_along_axis(high, source, axis=1, mode="promise_in_bounds"),
        jnp.take_along_axis(low, source, axis=1, mode="promise_in_bounds"),
    )


def lanes_of(values):
    lane = lax.broadcasted_iota(jnp.int32, (values.shape[0], HALF), 1)
    return lane // IMG, lane % IMG


def by_parity(values):
    line, col = lanes_of(values)
    low, high = values[:, :HALF], values[:, HALF:]
    half = IMG // 4
    return jnp.concatenate(
        [
            picked(low, high, (2 * (line % half) + odd) * IMG + col, line >= half)
            for odd in range(2)
        ],
        axis=1,
    )


def in_order(values):
    line, col = lanes_of(values)
    even, odd = values[:, :HALF], values[:, HALF:]
    return jnp.concatenate(
        [
            picked(even, odd, (half * (IMG // 4) + line // 2) * IMG + col, line % 2 == 1)
            for half in range(2)
        ],
        axis=1,
    )


def taps_of(values):
    even, odd = values[:, :HALF], values[:, HALF:]
    lane = lax.broadcasted_iota(jnp.int16, even.shape, 1)
    col = lane & (IMG - 1)
    cols = {-1: [col >= 1], 0: [], 1: [col < IMG - 1]}

    def turned(half, lines, right):
        by = lines * IMG + right
        if not by:
            return half
        tests = cols[right] + {-1: [lane >= IMG], 0: [], 1: [lane < HALF - IMG]}[lines]
        part = pltpu.roll(half, -by % HALF, 1)
        return jnp.where(functools.reduce(jnp.logical_and, tests), part, jnp.zeros_like(part))

    above, here, below = [], [], []
    for right in (-1, 0, 1):
        same = turned(even, 0, right), turned(odd, 0, right)
        above.append((turned(odd, -1, right), same[0]))
        here.append(same)
        below.append((same[1], turned(even, 1, right)))
    return jnp.concatenate(
        [jnp.concatenate(pair, axis=1) for pair in above + here + below], axis=0
    )


def permutation(chans):
    size = TAPS * chans
    row = lax.broadcasted_iota(jnp.int32, (size, size), 0)
    column = lax.broadcasted_iota(jnp.int32, (size, size), 1)
    tap = lax.div(row, chans)
    return jnp.where(column == (row - tap * chans) * TAPS + tap, 1.0, 0.0).astype(jnp.bfloat16)


def dot(a, b, dims):
    return lax.dot_general(a, b, (dims, ((), ())), preferred_element_type=jnp.float32)


def convolve(weight, values):
    return dot(weight, taps_of(values), ((1,), (0,)))


def relax_kernel(
    state_hbm,
    adj_hbm,
    w_hbm,
    bias_hbm,
    guess_ref,
    sent_ref,
    slope_ref,
    rounded_ref,
    back_w_ref,
    state_ref,
    adj_ref,
    w_ref,
    bias_ref,
    sems,
):
    copies = [
        pltpu.make_async_copy(src, dst, sems.at[k])
        for k, (src, dst) in enumerate(
            ((w_hbm, w_ref), (state_hbm, state_ref), (bias_hbm, bias_ref), (adj_hbm, adj_ref))
        )
    ]
    for copy in copies:
        copy.start()
    depth, chans, width = w_ref.shape
    perm = permutation(chans)
    eye = lax.broadcasted_iota(jnp.int32, (chans, chans), 0) == lax.broadcasted_iota(
        jnp.int32, (chans, chans), 1
    )
    for copy in copies:
        copy.wait()
    weights = w_ref[...].reshape(depth * chans, width)
    by_tap = dot(weights, perm, ((1,), (1,)))
    turned = dot(perm, weights, ((1,), (1,))).astype(jnp.bfloat16)
    middle = TAPS // 2 * chans
    start = by_parity(state_ref[0, 0])
    guess = by_parity(adj_ref[0, 0])
    guess_ref[...] = guess
    state = start
    gain = None
    slopes = []
    backs = []
    for n in range(depth):
        mine = slice(n * chans, (n + 1) * chans)
        bias = jnp.broadcast_to(bias_ref[n : n + 1, :], (chans, chans))
        bias, kc = (
            jnp.sum(jnp.where(eye, square, 0.0), axis=1, keepdims=True)
            for square in (bias, by_tap[mine, middle : middle + chans])
        )
        rounded = state.astype(jnp.bfloat16)
        rounded_ref[n] = rounded
        squash = jnp.tanh(convolve(by_tap[mine].astype(jnp.bfloat16), rounded) + bias)
        slope = STEP * (1.0 - squash * squash)
        slope_ref[n] = slope
        slopes.append(slope)
        state = state + STEP * squash
        factor = 1.0 + slope * kc
        gain = factor if gain is None else gain * factor
        back_w = jnp.concatenate(
            [turned[t * chans : (t + 1) * chans, mine] for t in reversed(range(TAPS))], axis=1
        )
        back_w_ref[n] = back_w
        backs.append(back_w)
    back = guess
    for n in reversed(range(depth)):
        back = back + convolve(backs[n], (back * slopes[n]).astype(jnp.bfloat16))
    place = lax.axis_index("layer")
    first = jnp.where(place == 0, 0.0, start)
    last = jnp.where(place == lax.axis_size("layer") - 1, 0.0, guess)
    sent_ref[0] = gain
    sent_ref[1] = state - gain * first
    sent_ref[2] = back - gain * last


def patch_kernel(rounded_ref, patch_ref):
    depth, chans, _ = rounded_ref.shape
    perm = permutation(chans)
    for n in range(depth):
        patch = taps_of(rounded_ref[n])
        patch_ref[n] = dot(perm, patch, ((0,), (0,))).astype(jnp.bfloat16)


def joined(bit, total, mine, got):
    gain, fwd, bwd = total
    pre_gain, pre, post_gain, post = mine
    got_gain, got_fwd, got_bwd = got
    total = (
        gain * got_gain,
        jnp.where(bit, gain * got_fwd + fwd, got_gain * fwd + got_fwd),
        jnp.where(bit, got_gain * bwd + got_bwd, gain * got_bwd + bwd),
    )
    mine = (
        jnp.where(bit, pre_gain * got_gain, pre_gain),
        jnp.where(bit, pre_gain * got_fwd + pre, pre),
        jnp.where(bit, post_gain, post_gain * got_gain),
        jnp.where(bit, post, post_gain * got_bwd + post),
    )
    return total, mine


def bit_of(axis, step):
    return lax.rem(lax.div(lax.axis_index(axis), 2**step), 2) == 1


def put_joined(step, final, total, mine, sent_ref, mine_out):
    for k in range(4):
        mine_out[k] = mine[k]
    if final:
        sent_ref[...] = jnp.where(bit_of("layer", step), total[2], total[1])
    else:
        for k in range(3):
            sent_ref[k] = total[k]


def four_kernel(final, own_ref, first_ref, second_ref, third_ref, sent_ref, mine_out):
    low, high = bit_of("layer", 0), bit_of("layer", 1)
    place = lax.rem(lax.axis_index("layer"), 4)
    maps = [
        tuple(ref[k] for k in range(3)) for ref in (own_ref, first_ref, second_ref, third_ref)
    ]
    for bit, mask in ((low, 1), (high, 2)):
        maps = [
            tuple(jnp.where(bit, b, a) for a, b in zip(maps[k], maps[k ^ mask])) for k in range(4)
        ]
    one, zero = jnp.ones_like(maps[0][0]), jnp.zeros_like(maps[0][0])
    gain, fwd, bwd = maps[0]
    pre_gain, pre, post_gain, post = one, zero, one, zero
    for k in range(4):
        here = maps[k]
        before = k < place
        pre = jnp.where(before, here[0] * pre + here[1], pre)
        pre_gain = jnp.where(before, pre_gain * here[0], pre_gain)
        if k:
            bwd = bwd + gain * here[2]
            fwd = here[0] * fwd + here[1]
            gain = gain * here[0]
    for k in reversed(range(4)):
        here = maps[k]
        after = k > place
        post = jnp.where(after, here[0] * post + here[2], post)
        post_gain = jnp.where(after, post_gain * here[0], post_gain)
    mine = (pre_gain, pre, post_gain, post)
    put_joined(2, final, (gain, fwd, bwd), mine, sent_ref, mine_out)


def join_kernel(step, final, total_ref, got_ref, mine_ref, sent_ref, mine_out):
    total, got = (tuple(ref[k] for k in range(3)) for ref in (total_ref, got_ref))
    mine = tuple(mine_ref[k] for k in range(4))
    total, mine = joined(bit_of("layer", step - 1), total, mine, got)
    put_joined(step, final, total, mine, sent_ref, mine_out)


def later_fixed(steps, got_ref, mine_ref):
    got = jnp.where(bit_of("layer", steps - 1), 0.0, mine_ref[2] * got_ref[...])
    return mine_ref[3] + got


def fixed_kernel(steps, _, got_ref, mine_ref, guess_ref, start_ref, adj_ref, state_ref):
    place = lax.axis_index("layer")
    adj = in_order(later_fixed(steps, got_ref, mine_ref))
    got = jnp.where(bit_of("layer", steps - 1), mine_ref[0] * got_ref[...], 0.0)
    state = in_order(mine_ref[1] + got)
    adj_ref[0, 0] = jnp.where(place == lax.axis_size("layer") - 1, guess_ref[0, 0], adj)
    state_ref[0, 0] = jnp.where(place == 0, start_ref[0, 0], state)


def grad_kernel(
    steps,
    got_ref,
    mine_ref,
    guess_ref,
    slope_ref,
    patch_ref,
    back_w_ref,
    *part_refs,
):
    depth, chans, rows = back_w_ref.shape
    shares = len(part_refs)
    own = chans // shares
    last = lax.axis_index("layer") == lax.axis_size("layer") - 1
    adj = jnp.where(last, guess_ref[...], later_fixed(steps, got_ref, mine_ref))
    pad = part_refs[0].shape[1] - rows
    odd, high = bit_of("dp", 0), bit_of("dp", 1)

    def layer(n, adj):
        dz = adj * slope_ref[n]
        dzb = dz.astype(jnp.bfloat16)
        grad = dot(dzb, patch_ref[n], ((1,), (1,)))
        bias = jnp.broadcast_to(jnp.sum(dz, axis=1, keepdims=True), (chans, pad))
        both = jnp.concatenate([grad, bias], axis=1)
        where = pl.ds(pl.multiple_of(n * own, own), own)
        parts = [both[k * own : (k + 1) * own] for k in range(shares)]
        parts = [jnp.where(odd, parts[i ^ 1], parts[i]) for i in range(shares)]
        parts = [jnp.where(high, parts[i ^ 2], parts[i]) for i in range(shares)]
        for part, ref in zip(parts, part_refs):
            ref[where] = part
        return dzb

    def behind(i, adj):
        n = depth - 1 - i
        return adj + convolve(back_w_ref[n], layer(n, adj))

    layer(0, lax.fori_loop(0, depth - 1, behind, adj))


def total_kernel(mine_ref, both_ref, chip_ref, core_ref, grad_ref, bias_ref):
    depth, own, width = grad_ref.shape
    total = (mine_ref[...] + core_ref[...]) + (chip_ref[...] + both_ref[...])
    eye = lax.broadcasted_iota(jnp.int32, (own, own), 0) == lax.broadcasted_iota(
        jnp.int32, (own, own), 1
    )
    for n in range(depth):
        mine = total[n * own : (n + 1) * own]
        grad_ref[n] = mine[:, :width]
        column = jnp.broadcast_to(mine[:, width : width + 1], (own, own))
        bias_ref[n : n + 1, :] = jnp.sum(jnp.where(eye, column, 0.0), axis=0, keepdims=True)


def call(kernel, out_shape, args, hbm_in=(), hbm_out=(), scratch=()):
    return pl.pallas_call(
        kernel,
        out_shape=out_shape,
        in_specs=[HBM if k in hbm_in else VMEM for k in range(len(args))],
        out_specs=[HBM if k in hbm_out else VMEM for k in range(len(out_shape))],
        scratch_shapes=list(scratch),
        compiler_params=pltpu.CompilerParams(vmem_limit_bytes=LIMIT),
        cost_estimate=pl.CostEstimate(flops=2**28, bytes_accessed=2**20, transcendentals=0),
    )(*(pltpu.with_memory_space_constraint(a, pltpu.HBM) if k in hbm_in else a for k, a in enumerate(args)))


def f32(*shape):
    return jax.ShapeDtypeStruct(shape, jnp.float32)


def bf16(*shape):
    return jax.ShapeDtypeStruct(shape, jnp.bfloat16)


def exchange(x, axis, mask):
    return lax.ppermute(x, axis, [(i, i ^ mask) for i in range(lax.axis_size(axis))])


def local(state_guess, adjoint_guess, conv_weight, conv_bias):
    depth, chans, width = conv_weight.shape
    shares = lax.axis_size("dp")
    steps = lax.axis_size("layer").bit_length() - 1
    args = (state_guess, adjoint_guess, conv_weight, conv_bias)
    guess, total, slope, rounded, back_w = call(
        relax_kernel,
        (
            f32(chans, HW),
            f32(3, chans, HW),
            f32(depth, chans, HW),
            bf16(depth, chans, HW),
            bf16(depth, chans, width),
        ),
        args,
        hbm_in=range(4),
        scratch=[pltpu.VMEM(a.shape, a.dtype) for a in args] + [pltpu.SemaphoreType.DMA((4,))],
    )
    (patch,) = call(patch_kernel, (bf16(depth, width, HW),), (rounded,))
    one = f32(chans, HW)
    shapes = [(f32(3, chans, HW), f32(4, chans, HW))] * (steps - 3) + [(one, f32(4, chans, HW))]
    total, mine = call(
        functools.partial(four_kernel, steps == 3),
        shapes[0],
        (total, *(exchange(total, "layer", mask) for mask in (1, 2, 3))),
    )
    for step in range(3, steps):
        total, mine = call(
            functools.partial(join_kernel, step, step == steps - 1),
            shapes[step - 2],
            (total, exchange(total, "layer", 1 << (step - 1)), mine),
        )
    got = exchange(total, "layer", 1 << (steps - 1))
    lanes = -(-(width + 1) // HALF) * HALF
    part = (depth * chans // shares, lanes)
    keep, *sends = call(
        functools.partial(grad_kernel, steps),
        (f32(*part),) * shares,
        (got, mine, guess, slope, patch, back_w),
    )
    adjoint_fixed, state_fixed = call(
        functools.partial(fixed_kernel, steps),
        (f32(*adjoint_guess.shape), f32(*state_guess.shape)),
        (keep, got, mine, adjoint_guess, state_guess),
    )
    both = exchange(sends[2], "dp", 3)
    chip = exchange(sends[1], "dp", 2)
    core = exchange(sends[0], "dp", 1)
    weight_grad, bias_grad = call(
        total_kernel,
        (f32(depth, chans // shares, width), f32(depth, chans // shares)),
        (keep, both, chip, core),
    )
    return (state_fixed, adjoint_fixed, weight_grad, bias_grad)


def solution(mesh):
    placed = (
        P("layer", "dp", None, None),
        P("layer", "dp", None, None),
        P("layer", None, None),
        P("layer", None),
    )
    return jax.shard_map(
        local,
        mesh=mesh,
        in_specs=placed,
        out_specs=(
            P("layer", "dp", None, None),
            P("layer", "dp", None, None),
            P("layer", "dp", None),
            P("layer", "dp"),
        ),
        check_vma=False,
    )
```

```python
import functools

import jax
import jax.numpy as jnp
from jax import lax
from jax.experimental import pallas as pl
from jax.experimental.pallas import tpu as pltpu
from jax.sharding import PartitionSpec as P

IMG = 16
HW = IMG * IMG
HALF = 128
TAPS = 9
STEP = 0.5
LIMIT = 32 * 1024 * 1024
GRAD_WORK = 2**28
FIXED_WORK = 2**32

VMEM = pl.BlockSpec(memory_space=pltpu.VMEM)
HBM = pl.BlockSpec(memory_space=pltpu.HBM)


def picked(low, high, source, from_high):
    return jnp.where(
        from_high,
        jnp.take_along_axis(high, source, axis=1, mode="promise_in_bounds"),
        jnp.take_along_axis(low, source, axis=1, mode="promise_in_bounds"),
    )


def lanes_of(values):
    lane = lax.broadcasted_iota(jnp.int32, (values.shape[0], HALF), 1)
    return lane // IMG, lane % IMG


def by_parity(values):
    line, col = lanes_of(values)
    low, high = values[:, :HALF], values[:, HALF:]
    half = IMG // 4
    return jnp.concatenate(
        [
            picked(low, high, (2 * (line % half) + odd) * IMG + col, line >= half)
            for odd in range(2)
        ],
        axis=1,
    )


def in_order(values):
    line, col = lanes_of(values)
    even, odd = values[:, :HALF], values[:, HALF:]
    return jnp.concatenate(
        [
            picked(even, odd, (half * (IMG // 4) + line // 2) * IMG + col, line % 2 == 1)
            for half in range(2)
        ],
        axis=1,
    )


def taps_of(values):
    even, odd = values[:, :HALF], values[:, HALF:]
    lane = lax.broadcasted_iota(jnp.int16, even.shape, 1)
    col = lane & (IMG - 1)
    cols = {-1: [col >= 1], 0: [], 1: [col < IMG - 1]}

    def turned(half, lines, right):
        by = lines * IMG + right
        if not by:
            return half
        tests = cols[right] + {-1: [lane >= IMG], 0: [], 1: [lane < HALF - IMG]}[lines]
        part = pltpu.roll(half, -by % HALF, 1)
        return jnp.where(functools.reduce(jnp.logical_and, tests), part, jnp.zeros_like(part))

    above, here, below = [], [], []
    for right in (-1, 0, 1):
        same = turned(even, 0, right), turned(odd, 0, right)
        above.append((turned(odd, -1, right), same[0]))
        here.append(same)
        below.append((same[1], turned(even, 1, right)))
    return jnp.concatenate(
        [jnp.concatenate(pair, axis=1) for pair in above + here + below], axis=0
    )


def permutation(chans):
    size = TAPS * chans
    row = lax.broadcasted_iota(jnp.int32, (size, size), 0)
    column = lax.broadcasted_iota(jnp.int32, (size, size), 1)
    tap = lax.div(row, chans)
    return jnp.where(column == (row - tap * chans) * TAPS + tap, 1.0, 0.0).astype(jnp.bfloat16)


def dot(a, b, dims):
    return lax.dot_general(a, b, (dims, ((), ())), preferred_element_type=jnp.float32)


def convolve(weight, values):
    return dot(weight, taps_of(values), ((1,), (0,)))


def relax_kernel(
    state_hbm,
    adj_hbm,
    w_hbm,
    bias_hbm,
    guess_ref,
    sent_ref,
    ahead_ref,
    slope_ref,
    rounded_ref,
    back_w_ref,
    state_ref,
    adj_ref,
    w_ref,
    bias_ref,
    sems,
):
    copies = [
        pltpu.make_async_copy(src, dst, sems.at[k])
        for k, (src, dst) in enumerate(
            ((w_hbm, w_ref), (state_hbm, state_ref), (bias_hbm, bias_ref), (adj_hbm, adj_ref))
        )
    ]
    for copy in copies:
        copy.start()
    depth, chans, width = w_ref.shape
    perm = permutation(chans)
    eye = lax.broadcasted_iota(jnp.int32, (chans, chans), 0) == lax.broadcasted_iota(
        jnp.int32, (chans, chans), 1
    )
    for copy in copies:
        copy.wait()
    weights = w_ref[...].reshape(depth * chans, width)
    by_tap = dot(weights, perm, ((1,), (1,)))
    turned = dot(perm, weights, ((1,), (1,))).astype(jnp.bfloat16)
    middle = TAPS // 2 * chans
    start = by_parity(state_ref[0, 0])
    guess = by_parity(adj_ref[0, 0])
    guess_ref[...] = guess
    state = start
    gain = None
    slopes = []
    backs = []
    for n in range(depth):
        mine = slice(n * chans, (n + 1) * chans)
        bias = jnp.broadcast_to(bias_ref[n : n + 1, :], (chans, chans))
        bias, kc = (
            jnp.sum(jnp.where(eye, square, 0.0), axis=1, keepdims=True)
            for square in (bias, by_tap[mine, middle : middle + chans])
        )
        rounded = state.astype(jnp.bfloat16)
        rounded_ref[n] = rounded
        squash = jnp.tanh(convolve(by_tap[mine].astype(jnp.bfloat16), rounded) + bias)
        slope = STEP * (1.0 - squash * squash)
        slope_ref[n] = slope
        slopes.append(slope)
        state = state + STEP * squash
        factor = 1.0 + slope * kc
        gain = factor if gain is None else gain * factor
        back_w = jnp.concatenate(
            [turned[t * chans : (t + 1) * chans, mine] for t in reversed(range(TAPS))], axis=1
        )
        back_w_ref[n] = back_w
        backs.append(back_w)
    back = guess
    for n in reversed(range(depth)):
        back = back + convolve(backs[n], (back * slopes[n]).astype(jnp.bfloat16))
    place = lax.axis_index("layer")
    first = jnp.where(place == 0, 0.0, start)
    last = jnp.where(place == lax.axis_size("layer") - 1, 0.0, guess)
    sent_ref[0] = gain
    sent_ref[1] = back - gain * last
    ahead_ref[...] = state - gain * first


def patch_kernel(rounded_ref, patch_ref):
    depth, chans, _ = rounded_ref.shape
    perm = permutation(chans)
    for n in range(depth):
        patch = taps_of(rounded_ref[n])
        patch_ref[n] = dot(perm, patch, ((0,), (0,))).astype(jnp.bfloat16)


def bit_of(axis, step):
    return lax.rem(lax.div(lax.axis_index(axis), 2**step), 2) == 1


def in_places(own, first, second, third):
    values = [own, first, second, third]
    for step, mask in ((0, 1), (1, 2)):
        bit = bit_of("layer", step)
        values = [
            tuple(jnp.where(bit, b, a) for a, b in zip(values[k], values[k ^ mask]))
            for k in range(4)
        ]
    return values


def later_four_kernel(own_ref, first_ref, second_ref, third_ref, sent_ref, mine_out):
    place = lax.rem(lax.axis_index("layer"), 4)
    maps = in_places(*((r[0], r[1]) for r in (own_ref, first_ref, second_ref, third_ref)))
    gain, bwd = maps[0]
    for here in maps[1:]:
        bwd = bwd + gain * here[1]
        gain = gain * here[0]
    post_gain, post = jnp.ones_like(gain), jnp.zeros_like(gain)
    for k in reversed(range(1, 4)):
        after = k > place
        post = jnp.where(after, maps[k][0] * post + maps[k][1], post)
        post_gain = jnp.where(after, post_gain * maps[k][0], post_gain)
    mine_out[0], mine_out[1] = post_gain, post
    if len(sent_ref.shape) == 3:
        sent_ref[0], sent_ref[1] = gain, bwd
    else:
        sent_ref[...] = bwd


def earlier_four_kernel(*refs):
    gains, values, (sent_ref, mine_out) = refs[:4], refs[4:8], refs[8:]
    place = lax.rem(lax.axis_index("layer"), 4)
    maps = in_places(*((g[0], v[...]) for g, v in zip(gains, values)))
    fwd = maps[0][1]
    for here in maps[1:]:
        fwd = here[0] * fwd + here[1]
    pre_gain, pre = jnp.ones_like(fwd), jnp.zeros_like(fwd)
    for k in range(3):
        before = k < place
        pre = jnp.where(before, maps[k][0] * pre + maps[k][1], pre)
        pre_gain = jnp.where(before, pre_gain * maps[k][0], pre_gain)
    mine_out[0], mine_out[1] = pre_gain, pre
    sent_ref[...] = fwd


def later_kernel(step, total_ref, got_ref, mine_ref, sent_ref, mine_out):
    before = bit_of("layer", step)
    gain, bwd = total_ref[0], total_ref[1]
    got_gain, got = got_ref[0], got_ref[1]
    bwd = jnp.where(before, got_gain * bwd + got, gain * got + bwd)
    if len(sent_ref.shape) == 3:
        sent_ref[0], sent_ref[1] = gain * got_gain, bwd
    else:
        sent_ref[...] = bwd
    post_gain, post = mine_ref[0], mine_ref[1]
    mine_out[0] = jnp.where(before, post_gain, post_gain * got_gain)
    mine_out[1] = jnp.where(before, post, post_gain * got + post)


def earlier_kernel(step, total_ref, got_ref, fwd_ref, got_fwd_ref, mine_ref, sent_ref, mine_out):
    before = bit_of("layer", step)
    gain, got_gain = total_ref[0], got_ref[0]
    fwd, got = fwd_ref[...], got_fwd_ref[...]
    sent_ref[...] = jnp.where(before, gain * got + fwd, got_gain * fwd + got)
    pre_gain, pre = mine_ref[0], mine_ref[1]
    mine_out[0] = jnp.where(before, pre_gain * got_gain, pre_gain)
    mine_out[1] = jnp.where(before, pre_gain * got + pre, pre)


def later_fixed(steps, got_ref, mine_ref):
    got = jnp.where(bit_of("layer", steps - 1), 0.0, mine_ref[0] * got_ref[...])
    return mine_ref[1] + got


def fixed_kernel(
    steps, _, got_ref, mine_ref, late_ref, mine_fwd_ref, guess_ref, start_ref, adj_ref, state_ref
):
    place = lax.axis_index("layer")
    adj = in_order(later_fixed(steps, got_ref, mine_ref))
    late = jnp.where(bit_of("layer", steps - 1), mine_fwd_ref[0] * late_ref[...], 0.0)
    state = in_order(mine_fwd_ref[1] + late)
    adj_ref[0, 0] = jnp.where(place == lax.axis_size("layer") - 1, guess_ref[0, 0], adj)
    state_ref[0, 0] = jnp.where(place == 0, start_ref[0, 0], state)


def grad_kernel(
    steps,
    got_ref,
    mine_ref,
    guess_ref,
    slope_ref,
    patch_ref,
    back_w_ref,
    *part_refs,
):
    depth, chans, rows = back_w_ref.shape
    shares = len(part_refs)
    own = chans // shares
    last = lax.axis_index("layer") == lax.axis_size("layer") - 1
    adj = jnp.where(last, guess_ref[...], later_fixed(steps, got_ref, mine_ref))
    pad = part_refs[0].shape[1] - rows
    odd, high = bit_of("dp", 0), bit_of("dp", 1)

    def layer(n, adj):
        dz = adj * slope_ref[n]
        dzb = dz.astype(jnp.bfloat16)
        grad = dot(dzb, patch_ref[n], ((1,), (1,)))
        bias = jnp.broadcast_to(jnp.sum(dz, axis=1, keepdims=True), (chans, pad))
        both = jnp.concatenate([grad, bias], axis=1)
        where = pl.ds(pl.multiple_of(n * own, own), own)
        parts = [both[k * own : (k + 1) * own] for k in range(shares)]
        parts = [jnp.where(odd, parts[i ^ 1], parts[i]) for i in range(shares)]
        parts = [jnp.where(high, parts[i ^ 2], parts[i]) for i in range(shares)]
        for part, ref in zip(parts, part_refs):
            ref[where] = part
        return dzb

    def behind(i, adj):
        n = depth - 1 - i
        return adj + convolve(back_w_ref[n], layer(n, adj))

    layer(0, lax.fori_loop(0, depth - 1, behind, adj))


def total_kernel(mine_ref, both_ref, chip_ref, core_ref, grad_ref, bias_ref):
    depth, own, width = grad_ref.shape
    total = (mine_ref[...] + core_ref[...]) + (chip_ref[...] + both_ref[...])
    eye = lax.broadcasted_iota(jnp.int32, (own, own), 0) == lax.broadcasted_iota(
        jnp.int32, (own, own), 1
    )
    for n in range(depth):
        mine = total[n * own : (n + 1) * own]
        grad_ref[n] = mine[:, :width]
        column = jnp.broadcast_to(mine[:, width : width + 1], (own, own))
        bias_ref[n : n + 1, :] = jnp.sum(jnp.where(eye, column, 0.0), axis=0, keepdims=True)


def call(kernel, out_shape, args, hbm_in=(), hbm_out=(), scratch=(), work=2**28):
    return pl.pallas_call(
        kernel,
        out_shape=out_shape,
        in_specs=[HBM if k in hbm_in else VMEM for k in range(len(args))],
        out_specs=[HBM if k in hbm_out else VMEM for k in range(len(out_shape))],
        scratch_shapes=list(scratch),
        compiler_params=pltpu.CompilerParams(vmem_limit_bytes=LIMIT),
        cost_estimate=pl.CostEstimate(flops=work, bytes_accessed=0, transcendentals=0),
    )(*(pltpu.with_memory_space_constraint(a, pltpu.HBM) if k in hbm_in else a for k, a in enumerate(args)))


def f32(*shape):
    return jax.ShapeDtypeStruct(shape, jnp.float32)


def bf16(*shape):
    return jax.ShapeDtypeStruct(shape, jnp.bfloat16)


def exchange(x, axis, mask):
    return lax.ppermute(x, axis, [(i, i ^ mask) for i in range(lax.axis_size(axis))])


def local(state_guess, adjoint_guess, conv_weight, conv_bias):
    depth, chans, width = conv_weight.shape
    shares = lax.axis_size("dp")
    steps = lax.axis_size("layer").bit_length() - 1
    args = (state_guess, adjoint_guess, conv_weight, conv_bias)
    guess, total, fwd, slope, rounded, back_w = call(
        relax_kernel,
        (
            f32(chans, HW),
            f32(2, chans, HW),
            f32(chans, HW),
            f32(depth, chans, HW),
            bf16(depth, chans, HW),
            bf16(depth, chans, width),
        ),
        args,
        hbm_in=range(4),
        scratch=[pltpu.VMEM(a.shape, a.dtype) for a in args] + [pltpu.SemaphoreType.DMA((4,))],
    )
    (patch,) = call(patch_kernel, (bf16(depth, width, HW),), (rounded,))
    one, pair = f32(chans, HW), f32(2, chans, HW)
    gots = [exchange(total, "layer", mask) for mask in (1, 2, 3)]
    got_fwds = [exchange(fwd, "layer", mask) for mask in (1, 2, 3)]
    fwd, mine_fwd = call(
        earlier_four_kernel, (one, pair), (total, *gots, fwd, *got_fwds), work=0
    )
    total, mine = call(
        later_four_kernel, (one if steps == 3 else pair, pair), (total, *gots), work=0
    )
    for step in range(2, steps - 1):
        got, got_fwd = (exchange(x, "layer", 1 << step) for x in (total, fwd))
        fwd, mine_fwd = call(
            functools.partial(earlier_kernel, step),
            (one, pair),
            (total, got, fwd, got_fwd, mine_fwd),
            work=0,
        )
        total, mine = call(
            functools.partial(later_kernel, step),
            (one if step == steps - 2 else pair, pair),
            (total, got, mine),
            work=0,
        )
    got, late = (exchange(x, "layer", 1 << (steps - 1)) for x in (total, fwd))
    lanes = -(-(width + 1) // HALF) * HALF
    part = (depth * chans // shares, lanes)
    keep, *sends = call(
        functools.partial(grad_kernel, steps),
        (f32(*part),) * shares,
        (got, mine, guess, slope, patch, back_w),
        work=GRAD_WORK,
    )
    adjoint_fixed, state_fixed = call(
        functools.partial(fixed_kernel, steps),
        (f32(*adjoint_guess.shape), f32(*state_guess.shape)),
        (keep, got, mine, late, mine_fwd, adjoint_guess, state_guess),
        work=FIXED_WORK,
    )
    both = exchange(sends[2], "dp", 3)
    chip = exchange(sends[1], "dp", 2)
    core = exchange(sends[0], "dp", 1)
    weight_grad, bias_grad = call(
        total_kernel,
        (f32(depth, chans // shares, width), f32(depth, chans // shares)),
        (keep, both, chip, core),
    )
    return (state_fixed, adjoint_fixed, weight_grad, bias_grad)


def solution(mesh):
    placed = (
        P("layer", "dp", None, None),
        P("layer", "dp", None, None),
        P("layer", None, None),
        P("layer", None),
    )
    return jax.shard_map(
        local,
        mesh=mesh,
        in_specs=placed,
        out_specs=(
            P("layer", "dp", None, None),
            P("layer", "dp", None, None),
            P("layer", "dp", None),
            P("layer", "dp"),
        ),
        check_vma=False,
    )
```

```python
import functools

import jax
import jax.numpy as jnp
from jax import lax
from jax.experimental import pallas as pl
from jax.experimental.pallas import tpu as pltpu
from jax.sharding import PartitionSpec as P

IMG = 16
HW = IMG * IMG
HALF = 128
TAPS = 9
STEP = 0.5
LIMIT = 32 * 1024 * 1024

VMEM = pl.BlockSpec(memory_space=pltpu.VMEM)
HBM = pl.BlockSpec(memory_space=pltpu.HBM)


def picked(low, high, source, from_high):
    return jnp.where(
        from_high,
        jnp.take_along_axis(high, source, axis=1, mode="promise_in_bounds"),
        jnp.take_along_axis(low, source, axis=1, mode="promise_in_bounds"),
    )


def lanes_of(values):
    lane = lax.broadcasted_iota(jnp.int32, (values.shape[0], HALF), 1)
    return lane // IMG, lane % IMG


def by_parity(values):
    line, col = lanes_of(values)
    low, high = values[:, :HALF], values[:, HALF:]
    half = IMG // 4
    return jnp.concatenate(
        [
            picked(low, high, (2 * (line % half) + odd) * IMG + col, line >= half)
            for odd in range(2)
        ],
        axis=1,
    )


def in_order(values):
    line, col = lanes_of(values)
    even, odd = values[:, :HALF], values[:, HALF:]
    return jnp.concatenate(
        [
            picked(even, odd, (half * (IMG // 4) + line // 2) * IMG + col, line % 2 == 1)
            for half in range(2)
        ],
        axis=1,
    )


def taps_of(values):
    even, odd = values[:, :HALF], values[:, HALF:]
    lane = lax.broadcasted_iota(jnp.int16, even.shape, 1)
    col = lane & (IMG - 1)
    cols = {-1: [col >= 1], 0: [], 1: [col < IMG - 1]}

    def turned(half, lines, right):
        by = lines * IMG + right
        if not by:
            return half
        tests = cols[right] + {-1: [lane >= IMG], 0: [], 1: [lane < HALF - IMG]}[lines]
        part = pltpu.roll(half, -by % HALF, 1)
        return jnp.where(functools.reduce(jnp.logical_and, tests), part, jnp.zeros_like(part))

    above, here, below = [], [], []
    for right in (-1, 0, 1):
        same = turned(even, 0, right), turned(odd, 0, right)
        above.append((turned(odd, -1, right), same[0]))
        here.append(same)
        below.append((same[1], turned(even, 1, right)))
    return jnp.concatenate(
        [jnp.concatenate(pair, axis=1) for pair in above + here + below], axis=0
    )


def permutation(chans):
    size = TAPS * chans
    row = lax.broadcasted_iota(jnp.int32, (size, size), 0)
    column = lax.broadcasted_iota(jnp.int32, (size, size), 1)
    tap = lax.div(row, chans)
    return jnp.where(column == (row - tap * chans) * TAPS + tap, 1.0, 0.0).astype(jnp.bfloat16)


def dot(a, b, dims):
    return lax.dot_general(a, b, (dims, ((), ())), preferred_element_type=jnp.float32)


def convolve(weight, values):
    return dot(weight, taps_of(values), ((1,), (0,)))


def relax_kernel(
    state_hbm,
    adj_hbm,
    w_hbm,
    bias_hbm,
    guess_ref,
    sent_ref,
    slope_ref,
    rounded_ref,
    back_w_ref,
    state_ref,
    adj_ref,
    w_ref,
    bias_ref,
    sems,
):
    copies = [
        pltpu.make_async_copy(src, dst, sems.at[k])
        for k, (src, dst) in enumerate(
            ((w_hbm, w_ref), (state_hbm, state_ref), (bias_hbm, bias_ref), (adj_hbm, adj_ref))
        )
    ]
    for copy in copies:
        copy.start()
    depth, chans, width = w_ref.shape
    perm = permutation(chans)
    eye = lax.broadcasted_iota(jnp.int32, (chans, chans), 0) == lax.broadcasted_iota(
        jnp.int32, (chans, chans), 1
    )
    for copy in copies:
        copy.wait()
    weights = w_ref[...].reshape(depth * chans, width)
    by_tap = dot(weights, perm, ((1,), (1,)))
    turned = dot(perm, weights, ((1,), (1,))).astype(jnp.bfloat16)
    middle = TAPS // 2 * chans
    start = by_parity(state_ref[0, 0])
    guess = by_parity(adj_ref[0, 0])
    guess_ref[...] = guess
    state = start
    gain = None
    slopes = []
    backs = []
    for n in range(depth):
        mine = slice(n * chans, (n + 1) * chans)
        bias = jnp.broadcast_to(bias_ref[n : n + 1, :], (chans, chans))
        bias, kc = (
            jnp.sum(jnp.where(eye, square, 0.0), axis=1, keepdims=True)
            for square in (bias, by_tap[mine, middle : middle + chans])
        )
        rounded = state.astype(jnp.bfloat16)
        rounded_ref[n] = rounded
        squash = jnp.tanh(convolve(by_tap[mine].astype(jnp.bfloat16), rounded) + bias)
        slope = STEP * (1.0 - squash * squash)
        slope_ref[n] = slope
        slopes.append(slope)
        state = state + STEP * squash
        factor = 1.0 + slope * kc
        gain = factor if gain is None else gain * factor
        back_w = jnp.concatenate(
            [turned[t * chans : (t + 1) * chans, mine] for t in reversed(range(TAPS))], axis=1
        )
        back_w_ref[n] = back_w
        backs.append(back_w)
    back = guess
    for n in reversed(range(depth)):
        back = back + convolve(backs[n], (back * slopes[n]).astype(jnp.bfloat16))
    place = lax.axis_index("layer")
    first = jnp.where(place == 0, 0.0, start)
    last = jnp.where(place == lax.axis_size("layer") - 1, 0.0, guess)
    sent_ref[0] = gain
    sent_ref[1] = state - gain * first
    sent_ref[2] = back - gain * last


def put_patches(rounded_ref, patch_ref):
    depth, chans, _ = rounded_ref.shape
    perm = permutation(chans)
    for n in range(depth):
        patch = taps_of(rounded_ref[n])
        patch_ref[n] = dot(perm, patch, ((0,), (0,))).astype(jnp.bfloat16)


def patch_kernel(rounded_ref, early_ref, patch_ref):
    @pl.when(jnp.logical_not(bit_of("dp", 0)))
    def _():
        put_patches(rounded_ref, patch_ref)


def early_patch_kernel(rounded_ref, total_ref, patch_ref, sent_ref):
    sent_ref[...] = total_ref[...]

    @pl.when(bit_of("dp", 0))
    def _():
        put_patches(rounded_ref, patch_ref)


def joined(bit, total, mine, got):
    gain, fwd, bwd = total
    pre_gain, pre, post_gain, post = mine
    got_gain, got_fwd, got_bwd = got
    total = (
        gain * got_gain,
        jnp.where(bit, gain * got_fwd + fwd, got_gain * fwd + got_fwd),
        jnp.where(bit, got_gain * bwd + got_bwd, gain * got_bwd + bwd),
    )
    mine = (
        jnp.where(bit, pre_gain * got_gain, pre_gain),
        jnp.where(bit, pre_gain * got_fwd + pre, pre),
        jnp.where(bit, post_gain, post_gain * got_gain),
        jnp.where(bit, post, post_gain * got_bwd + post),
    )
    return total, mine


def bit_of(axis, step):
    return lax.rem(lax.div(lax.axis_index(axis), 2**step), 2) == 1


def put_joined(step, final, total, mine, sent_ref, mine_out):
    for k in range(4):
        mine_out[k] = mine[k]
    if final:
        sent_ref[...] = jnp.where(bit_of("layer", step), total[2], total[1])
    else:
        for k in range(3):
            sent_ref[k] = total[k]


def four_kernel(final, own_ref, first_ref, second_ref, third_ref, sent_ref, mine_out):
    low, high = bit_of("layer", 0), bit_of("layer", 1)
    place = lax.rem(lax.axis_index("layer"), 4)
    maps = [
        tuple(ref[k] for k in range(3)) for ref in (own_ref, first_ref, second_ref, third_ref)
    ]
    for bit, mask in ((low, 1), (high, 2)):
        maps = [
            tuple(jnp.where(bit, b, a) for a, b in zip(maps[k], maps[k ^ mask])) for k in range(4)
        ]
    one, zero = jnp.ones_like(maps[0][0]), jnp.zeros_like(maps[0][0])
    gain, fwd, bwd = maps[0]
    pre_gain, pre, post_gain, post = one, zero, one, zero
    for k in range(4):
        here = maps[k]
        before = k < place
        pre = jnp.where(before, here[0] * pre + here[1], pre)
        pre_gain = jnp.where(before, pre_gain * here[0], pre_gain)
        if k:
            bwd = bwd + gain * here[2]
            fwd = here[0] * fwd + here[1]
            gain = gain * here[0]
    for k in reversed(range(4)):
        here = maps[k]
        after = k > place
        post = jnp.where(after, here[0] * post + here[2], post)
        post_gain = jnp.where(after, post_gain * here[0], post_gain)
    mine = (pre_gain, pre, post_gain, post)
    put_joined(2, final, (gain, fwd, bwd), mine, sent_ref, mine_out)


def join_kernel(step, final, total_ref, got_ref, mine_ref, sent_ref, mine_out):
    total, got = (tuple(ref[k] for k in range(3)) for ref in (total_ref, got_ref))
    mine = tuple(mine_ref[k] for k in range(4))
    total, mine = joined(bit_of("layer", step - 1), total, mine, got)
    put_joined(step, final, total, mine, sent_ref, mine_out)


def later_fixed(steps, got_ref, mine_ref):
    got = jnp.where(bit_of("layer", steps - 1), 0.0, mine_ref[2] * got_ref[...])
    return mine_ref[3] + got


def fixed_kernel(steps, _, got_ref, mine_ref, guess_ref, start_ref, adj_ref, state_ref):
    place = lax.axis_index("layer")
    adj = in_order(later_fixed(steps, got_ref, mine_ref))
    got = jnp.where(bit_of("layer", steps - 1), mine_ref[0] * got_ref[...], 0.0)
    state = in_order(mine_ref[1] + got)
    adj_ref[0, 0] = jnp.where(place == lax.axis_size("layer") - 1, guess_ref[0, 0], adj)
    state_ref[0, 0] = jnp.where(place == 0, start_ref[0, 0], state)


def grad_kernel(
    steps,
    got_ref,
    mine_ref,
    guess_ref,
    slope_ref,
    patch_ref,
    back_w_ref,
    *part_refs,
):
    depth, chans, rows = back_w_ref.shape
    shares = len(part_refs)
    own = chans // shares
    last = lax.axis_index("layer") == lax.axis_size("layer") - 1
    adj = jnp.where(last, guess_ref[...], later_fixed(steps, got_ref, mine_ref))
    pad = part_refs[0].shape[1] - rows
    odd, high = bit_of("dp", 0), bit_of("dp", 1)

    def layer(n, adj):
        dz = adj * slope_ref[n]
        dzb = dz.astype(jnp.bfloat16)
        grad = dot(dzb, patch_ref[n], ((1,), (1,)))
        bias = jnp.broadcast_to(jnp.sum(dz, axis=1, keepdims=True), (chans, pad))
        both = jnp.concatenate([grad, bias], axis=1)
        where = pl.ds(pl.multiple_of(n * own, own), own)
        parts = [both[k * own : (k + 1) * own] for k in range(shares)]
        parts = [jnp.where(odd, parts[i ^ 1], parts[i]) for i in range(shares)]
        parts = [jnp.where(high, parts[i ^ 2], parts[i]) for i in range(shares)]
        for part, ref in zip(parts, part_refs):
            ref[where] = part
        return dzb

    def behind(i, adj):
        n = depth - 1 - i
        return adj + convolve(back_w_ref[n], layer(n, adj))

    layer(0, lax.fori_loop(0, depth - 1, behind, adj))


def total_kernel(mine_ref, both_ref, chip_ref, core_ref, grad_ref, bias_ref):
    depth, own, width = grad_ref.shape
    total = (mine_ref[...] + core_ref[...]) + (chip_ref[...] + both_ref[...])
    eye = lax.broadcasted_iota(jnp.int32, (own, own), 0) == lax.broadcasted_iota(
        jnp.int32, (own, own), 1
    )
    for n in range(depth):
        mine = total[n * own : (n + 1) * own]
        grad_ref[n] = mine[:, :width]
        column = jnp.broadcast_to(mine[:, width : width + 1], (own, own))
        bias_ref[n : n + 1, :] = jnp.sum(jnp.where(eye, column, 0.0), axis=0, keepdims=True)


def call(kernel, out_shape, args, hbm_in=(), hbm_out=(), scratch=(), aliases={}):
    return pl.pallas_call(
        kernel,
        out_shape=out_shape,
        in_specs=[HBM if k in hbm_in else VMEM for k in range(len(args))],
        out_specs=[HBM if k in hbm_out else VMEM for k in range(len(out_shape))],
        scratch_shapes=list(scratch),
        input_output_aliases=aliases,
        compiler_params=pltpu.CompilerParams(vmem_limit_bytes=LIMIT),
        cost_estimate=pl.CostEstimate(flops=2**28, bytes_accessed=2**20, transcendentals=0),
    )(*(pltpu.with_memory_space_constraint(a, pltpu.HBM) if k in hbm_in else a for k, a in enumerate(args)))


def f32(*shape):
    return jax.ShapeDtypeStruct(shape, jnp.float32)


def bf16(*shape):
    return jax.ShapeDtypeStruct(shape, jnp.bfloat16)


def exchange(x, axis, mask):
    return lax.ppermute(x, axis, [(i, i ^ mask) for i in range(lax.axis_size(axis))])


def local(state_guess, adjoint_guess, conv_weight, conv_bias):
    depth, chans, width = conv_weight.shape
    shares = lax.axis_size("dp")
    steps = lax.axis_size("layer").bit_length() - 1
    args = (state_guess, adjoint_guess, conv_weight, conv_bias)
    guess, total, slope, rounded, back_w = call(
        relax_kernel,
        (
            f32(chans, HW),
            f32(3, chans, HW),
            f32(depth, chans, HW),
            bf16(depth, chans, HW),
            bf16(depth, chans, width),
        ),
        args,
        hbm_in=range(4),
        scratch=[pltpu.VMEM(a.shape, a.dtype) for a in args] + [pltpu.SemaphoreType.DMA((4,))],
    )
    early, total = call(
        early_patch_kernel, (bf16(depth, width, HW), f32(3, chans, HW)), (rounded, total)
    )
    (patch,) = call(patch_kernel, (bf16(depth, width, HW),), (rounded, early), aliases={1: 0})
    one = f32(chans, HW)
    shapes = [(f32(3, chans, HW), f32(4, chans, HW))] * (steps - 3) + [(one, f32(4, chans, HW))]
    total, mine = call(
        functools.partial(four_kernel, steps == 3),
        shapes[0],
        (total, *(exchange(total, "layer", mask) for mask in (1, 2, 3))),
    )
    for step in range(3, steps):
        total, mine = call(
            functools.partial(join_kernel, step, step == steps - 1),
            shapes[step - 2],
            (total, exchange(total, "layer", 1 << (step - 1)), mine),
        )
    got = exchange(total, "layer", 1 << (steps - 1))
    lanes = -(-(width + 1) // HALF) * HALF
    part = (depth * chans // shares, lanes)
    keep, *sends = call(
        functools.partial(grad_kernel, steps),
        (f32(*part),) * shares,
        (got, mine, guess, slope, patch, back_w),
    )
    adjoint_fixed, state_fixed = call(
        functools.partial(fixed_kernel, steps),
        (f32(*adjoint_guess.shape), f32(*state_guess.shape)),
        (keep, got, mine, adjoint_guess, state_guess),
    )
    both = exchange(sends[2], "dp", 3)
    chip = exchange(sends[1], "dp", 2)
    core = exchange(sends[0], "dp", 1)
    weight_grad, bias_grad = call(
        total_kernel,
        (f32(depth, chans // shares, width), f32(depth, chans // shares)),
        (keep, both, chip, core),
    )
    return (state_fixed, adjoint_fixed, weight_grad, bias_grad)


def solution(mesh):
    placed = (
        P("layer", "dp", None, None),
        P("layer", "dp", None, None),
        P("layer", None, None),
        P("layer", None),
    )
    return jax.shard_map(
        local,
        mesh=mesh,
        in_specs=placed,
        out_specs=(
            P("layer", "dp", None, None),
            P("layer", "dp", None, None),
            P("layer", "dp", None),
            P("layer", "dp"),
        ),
        check_vma=False,
    )
```

```python
import functools

import jax
import jax.numpy as jnp
from jax import lax
from jax.experimental import pallas as pl
from jax.experimental.pallas import tpu as pltpu
from jax.sharding import PartitionSpec as P

IMG = 16
HW = IMG * IMG
HALF = 128
TAPS = 9
STEP = 0.5
LIMIT = 32 * 1024 * 1024

VMEM = pl.BlockSpec(memory_space=pltpu.VMEM)
HBM = pl.BlockSpec(memory_space=pltpu.HBM)


def picked(low, high, source, from_high):
    return jnp.where(
        from_high,
        jnp.take_along_axis(high, source, axis=1, mode="promise_in_bounds"),
        jnp.take_along_axis(low, source, axis=1, mode="promise_in_bounds"),
    )


def lanes_of(values):
    lane = lax.broadcasted_iota(jnp.int32, (values.shape[0], HALF), 1)
    return lane // IMG, lane % IMG


def by_parity(values):
    line, col = lanes_of(values)
    low, high = values[:, :HALF], values[:, HALF:]
    half = IMG // 4
    return jnp.concatenate(
        [
            picked(low, high, (2 * (line % half) + odd) * IMG + col, line >= half)
            for odd in range(2)
        ],
        axis=1,
    )


def in_order(values):
    line, col = lanes_of(values)
    even, odd = values[:, :HALF], values[:, HALF:]
    return jnp.concatenate(
        [
            picked(even, odd, (half * (IMG // 4) + line // 2) * IMG + col, line % 2 == 1)
            for half in range(2)
        ],
        axis=1,
    )


def taps_of(values):
    even, odd = values[:, :HALF], values[:, HALF:]
    lane = lax.broadcasted_iota(jnp.int16, even.shape, 1)
    col = lane & (IMG - 1)
    cols = {-1: [col >= 1], 0: [], 1: [col < IMG - 1]}

    def turned(half, lines, right):
        by = lines * IMG + right
        if not by:
            return half
        tests = cols[right] + {-1: [lane >= IMG], 0: [], 1: [lane < HALF - IMG]}[lines]
        part = pltpu.roll(half, -by % HALF, 1)
        return jnp.where(functools.reduce(jnp.logical_and, tests), part, jnp.zeros_like(part))

    above, here, below = [], [], []
    for right in (-1, 0, 1):
        same = turned(even, 0, right), turned(odd, 0, right)
        above.append((turned(odd, -1, right), same[0]))
        here.append(same)
        below.append((same[1], turned(even, 1, right)))
    return jnp.concatenate(
        [jnp.concatenate(pair, axis=1) for pair in above + here + below], axis=0
    )


def permutation(chans):
    size = TAPS * chans
    row = lax.broadcasted_iota(jnp.int32, (size, size), 0)
    column = lax.broadcasted_iota(jnp.int32, (size, size), 1)
    tap = lax.div(row, chans)
    return jnp.where(column == (row - tap * chans) * TAPS + tap, 1.0, 0.0).astype(jnp.bfloat16)


def dot(a, b, dims):
    return lax.dot_general(a, b, (dims, ((), ())), preferred_element_type=jnp.float32)


def convolve(weight, values):
    return dot(weight, taps_of(values), ((1,), (0,)))


def relax_kernel(
    state_hbm,
    adj_hbm,
    w_hbm,
    bias_hbm,
    guess_ref,
    sent_ref,
    slope_ref,
    rounded_ref,
    back_w_ref,
    state_ref,
    adj_ref,
    w_ref,
    bias_ref,
    sems,
):
    copies = [
        pltpu.make_async_copy(src, dst, sems.at[k])
        for k, (src, dst) in enumerate(
            ((w_hbm, w_ref), (state_hbm, state_ref), (bias_hbm, bias_ref), (adj_hbm, adj_ref))
        )
    ]
    for copy in copies:
        copy.start()
    depth, chans, width = w_ref.shape
    perm = permutation(chans)
    eye = lax.broadcasted_iota(jnp.int32, (chans, chans), 0) == lax.broadcasted_iota(
        jnp.int32, (chans, chans), 1
    )
    for copy in copies:
        copy.wait()
    weights = w_ref[...].reshape(depth * chans, width)
    by_tap = dot(weights, perm, ((1,), (1,)))
    turned = dot(perm, weights, ((1,), (1,))).astype(jnp.bfloat16)
    middle = TAPS // 2 * chans
    start = by_parity(state_ref[0, 0])
    guess = by_parity(adj_ref[0, 0])
    guess_ref[...] = guess
    state = start
    gain = None
    slopes = []
    backs = []
    for n in range(depth):
        mine = slice(n * chans, (n + 1) * chans)
        bias = jnp.broadcast_to(bias_ref[n : n + 1, :], (chans, chans))
        bias, kc = (
            jnp.sum(jnp.where(eye, square, 0.0), axis=1, keepdims=True)
            for square in (bias, by_tap[mine, middle : middle + chans])
        )
        rounded = state.astype(jnp.bfloat16)
        rounded_ref[n] = rounded
        squash = jnp.tanh(convolve(by_tap[mine].astype(jnp.bfloat16), rounded) + bias)
        slope = STEP * (1.0 - squash * squash)
        slope_ref[n] = slope
        slopes.append(slope)
        state = state + STEP * squash
        factor = 1.0 + slope * kc
        gain = factor if gain is None else gain * factor
        back_w = jnp.concatenate(
            [turned[t * chans : (t + 1) * chans, mine] for t in reversed(range(TAPS))], axis=1
        )
        back_w_ref[n] = back_w
        backs.append(back_w)
    back = guess
    for n in reversed(range(depth)):
        back = back + convolve(backs[n], (back * slopes[n]).astype(jnp.bfloat16))
    place = lax.axis_index("layer")
    first = jnp.where(place == 0, 0.0, start)
    last = jnp.where(place == lax.axis_size("layer") - 1, 0.0, guess)
    sent_ref[0] = gain
    sent_ref[1] = state - gain * first
    sent_ref[2] = back - gain * last


def patch_kernel(rounded_ref, patch_ref):
    depth, chans, _ = rounded_ref.shape
    perm = permutation(chans)
    for n in range(depth):
        patch = taps_of(rounded_ref[n])
        patch_ref[n] = dot(perm, patch, ((0,), (0,))).astype(jnp.bfloat16)


def joined(bit, total, mine, got):
    gain, fwd, bwd = total
    pre_gain, pre, post_gain, post = mine
    got_gain, got_fwd, got_bwd = got
    total = (
        gain * got_gain,
        jnp.where(bit, gain * got_fwd + fwd, got_gain * fwd + got_fwd),
        jnp.where(bit, got_gain * bwd + got_bwd, gain * got_bwd + bwd),
    )
    mine = (
        jnp.where(bit, pre_gain * got_gain, pre_gain),
        jnp.where(bit, pre_gain * got_fwd + pre, pre),
        jnp.where(bit, post_gain, post_gain * got_gain),
        jnp.where(bit, post, post_gain * got_bwd + post),
    )
    return total, mine


def bit_of(axis, step):
    return lax.rem(lax.div(lax.axis_index(axis), 2**step), 2) == 1


def put_joined(step, final, total, mine, sent_ref, mine_out):
    for k in range(4):
        mine_out[k] = mine[k]
    if final:
        sent_ref[...] = jnp.where(bit_of("layer", step), total[2], total[1])
    else:
        for k in range(3):
            sent_ref[k] = total[k]


def four_kernel(final, own_ref, second_ref, first_ref, third_ref, sent_ref, mine_out):
    low, high = bit_of("layer", 0), bit_of("layer", 1)
    place = lax.rem(lax.axis_index("layer"), 4)
    maps = [
        tuple(ref[k] for k in range(3)) for ref in (own_ref, first_ref, second_ref, third_ref)
    ]
    for bit, mask in ((low, 1), (high, 2)):
        maps = [
            tuple(jnp.where(bit, b, a) for a, b in zip(maps[k], maps[k ^ mask])) for k in range(4)
        ]
    one, zero = jnp.ones_like(maps[0][0]), jnp.zeros_like(maps[0][0])
    gain, fwd, bwd = maps[0]
    pre_gain, pre, post_gain, post = one, zero, one, zero
    for k in range(4):
        here = maps[k]
        before = k < place
        pre = jnp.where(before, here[0] * pre + here[1], pre)
        pre_gain = jnp.where(before, pre_gain * here[0], pre_gain)
        if k:
            bwd = bwd + gain * here[2]
            fwd = here[0] * fwd + here[1]
            gain = gain * here[0]
    for k in reversed(range(4)):
        here = maps[k]
        after = k > place
        post = jnp.where(after, here[0] * post + here[2], post)
        post_gain = jnp.where(after, post_gain * here[0], post_gain)
    mine = (pre_gain, pre, post_gain, post)
    put_joined(2, final, (gain, fwd, bwd), mine, sent_ref, mine_out)


def join_kernel(step, final, total_ref, got_ref, mine_ref, sent_ref, mine_out):
    total, got = (tuple(ref[k] for k in range(3)) for ref in (total_ref, got_ref))
    mine = tuple(mine_ref[k] for k in range(4))
    total, mine = joined(bit_of("layer", step - 1), total, mine, got)
    put_joined(step, final, total, mine, sent_ref, mine_out)


def later_fixed(steps, got_ref, mine_ref):
    got = jnp.where(bit_of("layer", steps - 1), 0.0, mine_ref[2] * got_ref[...])
    return mine_ref[3] + got


def fixed_kernel(steps, _, got_ref, mine_ref, guess_ref, start_ref, adj_ref, state_ref):
    place = lax.axis_index("layer")
    adj = in_order(later_fixed(steps, got_ref, mine_ref))
    got = jnp.where(bit_of("layer", steps - 1), mine_ref[0] * got_ref[...], 0.0)
    state = in_order(mine_ref[1] + got)
    adj_ref[0, 0] = jnp.where(place == lax.axis_size("layer") - 1, guess_ref[0, 0], adj)
    state_ref[0, 0] = jnp.where(place == 0, start_ref[0, 0], state)


def grad_kernel(
    steps,
    got_ref,
    mine_ref,
    guess_ref,
    slope_ref,
    patch_ref,
    back_w_ref,
    *part_refs,
):
    depth, chans, rows = back_w_ref.shape
    shares = len(part_refs)
    own = chans // shares
    last = lax.axis_index("layer") == lax.axis_size("layer") - 1
    adj = jnp.where(last, guess_ref[...], later_fixed(steps, got_ref, mine_ref))
    pad = part_refs[0].shape[1] - rows
    odd, high = bit_of("dp", 0), bit_of("dp", 1)

    def layer(n, adj):
        dz = adj * slope_ref[n]
        dzb = dz.astype(jnp.bfloat16)
        grad = dot(dzb, patch_ref[n], ((1,), (1,)))
        bias = jnp.broadcast_to(jnp.sum(dz, axis=1, keepdims=True), (chans, pad))
        both = jnp.concatenate([grad, bias], axis=1)
        where = pl.ds(pl.multiple_of(n * own, own), own)
        parts = [both[k * own : (k + 1) * own] for k in range(shares)]
        parts = [jnp.where(odd, parts[i ^ 1], parts[i]) for i in range(shares)]
        parts = [jnp.where(high, parts[i ^ 2], parts[i]) for i in range(shares)]
        for part, ref in zip(parts, part_refs):
            ref[where] = part
        return dzb

    def behind(i, adj):
        n = depth - 1 - i
        return adj + convolve(back_w_ref[n], layer(n, adj))

    layer(0, lax.fori_loop(0, depth - 1, behind, adj))


def total_kernel(mine_ref, chip_ref, both_ref, core_ref, grad_ref, bias_ref):
    depth, own, width = grad_ref.shape
    total = (mine_ref[...] + core_ref[...]) + (chip_ref[...] + both_ref[...])
    eye = lax.broadcasted_iota(jnp.int32, (own, own), 0) == lax.broadcasted_iota(
        jnp.int32, (own, own), 1
    )
    for n in range(depth):
        mine = total[n * own : (n + 1) * own]
        grad_ref[n] = mine[:, :width]
        column = jnp.broadcast_to(mine[:, width : width + 1], (own, own))
        bias_ref[n : n + 1, :] = jnp.sum(jnp.where(eye, column, 0.0), axis=0, keepdims=True)


def call(kernel, out_shape, args, hbm_in=(), hbm_out=(), scratch=()):
    return pl.pallas_call(
        kernel,
        out_shape=out_shape,
        in_specs=[HBM if k in hbm_in else VMEM for k in range(len(args))],
        out_specs=[HBM if k in hbm_out else VMEM for k in range(len(out_shape))],
        scratch_shapes=list(scratch),
        compiler_params=pltpu.CompilerParams(vmem_limit_bytes=LIMIT),
        cost_estimate=pl.CostEstimate(flops=2**28, bytes_accessed=2**20, transcendentals=0),
    )(*(pltpu.with_memory_space_constraint(a, pltpu.HBM) if k in hbm_in else a for k, a in enumerate(args)))


def f32(*shape):
    return jax.ShapeDtypeStruct(shape, jnp.float32)


def bf16(*shape):
    return jax.ShapeDtypeStruct(shape, jnp.bfloat16)


def exchange(x, axis, mask):
    return lax.ppermute(x, axis, [(i, i ^ mask) for i in range(lax.axis_size(axis))])


def local(state_guess, adjoint_guess, conv_weight, conv_bias):
    depth, chans, width = conv_weight.shape
    shares = lax.axis_size("dp")
    steps = lax.axis_size("layer").bit_length() - 1
    args = (state_guess, adjoint_guess, conv_weight, conv_bias)
    guess, total, slope, rounded, back_w = call(
        relax_kernel,
        (
            f32(chans, HW),
            f32(3, chans, HW),
            f32(depth, chans, HW),
            bf16(depth, chans, HW),
            bf16(depth, chans, width),
        ),
        args,
        hbm_in=range(4),
        scratch=[pltpu.VMEM(a.shape, a.dtype) for a in args] + [pltpu.SemaphoreType.DMA((4,))],
    )
    (patch,) = call(patch_kernel, (bf16(depth, width, HW),), (rounded,))
    one = f32(chans, HW)
    shapes = [(f32(3, chans, HW), f32(4, chans, HW))] * (steps - 3) + [(one, f32(4, chans, HW))]
    total, mine = call(
        functools.partial(four_kernel, steps == 3),
        shapes[0],
        (total, *(exchange(total, "layer", mask) for mask in (2, 1, 3))),
    )
    for step in range(3, steps):
        total, mine = call(
            functools.partial(join_kernel, step, step == steps - 1),
            shapes[step - 2],
            (total, exchange(total, "layer", 1 << (step - 1)), mine),
        )
    got = exchange(total, "layer", 1 << (steps - 1))
    lanes = -(-(width + 1) // HALF) * HALF
    part = (depth * chans // shares, lanes)
    keep, *sends = call(
        functools.partial(grad_kernel, steps),
        (f32(*part),) * shares,
        (got, mine, guess, slope, patch, back_w),
    )
    adjoint_fixed, state_fixed = call(
        functools.partial(fixed_kernel, steps),
        (f32(*adjoint_guess.shape), f32(*state_guess.shape)),
        (keep, got, mine, adjoint_guess, state_guess),
    )
    both = exchange(sends[2], "dp", 3)
    chip = exchange(sends[1], "dp", 2)
    core = exchange(sends[0], "dp", 1)
    weight_grad, bias_grad = call(
        total_kernel,
        (f32(depth, chans // shares, width), f32(depth, chans // shares)),
        (keep, chip, both, core),
    )
    return (state_fixed, adjoint_fixed, weight_grad, bias_grad)


def solution(mesh):
    placed = (
        P("layer", "dp", None, None),
        P("layer", "dp", None, None),
        P("layer", None, None),
        P("layer", None),
    )
    return jax.shard_map(
        local,
        mesh=mesh,
        in_specs=placed,
        out_specs=(
            P("layer", "dp", None, None),
            P("layer", "dp", None, None),
            P("layer", "dp", None),
            P("layer", "dp"),
        ),
        check_vma=False,
    )
```

```python
import functools

import jax
import jax.numpy as jnp
from jax import lax
from jax.experimental import pallas as pl
from jax.experimental.pallas import tpu as pltpu
from jax.sharding import PartitionSpec as P

IMG = 16
HW = IMG * IMG
HALF = 128
TAPS = 9
STEP = 0.5
LIMIT = 32 * 1024 * 1024

VMEM = pl.BlockSpec(memory_space=pltpu.VMEM)
HBM = pl.BlockSpec(memory_space=pltpu.HBM)


def picked(low, high, source, from_high):
    return jnp.where(
        from_high,
        jnp.take_along_axis(high, source, axis=1, mode="promise_in_bounds"),
        jnp.take_along_axis(low, source, axis=1, mode="promise_in_bounds"),
    )


def lanes_of(values):
    lane = lax.broadcasted_iota(jnp.int32, (values.shape[0], HALF), 1)
    return lane // IMG, lane % IMG


def by_parity(values):
    line, col = lanes_of(values)
    low, high = values[:, :HALF], values[:, HALF:]
    half = IMG // 4
    return jnp.concatenate(
        [
            picked(low, high, (2 * (line % half) + odd) * IMG + col, line >= half)
            for odd in range(2)
        ],
        axis=1,
    )


def in_order(values):
    line, col = lanes_of(values)
    even, odd = values[:, :HALF], values[:, HALF:]
    return jnp.concatenate(
        [
            picked(even, odd, (half * (IMG // 4) + line // 2) * IMG + col, line % 2 == 1)
            for half in range(2)
        ],
        axis=1,
    )


def taps_of(values):
    even, odd = values[:, :HALF], values[:, HALF:]
    lane = lax.broadcasted_iota(jnp.int16, even.shape, 1)
    col = lane & (IMG - 1)
    cols = {-1: [col >= 1], 0: [], 1: [col < IMG - 1]}

    def turned(half, lines, right):
        by = lines * IMG + right
        if not by:
            return half
        tests = cols[right] + {-1: [lane >= IMG], 0: [], 1: [lane < HALF - IMG]}[lines]
        part = pltpu.roll(half, -by % HALF, 1)
        return jnp.where(functools.reduce(jnp.logical_and, tests), part, jnp.zeros_like(part))

    above, here, below = [], [], []
    for right in (-1, 0, 1):
        same = turned(even, 0, right), turned(odd, 0, right)
        above.append((turned(odd, -1, right), same[0]))
        here.append(same)
        below.append((same[1], turned(even, 1, right)))
    return jnp.concatenate(
        [jnp.concatenate(pair, axis=1) for pair in above + here + below], axis=0
    )


def permutation(chans):
    size = TAPS * chans
    row = lax.broadcasted_iota(jnp.int32, (size, size), 0)
    column = lax.broadcasted_iota(jnp.int32, (size, size), 1)
    tap = lax.div(row, chans)
    return jnp.where(column == (row - tap * chans) * TAPS + tap, 1.0, 0.0).astype(jnp.bfloat16)


def dot(a, b, dims):
    return lax.dot_general(a, b, (dims, ((), ())), preferred_element_type=jnp.float32)


def convolve(weight, values):
    return dot(weight, taps_of(values), ((1,), (0,)))


def relax_kernel(
    state_hbm,
    adj_hbm,
    w_hbm,
    bias_hbm,
    guess_ref,
    sent_ref,
    slope_ref,
    rounded_ref,
    back_w_ref,
    state_ref,
    adj_ref,
    w_ref,
    bias_ref,
    sems,
):
    copies = [
        pltpu.make_async_copy(src, dst, sems.at[k])
        for k, (src, dst) in enumerate(
            ((w_hbm, w_ref), (state_hbm, state_ref), (bias_hbm, bias_ref), (adj_hbm, adj_ref))
        )
    ]
    for copy in copies:
        copy.start()
    depth, chans, width = w_ref.shape
    perm = permutation(chans)
    eye = lax.broadcasted_iota(jnp.int32, (chans, chans), 0) == lax.broadcasted_iota(
        jnp.int32, (chans, chans), 1
    )
    for copy in copies:
        copy.wait()
    weights = w_ref[...].reshape(depth * chans, width)
    by_tap = dot(weights, perm, ((1,), (1,)))
    turned = dot(perm, weights, ((1,), (1,))).astype(jnp.bfloat16)
    middle = TAPS // 2 * chans
    start = by_parity(state_ref[0, 0])
    guess = by_parity(adj_ref[0, 0])
    guess_ref[...] = guess
    state = start
    gain = None
    slopes = []
    backs = []
    for n in range(depth):
        mine = slice(n * chans, (n + 1) * chans)
        bias = jnp.broadcast_to(bias_ref[n : n + 1, :], (chans, chans))
        bias, kc = (
            jnp.sum(jnp.where(eye, square, 0.0), axis=1, keepdims=True)
            for square in (bias, by_tap[mine, middle : middle + chans])
        )
        rounded = state.astype(jnp.bfloat16)
        rounded_ref[n] = rounded
        squash = jnp.tanh(convolve(by_tap[mine].astype(jnp.bfloat16), rounded) + bias)
        slope = STEP * (1.0 - squash * squash)
        slope_ref[n] = slope
        slopes.append(slope)
        state = state + STEP * squash
        factor = 1.0 + slope * kc
        gain = factor if gain is None else gain * factor
        back_w = jnp.concatenate(
            [turned[t * chans : (t + 1) * chans, mine] for t in reversed(range(TAPS))], axis=1
        )
        back_w_ref[n] = back_w
        backs.append(back_w)
    back = guess
    for n in reversed(range(depth)):
        back = back + convolve(backs[n], (back * slopes[n]).astype(jnp.bfloat16))
    place = lax.axis_index("layer")
    first = jnp.where(place == 0, 0.0, start)
    last = jnp.where(place == lax.axis_size("layer") - 1, 0.0, guess)
    sent_ref[0] = gain
    sent_ref[1] = state - gain * first
    sent_ref[2] = back - gain * last


def patch_kernel(rounded_ref, patch_ref):
    depth, chans, _ = rounded_ref.shape
    perm = permutation(chans)
    for n in range(depth):
        patch = taps_of(rounded_ref[n])
        patch_ref[n] = dot(perm, patch, ((0,), (0,))).astype(jnp.bfloat16)


def joined(bit, total, mine, got):
    gain, fwd, bwd = total
    pre_gain, pre, post_gain, post = mine
    got_gain, got_fwd, got_bwd = got
    total = (
        gain * got_gain,
        jnp.where(bit, gain * got_fwd + fwd, got_gain * fwd + got_fwd),
        jnp.where(bit, got_gain * bwd + got_bwd, gain * got_bwd + bwd),
    )
    mine = (
        jnp.where(bit, pre_gain * got_gain, pre_gain),
        jnp.where(bit, pre_gain * got_fwd + pre, pre),
        jnp.where(bit, post_gain, post_gain * got_gain),
        jnp.where(bit, post, post_gain * got_bwd + post),
    )
    return total, mine


def bit_of(axis, step):
    return lax.rem(lax.div(lax.axis_index(axis), 2**step), 2) == 1


def put_joined(step, final, total, mine, sent_ref, mine_out):
    for k in range(4):
        mine_out[k] = mine[k]
    if final:
        sent_ref[...] = jnp.where(bit_of("layer", step), total[2], total[1])
    else:
        for k in range(3):
            sent_ref[k] = total[k]


def four_kernel(final, own_ref, second_ref, first_ref, third_ref, sent_ref, mine_out):
    low, high = bit_of("layer", 0), bit_of("layer", 1)
    place = lax.rem(lax.axis_index("layer"), 4)
    maps = [
        tuple(ref[k] for k in range(3)) for ref in (own_ref, first_ref, second_ref, third_ref)
    ]
    for bit, mask in ((low, 1), (high, 2)):
        maps = [
            tuple(jnp.where(bit, b, a) for a, b in zip(maps[k], maps[k ^ mask])) for k in range(4)
        ]
    one, zero = jnp.ones_like(maps[0][0]), jnp.zeros_like(maps[0][0])
    gain, fwd, bwd = maps[0]
    pre_gain, pre, post_gain, post = one, zero, one, zero
    for k in range(4):
        here = maps[k]
        before = k < place
        pre = jnp.where(before, here[0] * pre + here[1], pre)
        pre_gain = jnp.where(before, pre_gain * here[0], pre_gain)
        if k:
            bwd = bwd + gain * here[2]
            fwd = here[0] * fwd + here[1]
            gain = gain * here[0]
    for k in reversed(range(4)):
        here = maps[k]
        after = k > place
        post = jnp.where(after, here[0] * post + here[2], post)
        post_gain = jnp.where(after, post_gain * here[0], post_gain)
    mine = (pre_gain, pre, post_gain, post)
    put_joined(2, final, (gain, fwd, bwd), mine, sent_ref, mine_out)


def join_kernel(step, final, total_ref, got_ref, mine_ref, sent_ref, mine_out):
    total, got = (tuple(ref[k] for k in range(3)) for ref in (total_ref, got_ref))
    mine = tuple(mine_ref[k] for k in range(4))
    total, mine = joined(bit_of("layer", step - 1), total, mine, got)
    put_joined(step, final, total, mine, sent_ref, mine_out)


def later_fixed(steps, got_ref, mine_ref):
    got = jnp.where(bit_of("layer", steps - 1), 0.0, mine_ref[2] * got_ref[...])
    return mine_ref[3] + got


def fixed_kernel(steps, _, got_ref, mine_ref, guess_ref, start_ref, adj_ref, state_ref):
    place = lax.axis_index("layer")
    adj = in_order(later_fixed(steps, got_ref, mine_ref))
    got = jnp.where(bit_of("layer", steps - 1), mine_ref[0] * got_ref[...], 0.0)
    state = in_order(mine_ref[1] + got)
    adj_ref[0, 0] = jnp.where(place == lax.axis_size("layer") - 1, guess_ref[0, 0], adj)
    state_ref[0, 0] = jnp.where(place == 0, start_ref[0, 0], state)


def grad_kernel(
    steps,
    got_ref,
    mine_ref,
    guess_ref,
    slope_ref,
    patch_ref,
    back_w_ref,
    *part_refs,
):
    depth, chans, rows = back_w_ref.shape
    shares = len(part_refs)
    own = chans // shares
    last = lax.axis_index("layer") == lax.axis_size("layer") - 1
    adj = jnp.where(last, guess_ref[...], later_fixed(steps, got_ref, mine_ref))
    pad = part_refs[0].shape[1] - rows
    odd, high = bit_of("dp", 0), bit_of("dp", 1)

    def layer(n, adj):
        dz = adj * slope_ref[n]
        dzb = dz.astype(jnp.bfloat16)
        grad = dot(dzb, patch_ref[n], ((1,), (1,)))
        bias = jnp.broadcast_to(jnp.sum(dz, axis=1, keepdims=True), (chans, pad))
        both = jnp.concatenate([grad, bias], axis=1)
        where = pl.ds(pl.multiple_of(n * own, own), own)
        parts = [both[k * own : (k + 1) * own] for k in range(shares)]
        parts = [jnp.where(odd, parts[i ^ 1], parts[i]) for i in range(shares)]
        parts = [jnp.where(high, parts[i ^ 2], parts[i]) for i in range(shares)]
        for part, ref in zip(parts, part_refs):
            ref[where] = part
        return dzb

    def behind(i, adj):
        n = depth - 1 - i
        return adj + convolve(back_w_ref[n], layer(n, adj))

    layer(0, lax.fori_loop(0, depth - 1, behind, adj))


def total_kernel(mine_ref, both_ref, chip_ref, core_ref, grad_ref, bias_ref):
    depth, own, width = grad_ref.shape
    total = (mine_ref[...] + core_ref[...]) + (chip_ref[...] + both_ref[...])
    eye = lax.broadcasted_iota(jnp.int32, (own, own), 0) == lax.broadcasted_iota(
        jnp.int32, (own, own), 1
    )
    for n in range(depth):
        mine = total[n * own : (n + 1) * own]
        grad_ref[n] = mine[:, :width]
        column = jnp.broadcast_to(mine[:, width : width + 1], (own, own))
        bias_ref[n : n + 1, :] = jnp.sum(jnp.where(eye, column, 0.0), axis=0, keepdims=True)


def call(kernel, out_shape, args, hbm_in=(), hbm_out=(), scratch=()):
    return pl.pallas_call(
        kernel,
        out_shape=out_shape,
        in_specs=[HBM if k in hbm_in else VMEM for k in range(len(args))],
        out_specs=[HBM if k in hbm_out else VMEM for k in range(len(out_shape))],
        scratch_shapes=list(scratch),
        compiler_params=pltpu.CompilerParams(vmem_limit_bytes=LIMIT),
        cost_estimate=pl.CostEstimate(flops=2**28, bytes_accessed=2**20, transcendentals=0),
    )(*(pltpu.with_memory_space_constraint(a, pltpu.HBM) if k in hbm_in else a for k, a in enumerate(args)))


def f32(*shape):
    return jax.ShapeDtypeStruct(shape, jnp.float32)


def bf16(*shape):
    return jax.ShapeDtypeStruct(shape, jnp.bfloat16)


def exchange(x, axis, mask):
    return lax.ppermute(x, axis, [(i, i ^ mask) for i in range(lax.axis_size(axis))])


def local(state_guess, adjoint_guess, conv_weight, conv_bias):
    depth, chans, width = conv_weight.shape
    shares = lax.axis_size("dp")
    steps = lax.axis_size("layer").bit_length() - 1
    args = (state_guess, adjoint_guess, conv_weight, conv_bias)
    guess, total, slope, rounded, back_w = call(
        relax_kernel,
        (
            f32(chans, HW),
            f32(3, chans, HW),
            f32(depth, chans, HW),
            bf16(depth, chans, HW),
            bf16(depth, chans, width),
        ),
        args,
        hbm_in=range(4),
        scratch=[pltpu.VMEM(a.shape, a.dtype) for a in args] + [pltpu.SemaphoreType.DMA((4,))],
    )
    (patch,) = call(patch_kernel, (bf16(depth, width, HW),), (rounded,))
    one = f32(chans, HW)
    shapes = [(f32(3, chans, HW), f32(4, chans, HW))] * (steps - 3) + [(one, f32(4, chans, HW))]
    total, mine = call(
        functools.partial(four_kernel, steps == 3),
        shapes[0],
        (total, *(exchange(total, "layer", mask) for mask in (2, 1, 3))),
    )
    for step in range(3, steps):
        total, mine = call(
            functools.partial(join_kernel, step, step == steps - 1),
            shapes[step - 2],
            (total, exchange(total, "layer", 1 << (step - 1)), mine),
        )
    got = exchange(total, "layer", 1 << (steps - 1))
    lanes = -(-(width + 1) // HALF) * HALF
    part = (depth * chans // shares, lanes)
    keep, *sends = call(
        functools.partial(grad_kernel, steps),
        (f32(*part),) * shares,
        (got, mine, guess, slope, patch, back_w),
    )
    adjoint_fixed, state_fixed = call(
        functools.partial(fixed_kernel, steps),
        (f32(*adjoint_guess.shape), f32(*state_guess.shape)),
        (keep, got, mine, adjoint_guess, state_guess),
    )
    both = exchange(sends[2], "dp", 3)
    chip = exchange(sends[1], "dp", 2)
    core = exchange(sends[0], "dp", 1)
    weight_grad, bias_grad = call(
        total_kernel,
        (f32(depth, chans // shares, width), f32(depth, chans // shares)),
        (keep, both, chip, core),
    )
    return (state_fixed, adjoint_fixed, weight_grad, bias_grad)


def solution(mesh):
    placed = (
        P("layer", "dp", None, None),
        P("layer", "dp", None, None),
        P("layer", None, None),
        P("layer", None),
    )
    return jax.shard_map(
        local,
        mesh=mesh,
        in_specs=placed,
        out_specs=(
            P("layer", "dp", None, None),
            P("layer", "dp", None, None),
            P("layer", "dp", None),
            P("layer", "dp"),
        ),
        check_vma=False,
    )
```

```python
import functools

import jax
import jax.numpy as jnp
from jax import lax
from jax.experimental import pallas as pl
from jax.experimental.pallas import tpu as pltpu
from jax.sharding import PartitionSpec as P

IMG = 16
HW = IMG * IMG
HALF = 128
TAPS = 9
STEP = 0.5
LIMIT = 32 * 1024 * 1024

VMEM = pl.BlockSpec(memory_space=pltpu.VMEM)
HBM = pl.BlockSpec(memory_space=pltpu.HBM)


def picked(low, high, source, from_high):
    return jnp.where(
        from_high,
        jnp.take_along_axis(high, source, axis=1, mode="promise_in_bounds"),
        jnp.take_along_axis(low, source, axis=1, mode="promise_in_bounds"),
    )


def lanes_of(values):
    lane = lax.broadcasted_iota(jnp.int32, (values.shape[0], HALF), 1)
    return lane // IMG, lane % IMG


def by_parity(values):
    line, col = lanes_of(values)
    low, high = values[:, :HALF], values[:, HALF:]
    half = IMG // 4
    return jnp.concatenate(
        [
            picked(low, high, (2 * (line % half) + odd) * IMG + col, line >= half)
            for odd in range(2)
        ],
        axis=1,
    )


def in_order(values):
    line, col = lanes_of(values)
    even, odd = values[:, :HALF], values[:, HALF:]
    return jnp.concatenate(
        [
            picked(even, odd, (half * (IMG // 4) + line // 2) * IMG + col, line % 2 == 1)
            for half in range(2)
        ],
        axis=1,
    )


def taps_of(values):
    even, odd = values[:, :HALF], values[:, HALF:]
    lane = lax.broadcasted_iota(jnp.int16, even.shape, 1)
    col = lane & (IMG - 1)
    cols = {-1: [col >= 1], 0: [], 1: [col < IMG - 1]}

    def turned(half, lines, right):
        by = lines * IMG + right
        if not by:
            return half
        tests = cols[right] + {-1: [lane >= IMG], 0: [], 1: [lane < HALF - IMG]}[lines]
        part = pltpu.roll(half, -by % HALF, 1)
        return jnp.where(functools.reduce(jnp.logical_and, tests), part, jnp.zeros_like(part))

    above, here, below = [], [], []
    for right in (-1, 0, 1):
        same = turned(even, 0, right), turned(odd, 0, right)
        above.append((turned(odd, -1, right), same[0]))
        here.append(same)
        below.append((same[1], turned(even, 1, right)))
    return jnp.concatenate(
        [jnp.concatenate(pair, axis=1) for pair in above + here + below], axis=0
    )


def permutation(chans):
    size = TAPS * chans
    row = lax.broadcasted_iota(jnp.int32, (size, size), 0)
    column = lax.broadcasted_iota(jnp.int32, (size, size), 1)
    tap = lax.div(row, chans)
    return jnp.where(column == (row - tap * chans) * TAPS + tap, 1.0, 0.0).astype(jnp.bfloat16)


def dot(a, b, dims):
    return lax.dot_general(a, b, (dims, ((), ())), preferred_element_type=jnp.float32)


def convolve(weight, values):
    return dot(weight, taps_of(values), ((1,), (0,)))


def relax_kernel(
    state_hbm,
    adj_hbm,
    w_hbm,
    bias_hbm,
    guess_ref,
    sent_ref,
    slope_ref,
    rounded_ref,
    back_w_ref,
    state_ref,
    adj_ref,
    w_ref,
    bias_ref,
    sems,
):
    copies = [
        pltpu.make_async_copy(src, dst, sems.at[k])
        for k, (src, dst) in enumerate(
            ((w_hbm, w_ref), (state_hbm, state_ref), (bias_hbm, bias_ref), (adj_hbm, adj_ref))
        )
    ]
    for copy in copies:
        copy.start()
    depth, chans, width = w_ref.shape
    perm = permutation(chans)
    eye = lax.broadcasted_iota(jnp.int32, (chans, chans), 0) == lax.broadcasted_iota(
        jnp.int32, (chans, chans), 1
    )
    for copy in copies:
        copy.wait()
    weights = w_ref[...].reshape(depth * chans, width)
    by_tap = dot(weights, perm, ((1,), (1,)))
    middle = TAPS // 2 * chans
    start = by_parity(state_ref[0, 0])
    guess = by_parity(adj_ref[0, 0])
    guess_ref[...] = guess
    state = start
    gain = None
    slopes = []
    backs = []
    for n in range(depth):
        mine = slice(n * chans, (n + 1) * chans)
        bias = jnp.broadcast_to(bias_ref[n : n + 1, :], (chans, chans))
        bias, kc = (
            jnp.sum(jnp.where(eye, square, 0.0), axis=1, keepdims=True)
            for square in (bias, by_tap[mine, middle : middle + chans])
        )
        rounded = state.astype(jnp.bfloat16)
        rounded_ref[n] = rounded
        squash = jnp.tanh(convolve(by_tap[mine].astype(jnp.bfloat16), rounded) + bias)
        slope = STEP * (1.0 - squash * squash)
        slope_ref[n] = slope
        slopes.append(slope)
        state = state + STEP * squash
        factor = 1.0 + slope * kc
        gain = factor if gain is None else gain * factor
        if n == 1:
            turned = dot(perm, weights, ((1,), (1,))).astype(jnp.bfloat16)
    for n in range(depth):
        mine = slice(n * chans, (n + 1) * chans)
        back_w = jnp.concatenate(
            [turned[t * chans : (t + 1) * chans, mine] for t in reversed(range(TAPS))], axis=1
        )
        back_w_ref[n] = back_w
        backs.append(back_w)
    back = guess
    for n in reversed(range(depth)):
        back = back + convolve(backs[n], (back * slopes[n]).astype(jnp.bfloat16))
    place = lax.axis_index("layer")
    first = jnp.where(place == 0, 0.0, start)
    last = jnp.where(place == lax.axis_size("layer") - 1, 0.0, guess)
    sent_ref[0] = gain
    sent_ref[1] = state - gain * first
    sent_ref[2] = back - gain * last


def patch_kernel(rounded_ref, patch_ref):
    depth, chans, _ = rounded_ref.shape
    perm = permutation(chans)
    for n in range(depth):
        patch = taps_of(rounded_ref[n])
        patch_ref[n] = dot(perm, patch, ((0,), (0,))).astype(jnp.bfloat16)


def joined(bit, total, mine, got):
    gain, fwd, bwd = total
    pre_gain, pre, post_gain, post = mine
    got_gain, got_fwd, got_bwd = got
    total = (
        gain * got_gain,
        jnp.where(bit, gain * got_fwd + fwd, got_gain * fwd + got_fwd),
        jnp.where(bit, got_gain * bwd + got_bwd, gain * got_bwd + bwd),
    )
    mine = (
        jnp.where(bit, pre_gain * got_gain, pre_gain),
        jnp.where(bit, pre_gain * got_fwd + pre, pre),
        jnp.where(bit, post_gain, post_gain * got_gain),
        jnp.where(bit, post, post_gain * got_bwd + post),
    )
    return total, mine


def bit_of(axis, step):
    return lax.rem(lax.div(lax.axis_index(axis), 2**step), 2) == 1


def put_joined(step, final, total, mine, sent_ref, mine_out):
    for k in range(4):
        mine_out[k] = mine[k]
    if final:
        sent_ref[...] = jnp.where(bit_of("layer", step), total[2], total[1])
    else:
        for k in range(3):
            sent_ref[k] = total[k]


def four_kernel(final, own_ref, first_ref, second_ref, third_ref, sent_ref, mine_out):
    low, high = bit_of("layer", 0), bit_of("layer", 1)
    place = lax.rem(lax.axis_index("layer"), 4)
    maps = [
        tuple(ref[k] for k in range(3)) for ref in (own_ref, first_ref, second_ref, third_ref)
    ]
    for bit, mask in ((low, 1), (high, 2)):
        maps = [
            tuple(jnp.where(bit, b, a) for a, b in zip(maps[k], maps[k ^ mask])) for k in range(4)
        ]
    one, zero = jnp.ones_like(maps[0][0]), jnp.zeros_like(maps[0][0])
    gain, fwd, bwd = maps[0]
    pre_gain, pre, post_gain, post = one, zero, one, zero
    for k in range(4):
        here = maps[k]
        before = k < place
        pre = jnp.where(before, here[0] * pre + here[1], pre)
        pre_gain = jnp.where(before, pre_gain * here[0], pre_gain)
        if k:
            bwd = bwd + gain * here[2]
            fwd = here[0] * fwd + here[1]
            gain = gain * here[0]
    for k in reversed(range(4)):
        here = maps[k]
        after = k > place
        post = jnp.where(after, here[0] * post + here[2], post)
        post_gain = jnp.where(after, post_gain * here[0], post_gain)
    mine = (pre_gain, pre, post_gain, post)
    put_joined(2, final, (gain, fwd, bwd), mine, sent_ref, mine_out)


def join_kernel(step, final, total_ref, got_ref, mine_ref, sent_ref, mine_out):
    total, got = (tuple(ref[k] for k in range(3)) for ref in (total_ref, got_ref))
    mine = tuple(mine_ref[k] for k in range(4))
    total, mine = joined(bit_of("layer", step - 1), total, mine, got)
    put_joined(step, final, total, mine, sent_ref, mine_out)


def later_fixed(steps, got_ref, mine_ref):
    got = jnp.where(bit_of("layer", steps - 1), 0.0, mine_ref[2] * got_ref[...])
    return mine_ref[3] + got


def fixed_kernel(steps, _, got_ref, mine_ref, guess_ref, start_ref, adj_ref, state_ref):
    place = lax.axis_index("layer")
    adj = in_order(later_fixed(steps, got_ref, mine_ref))
    got = jnp.where(bit_of("layer", steps - 1), mine_ref[0] * got_ref[...], 0.0)
    state = in_order(mine_ref[1] + got)
    adj_ref[0, 0] = jnp.where(place == lax.axis_size("layer") - 1, guess_ref[0, 0], adj)
    state_ref[0, 0] = jnp.where(place == 0, start_ref[0, 0], state)


def grad_kernel(
    steps,
    got_ref,
    mine_ref,
    guess_ref,
    slope_ref,
    patch_ref,
    back_w_ref,
    *part_refs,
):
    depth, chans, rows = back_w_ref.shape
    shares = len(part_refs)
    own = chans // shares
    last = lax.axis_index("layer") == lax.axis_size("layer") - 1
    adj = jnp.where(last, guess_ref[...], later_fixed(steps, got_ref, mine_ref))
    pad = part_refs[0].shape[1] - rows
    odd, high = bit_of("dp", 0), bit_of("dp", 1)

    def through(n, adj):
        dz = adj * slope_ref[n]
        return dz, dz.astype(jnp.bfloat16)

    def gradients(n, dz, dzb):
        grad = dot(dzb, patch_ref[n], ((1,), (1,)))
        bias = jnp.broadcast_to(jnp.sum(dz, axis=1, keepdims=True), (chans, pad))
        both = jnp.concatenate([grad, bias], axis=1)
        where = pl.ds(pl.multiple_of(n * own, own), own)
        parts = [both[k * own : (k + 1) * own] for k in range(shares)]
        parts = [jnp.where(odd, parts[i ^ 1], parts[i]) for i in range(shares)]
        parts = [jnp.where(high, parts[i ^ 2], parts[i]) for i in range(shares)]
        for part, ref in zip(parts, part_refs):
            ref[where] = part

    def behind(i, adj):
        n = depth - 1 - i
        dz, dzb = through(n, adj)
        adj = adj + convolve(back_w_ref[n], dzb)
        gradients(n, dz, dzb)
        return adj

    gradients(0, *through(0, lax.fori_loop(0, depth - 1, behind, adj)))


def total_kernel(mine_ref, both_ref, chip_ref, core_ref, grad_ref, bias_ref):
    depth, own, width = grad_ref.shape
    total = (mine_ref[...] + core_ref[...]) + (chip_ref[...] + both_ref[...])
    eye = lax.broadcasted_iota(jnp.int32, (own, own), 0) == lax.broadcasted_iota(
        jnp.int32, (own, own), 1
    )
    for n in range(depth):
        mine = total[n * own : (n + 1) * own]
        grad_ref[n] = mine[:, :width]
        column = jnp.broadcast_to(mine[:, width : width + 1], (own, own))
        bias_ref[n : n + 1, :] = jnp.sum(jnp.where(eye, column, 0.0), axis=0, keepdims=True)


def call(kernel, out_shape, args, hbm_in=(), hbm_out=(), scratch=()):
    return pl.pallas_call(
        kernel,
        out_shape=out_shape,
        in_specs=[HBM if k in hbm_in else VMEM for k in range(len(args))],
        out_specs=[HBM if k in hbm_out else VMEM for k in range(len(out_shape))],
        scratch_shapes=list(scratch),
        compiler_params=pltpu.CompilerParams(vmem_limit_bytes=LIMIT),
        cost_estimate=pl.CostEstimate(flops=2**28, bytes_accessed=2**20, transcendentals=0),
    )(*(pltpu.with_memory_space_constraint(a, pltpu.HBM) if k in hbm_in else a for k, a in enumerate(args)))


def f32(*shape):
    return jax.ShapeDtypeStruct(shape, jnp.float32)


def bf16(*shape):
    return jax.ShapeDtypeStruct(shape, jnp.bfloat16)


def exchange(x, axis, mask):
    return lax.ppermute(x, axis, [(i, i ^ mask) for i in range(lax.axis_size(axis))])


def local(state_guess, adjoint_guess, conv_weight, conv_bias):
    depth, chans, width = conv_weight.shape
    shares = lax.axis_size("dp")
    steps = lax.axis_size("layer").bit_length() - 1
    args = (state_guess, adjoint_guess, conv_weight, conv_bias)
    guess, total, slope, rounded, back_w = call(
        relax_kernel,
        (
            f32(chans, HW),
            f32(3, chans, HW),
            f32(depth, chans, HW),
            bf16(depth, chans, HW),
            bf16(depth, chans, width),
        ),
        args,
        hbm_in=range(4),
        scratch=[pltpu.VMEM(a.shape, a.dtype) for a in args] + [pltpu.SemaphoreType.DMA((4,))],
    )
    (patch,) = call(patch_kernel, (bf16(depth, width, HW),), (rounded,))
    one = f32(chans, HW)
    shapes = [(f32(3, chans, HW), f32(4, chans, HW))] * (steps - 3) + [(one, f32(4, chans, HW))]
    total, mine = call(
        functools.partial(four_kernel, steps == 3),
        shapes[0],
        (total, *(exchange(total, "layer", mask) for mask in (1, 2, 3))),
    )
    for step in range(3, steps):
        total, mine = call(
            functools.partial(join_kernel, step, step == steps - 1),
            shapes[step - 2],
            (total, exchange(total, "layer", 1 << (step - 1)), mine),
        )
    got = exchange(total, "layer", 1 << (steps - 1))
    lanes = -(-(width + 1) // HALF) * HALF
    part = (depth * chans // shares, lanes)
    keep, *sends = call(
        functools.partial(grad_kernel, steps),
        (f32(*part),) * shares,
        (got, mine, guess, slope, patch, back_w),
    )
    adjoint_fixed, state_fixed = call(
        functools.partial(fixed_kernel, steps),
        (f32(*adjoint_guess.shape), f32(*state_guess.shape)),
        (keep, got, mine, adjoint_guess, state_guess),
    )
    both = exchange(sends[2], "dp", 3)
    chip = exchange(sends[1], "dp", 2)
    core = exchange(sends[0], "dp", 1)
    weight_grad, bias_grad = call(
        total_kernel,
        (f32(depth, chans // shares, width), f32(depth, chans // shares)),
        (keep, both, chip, core),
    )
    return (state_fixed, adjoint_fixed, weight_grad, bias_grad)


def solution(mesh):
    placed = (
        P("layer", "dp", None, None),
        P("layer", "dp", None, None),
        P("layer", None, None),
        P("layer", None),
    )
    return jax.shard_map(
        local,
        mesh=mesh,
        in_specs=placed,
        out_specs=(
            P("layer", "dp", None, None),
            P("layer", "dp", None, None),
            P("layer", "dp", None),
            P("layer", "dp"),
        ),
        check_vma=False,
    )
```

```python
import functools

import jax
import jax.numpy as jnp
from jax import lax
from jax.experimental import pallas as pl
from jax.experimental.pallas import tpu as pltpu
from jax.sharding import PartitionSpec as P

IMG = 16
HW = IMG * IMG
HALF = 128
TAPS = 9
STEP = 0.5
LIMIT = 32 * 1024 * 1024

VMEM = pl.BlockSpec(memory_space=pltpu.VMEM)
HBM = pl.BlockSpec(memory_space=pltpu.HBM)


def picked(low, high, source, from_high):
    return jnp.where(
        from_high,
        jnp.take_along_axis(high, source, axis=1, mode="promise_in_bounds"),
        jnp.take_along_axis(low, source, axis=1, mode="promise_in_bounds"),
    )


def lanes_of(values):
    lane = lax.broadcasted_iota(jnp.int32, (values.shape[0], HALF), 1)
    return lane // IMG, lane % IMG


def by_parity(values):
    line, col = lanes_of(values)
    low, high = values[:, :HALF], values[:, HALF:]
    half = IMG // 4
    return jnp.concatenate(
        [
            picked(low, high, (2 * (line % half) + odd) * IMG + col, line >= half)
            for odd in range(2)
        ],
        axis=1,
    )


def in_order(values):
    line, col = lanes_of(values)
    even, odd = values[:, :HALF], values[:, HALF:]
    return jnp.concatenate(
        [
            picked(even, odd, (half * (IMG // 4) + line // 2) * IMG + col, line % 2 == 1)
            for half in range(2)
        ],
        axis=1,
    )


def taps_of(values):
    even, odd = values[:, :HALF], values[:, HALF:]
    lane = lax.broadcasted_iota(jnp.int16, even.shape, 1)
    col = lane & (IMG - 1)
    cols = {-1: [col >= 1], 0: [], 1: [col < IMG - 1]}

    def turned(half, lines, right):
        by = lines * IMG + right
        if not by:
            return half
        tests = cols[right] + {-1: [lane >= IMG], 0: [], 1: [lane < HALF - IMG]}[lines]
        part = pltpu.roll(half, -by % HALF, 1)
        return jnp.where(functools.reduce(jnp.logical_and, tests), part, jnp.zeros_like(part))

    above, here, below = [], [], []
    for right in (-1, 0, 1):
        same = turned(even, 0, right), turned(odd, 0, right)
        above.append((turned(odd, -1, right), same[0]))
        here.append(same)
        below.append((same[1], turned(even, 1, right)))
    return jnp.concatenate(
        [jnp.concatenate(pair, axis=1) for pair in above + here + below], axis=0
    )


def permutation(chans):
    size = TAPS * chans
    row = lax.broadcasted_iota(jnp.int32, (size, size), 0)
    column = lax.broadcasted_iota(jnp.int32, (size, size), 1)
    tap = lax.div(row, chans)
    return jnp.where(column == (row - tap * chans) * TAPS + tap, 1.0, 0.0).astype(jnp.bfloat16)


def dot(a, b, dims):
    return lax.dot_general(a, b, (dims, ((), ())), preferred_element_type=jnp.float32)


def convolve(weight, values):
    return dot(weight, taps_of(values), ((1,), (0,)))


def relax_kernel(
    state_hbm,
    adj_hbm,
    w_hbm,
    bias_hbm,
    guess_ref,
    sent_ref,
    slope_ref,
    rounded_ref,
    back_w_ref,
    state_ref,
    adj_ref,
    w_ref,
    bias_ref,
    sems,
):
    copies = [
        pltpu.make_async_copy(src, dst, sems.at[k])
        for k, (src, dst) in enumerate(
            ((w_hbm, w_ref), (state_hbm, state_ref), (bias_hbm, bias_ref), (adj_hbm, adj_ref))
        )
    ]
    for copy in copies:
        copy.start()
    depth, chans, width = w_ref.shape
    perm = permutation(chans)
    eye = lax.broadcasted_iota(jnp.int32, (chans, chans), 0) == lax.broadcasted_iota(
        jnp.int32, (chans, chans), 1
    )
    for copy in copies:
        copy.wait()
    weights = w_ref[...].reshape(depth * chans, width)
    by_tap = dot(weights, perm, ((1,), (1,)))
    turned = dot(perm, weights, ((1,), (1,))).astype(jnp.bfloat16)
    middle = TAPS // 2 * chans
    start = by_parity(state_ref[0, 0])
    guess = by_parity(adj_ref[0, 0])
    guess_ref[...] = guess
    state = start
    gain = None
    slopes = []
    backs = []
    for n in range(depth):
        mine = slice(n * chans, (n + 1) * chans)
        bias = jnp.broadcast_to(bias_ref[n : n + 1, :], (chans, chans))
        bias, kc = (
            jnp.sum(jnp.where(eye, square, 0.0), axis=1, keepdims=True)
            for square in (bias, by_tap[mine, middle : middle + chans])
        )
        rounded = state.astype(jnp.bfloat16)
        rounded_ref[n] = rounded
        squash = jnp.tanh(convolve(by_tap[mine].astype(jnp.bfloat16), rounded) + bias)
        slope = STEP * (1.0 - squash * squash)
        slope_ref[n] = slope
        slopes.append(slope)
        state = state + STEP * squash
        factor = 1.0 + slope * kc
        gain = factor if gain is None else gain * factor
        back_w = jnp.concatenate(
            [turned[t * chans : (t + 1) * chans, mine] for t in reversed(range(TAPS))], axis=1
        )
        back_w_ref[n] = back_w
        backs.append(back_w)
    back = guess
    for n in reversed(range(depth)):
        back = back + convolve(backs[n], (back * slopes[n]).astype(jnp.bfloat16))
    place = lax.axis_index("layer")
    first = jnp.where(place == 0, 0.0, start)
    last = jnp.where(place == lax.axis_size("layer") - 1, 0.0, guess)
    sent_ref[0] = gain
    sent_ref[1] = state - gain * first
    sent_ref[2] = back - gain * last


def patch_kernel(rounded_ref, patch_ref):
    depth, chans, _ = rounded_ref.shape
    perm = permutation(chans)
    for n in range(depth):
        patch = taps_of(rounded_ref[n])
        patch_ref[n] = dot(perm, patch, ((0,), (0,))).astype(jnp.bfloat16)


def joined(bit, total, mine, got):
    gain, fwd, bwd = total
    pre_gain, pre, post_gain, post = mine
    got_gain, got_fwd, got_bwd = got
    total = (
        gain * got_gain,
        jnp.where(bit, gain * got_fwd + fwd, got_gain * fwd + got_fwd),
        jnp.where(bit, got_gain * bwd + got_bwd, gain * got_bwd + bwd),
    )
    mine = (
        jnp.where(bit, pre_gain * got_gain, pre_gain),
        jnp.where(bit, pre_gain * got_fwd + pre, pre),
        jnp.where(bit, post_gain, post_gain * got_gain),
        jnp.where(bit, post, post_gain * got_bwd + post),
    )
    return total, mine


def bit_of(axis, step):
    return lax.rem(lax.div(lax.axis_index(axis), 2**step), 2) == 1


def put_joined(step, final, total, mine, sent_ref, mine_out):
    for k in range(4):
        mine_out[k] = mine[k]
    if final:
        sent_ref[...] = jnp.where(bit_of("layer", step), total[2], total[1])
    else:
        for k in range(3):
            sent_ref[k] = total[k]


def four_kernel(final, own_ref, first_ref, second_ref, third_ref, sent_ref, mine_out):
    low, high = bit_of("layer", 0), bit_of("layer", 1)
    place = lax.rem(lax.axis_index("layer"), 4)
    maps = [
        tuple(ref[k] for k in range(3)) for ref in (own_ref, first_ref, second_ref, third_ref)
    ]
    for bit, mask in ((low, 1), (high, 2)):
        maps = [
            tuple(jnp.where(bit, b, a) for a, b in zip(maps[k], maps[k ^ mask])) for k in range(4)
        ]
    one, zero = jnp.ones_like(maps[0][0]), jnp.zeros_like(maps[0][0])
    gain, fwd, bwd = maps[0]
    pre_gain, pre, post_gain, post = one, zero, one, zero
    for k in range(4):
        here = maps[k]
        before = k < place
        pre = jnp.where(before, here[0] * pre + here[1], pre)
        pre_gain = jnp.where(before, pre_gain * here[0], pre_gain)
        if k:
            bwd = bwd + gain * here[2]
            fwd = here[0] * fwd + here[1]
            gain = gain * here[0]
    for k in reversed(range(4)):
        here = maps[k]
        after = k > place
        post = jnp.where(after, here[0] * post + here[2], post)
        post_gain = jnp.where(after, post_gain * here[0], post_gain)
    mine = (pre_gain, pre, post_gain, post)
    put_joined(2, final, (gain, fwd, bwd), mine, sent_ref, mine_out)


def join_kernel(step, final, total_ref, got_ref, mine_ref, sent_ref, mine_out):
    total, got = (tuple(ref[k] for k in range(3)) for ref in (total_ref, got_ref))
    mine = tuple(mine_ref[k] for k in range(4))
    total, mine = joined(bit_of("layer", step - 1), total, mine, got)
    put_joined(step, final, total, mine, sent_ref, mine_out)


def later_fixed(steps, got_ref, mine_ref):
    got = jnp.where(bit_of("layer", steps - 1), 0.0, mine_ref[2] * got_ref[...])
    return mine_ref[3] + got


def fixed_kernel(steps, _, got_ref, mine_ref, guess_ref, start_ref, adj_ref, state_ref):
    place = lax.axis_index("layer")
    adj = in_order(later_fixed(steps, got_ref, mine_ref))
    got = jnp.where(bit_of("layer", steps - 1), mine_ref[0] * got_ref[...], 0.0)
    state = in_order(mine_ref[1] + got)
    adj_ref[0, 0] = jnp.where(place == lax.axis_size("layer") - 1, guess_ref[0, 0], adj)
    state_ref[0, 0] = jnp.where(place == 0, start_ref[0, 0], state)


def grad_kernel(
    steps,
    got_ref,
    mine_ref,
    guess_ref,
    slope_ref,
    patch_ref,
    back_w_ref,
    *part_refs,
):
    depth, chans, rows = back_w_ref.shape
    shares = len(part_refs)
    own = chans // shares
    last = lax.axis_index("layer") == lax.axis_size("layer") - 1
    adj = jnp.where(last, guess_ref[...], later_fixed(steps, got_ref, mine_ref))
    full = rows // HALF * HALF
    block, base = depth * own, depth * own * (full // HALF)
    odd, high = bit_of("dp", 0), bit_of("dp", 1)

    def layer(n, adj):
        dz = adj * slope_ref[n]
        dzb = dz.astype(jnp.bfloat16)
        grad = dot(dzb, patch_ref[n], ((1,), (1,)))
        bias = jnp.broadcast_to(jnp.sum(dz, axis=1, keepdims=True), (chans, HALF))
        start = pl.multiple_of(n * own, own)
        rest = jnp.concatenate([grad[:, full:]] * depth, axis=1)
        both = jnp.concatenate([grad[:, :full], rest, bias], axis=1)
        parts = [both[k * own : (k + 1) * own] for k in range(shares)]
        parts = [jnp.where(odd, parts[i ^ 1], parts[i]) for i in range(shares)]
        parts = [jnp.where(high, parts[i ^ 2], parts[i]) for i in range(shares)]
        lane = lax.broadcasted_iota(jnp.int32, (own, HALF), 1)
        for part, ref in zip(parts, part_refs):
            for k in range(full // HALF):
                ref[pl.ds(k * block + start, own)] = part[:, k * HALF : (k + 1) * HALF]
            for k, here in ((0, lane // (rows - full) == n), (1, lane % depth == n)):
                tile = slice(base + k * own, base + (k + 1) * own)
                at = full + k * HALF
                ref[tile] = jnp.where(here, part[:, at : at + HALF], ref[tile])
        return dzb

    def behind(i, adj):
        n = depth - 1 - i
        return adj + convolve(back_w_ref[n], layer(n, adj))

    layer(0, lax.fori_loop(0, depth - 1, behind, adj))


def total_kernel(mine_ref, both_ref, chip_ref, core_ref, grad_ref, bias_ref):
    depth, own, width = grad_ref.shape
    total = (mine_ref[...] + core_ref[...]) + (chip_ref[...] + both_ref[...])
    eye = lax.broadcasted_iota(jnp.int32, (own, own), 0) == lax.broadcasted_iota(
        jnp.int32, (own, own), 1
    )
    full = width // HALF
    base, rest = depth * own * full, width - full * HALF
    for n in range(depth):
        pieces = [total[(k * depth + n) * own : (k * depth + n + 1) * own] for k in range(full)]
        pieces.append(total[base : base + own, n * rest : (n + 1) * rest])
        grad_ref[n] = jnp.concatenate(pieces, axis=1)
        column = jnp.broadcast_to(total[base + own : base + 2 * own, n : n + 1], (own, own))
        bias_ref[n : n + 1, :] = jnp.sum(jnp.where(eye, column, 0.0), axis=0, keepdims=True)


def call(kernel, out_shape, args, hbm_in=(), hbm_out=(), scratch=()):
    return pl.pallas_call(
        kernel,
        out_shape=out_shape,
        in_specs=[HBM if k in hbm_in else VMEM for k in range(len(args))],
        out_specs=[HBM if k in hbm_out else VMEM for k in range(len(out_shape))],
        scratch_shapes=list(scratch),
        compiler_params=pltpu.CompilerParams(vmem_limit_bytes=LIMIT),
        cost_estimate=pl.CostEstimate(flops=2**28, bytes_accessed=2**20, transcendentals=0),
    )(*(pltpu.with_memory_space_constraint(a, pltpu.HBM) if k in hbm_in else a for k, a in enumerate(args)))


def f32(*shape):
    return jax.ShapeDtypeStruct(shape, jnp.float32)


def bf16(*shape):
    return jax.ShapeDtypeStruct(shape, jnp.bfloat16)


def exchange(x, axis, mask):
    return lax.ppermute(x, axis, [(i, i ^ mask) for i in range(lax.axis_size(axis))])


def local(state_guess, adjoint_guess, conv_weight, conv_bias):
    depth, chans, width = conv_weight.shape
    shares = lax.axis_size("dp")
    steps = lax.axis_size("layer").bit_length() - 1
    args = (state_guess, adjoint_guess, conv_weight, conv_bias)
    guess, total, slope, rounded, back_w = call(
        relax_kernel,
        (
            f32(chans, HW),
            f32(3, chans, HW),
            f32(depth, chans, HW),
            bf16(depth, chans, HW),
            bf16(depth, chans, width),
        ),
        args,
        hbm_in=range(4),
        scratch=[pltpu.VMEM(a.shape, a.dtype) for a in args] + [pltpu.SemaphoreType.DMA((4,))],
    )
    (patch,) = call(patch_kernel, (bf16(depth, width, HW),), (rounded,))
    one = f32(chans, HW)
    shapes = [(f32(3, chans, HW), f32(4, chans, HW))] * (steps - 3) + [(one, f32(4, chans, HW))]
    total, mine = call(
        functools.partial(four_kernel, steps == 3),
        shapes[0],
        (total, *(exchange(total, "layer", mask) for mask in (1, 2, 3))),
    )
    for step in range(3, steps):
        total, mine = call(
            functools.partial(join_kernel, step, step == steps - 1),
            shapes[step - 2],
            (total, exchange(total, "layer", 1 << (step - 1)), mine),
        )
    got = exchange(total, "layer", 1 << (steps - 1))
    own = chans // shares
    part = (depth * own * (width // HALF) + 2 * own, HALF)
    keep, *sends = call(
        functools.partial(grad_kernel, steps),
        (f32(*part),) * shares,
        (got, mine, guess, slope, patch, back_w),
    )
    adjoint_fixed, state_fixed = call(
        functools.partial(fixed_kernel, steps),
        (f32(*adjoint_guess.shape), f32(*state_guess.shape)),
        (keep, got, mine, adjoint_guess, state_guess),
    )
    both = exchange(sends[2], "dp", 3)
    chip = exchange(sends[1], "dp", 2)
    core = exchange(sends[0], "dp", 1)
    weight_grad, bias_grad = call(
        total_kernel,
        (f32(depth, chans // shares, width), f32(depth, chans // shares)),
        (keep, both, chip, core),
    )
    return (state_fixed, adjoint_fixed, weight_grad, bias_grad)


def solution(mesh):
    placed = (
        P("layer", "dp", None, None),
        P("layer", "dp", None, None),
        P("layer", None, None),
        P("layer", None),
    )
    return jax.shard_map(
        local,
        mesh=mesh,
        in_specs=placed,
        out_specs=(
            P("layer", "dp", None, None),
            P("layer", "dp", None, None),
            P("layer", "dp", None),
            P("layer", "dp"),
        ),
        check_vma=False,
    )
```

```python
import functools

import jax
import jax.numpy as jnp
from jax import lax
from jax.experimental import pallas as pl
from jax.experimental.pallas import tpu as pltpu
from jax.sharding import PartitionSpec as P

IMG = 16
HW = IMG * IMG
HALF = 128
TAPS = 9
STEP = 0.5
LIMIT = 32 * 1024 * 1024

VMEM = pl.BlockSpec(memory_space=pltpu.VMEM)
HBM = pl.BlockSpec(memory_space=pltpu.HBM)


def picked(low, high, source, from_high):
    return jnp.where(
        from_high,
        jnp.take_along_axis(high, source, axis=1, mode="promise_in_bounds"),
        jnp.take_along_axis(low, source, axis=1, mode="promise_in_bounds"),
    )


def lanes_of(values):
    lane = lax.broadcasted_iota(jnp.int32, (values.shape[0], HALF), 1)
    return lane // IMG, lane % IMG


def by_parity(values):
    line, col = lanes_of(values)
    low, high = values[:, :HALF], values[:, HALF:]
    half = IMG // 4
    return jnp.concatenate(
        [
            picked(low, high, (2 * (line % half) + odd) * IMG + col, line >= half)
            for odd in range(2)
        ],
        axis=1,
    )


def in_order(values):
    line, col = lanes_of(values)
    even, odd = values[:, :HALF], values[:, HALF:]
    return jnp.concatenate(
        [
            picked(even, odd, (half * (IMG // 4) + line // 2) * IMG + col, line % 2 == 1)
            for half in range(2)
        ],
        axis=1,
    )


def taps_of(values):
    even, odd = values[:, :HALF], values[:, HALF:]
    lane = lax.broadcasted_iota(jnp.int16, even.shape, 1)
    col = lane & (IMG - 1)
    cols = {-1: [col >= 1], 0: [], 1: [col < IMG - 1]}

    def turned(half, lines, right):
        by = lines * IMG + right
        if not by:
            return half
        tests = cols[right] + {-1: [lane >= IMG], 0: [], 1: [lane < HALF - IMG]}[lines]
        part = pltpu.roll(half, -by % HALF, 1)
        return jnp.where(functools.reduce(jnp.logical_and, tests), part, jnp.zeros_like(part))

    above, here, below = [], [], []
    for right in (-1, 0, 1):
        same = turned(even, 0, right), turned(odd, 0, right)
        above.append((turned(odd, -1, right), same[0]))
        here.append(same)
        below.append((same[1], turned(even, 1, right)))
    return jnp.concatenate(
        [jnp.concatenate(pair, axis=1) for pair in above + here + below], axis=0
    )


def permutation(chans):
    size = TAPS * chans
    row = lax.broadcasted_iota(jnp.int32, (size, size), 0)
    column = lax.broadcasted_iota(jnp.int32, (size, size), 1)
    tap = lax.div(row, chans)
    return jnp.where(column == (row - tap * chans) * TAPS + tap, 1.0, 0.0).astype(jnp.bfloat16)


def dot(a, b, dims):
    return lax.dot_general(a, b, (dims, ((), ())), preferred_element_type=jnp.float32)


def convolve(weight, values):
    return dot(weight, taps_of(values), ((1,), (0,)))


def relax_kernel(
    state_hbm,
    adj_hbm,
    w_hbm,
    bias_hbm,
    guess_ref,
    sent_ref,
    slope_ref,
    rounded_ref,
    back_w_ref,
    state_ref,
    adj_ref,
    w_ref,
    bias_ref,
    sems,
):
    copies = [
        pltpu.make_async_copy(src, dst, sems.at[k])
        for k, (src, dst) in enumerate(
            ((w_hbm, w_ref), (state_hbm, state_ref), (bias_hbm, bias_ref), (adj_hbm, adj_ref))
        )
    ]
    for copy in copies:
        copy.start()
    depth, chans, width = w_ref.shape
    perm = permutation(chans)
    eye = lax.broadcasted_iota(jnp.int32, (chans, chans), 0) == lax.broadcasted_iota(
        jnp.int32, (chans, chans), 1
    )
    for copy in copies:
        copy.wait()
    weights = w_ref[...].reshape(depth * chans, width)
    by_tap = dot(weights, perm, ((1,), (1,)))
    turned = dot(perm, weights, ((1,), (1,))).astype(jnp.bfloat16)
    middle = TAPS // 2 * chans
    start = by_parity(state_ref[0, 0])
    guess = by_parity(adj_ref[0, 0])
    guess_ref[...] = guess
    state = start
    gain = None
    slopes = []
    backs = []
    for n in range(depth):
        mine = slice(n * chans, (n + 1) * chans)
        bias = jnp.broadcast_to(bias_ref[n : n + 1, :], (chans, chans))
        bias, kc = (
            jnp.sum(jnp.where(eye, square, 0.0), axis=1, keepdims=True)
            for square in (bias, by_tap[mine, middle : middle + chans])
        )
        rounded = state.astype(jnp.bfloat16)
        rounded_ref[n] = rounded
        squash = jnp.tanh(convolve(by_tap[mine].astype(jnp.bfloat16), rounded) + bias)
        slope = STEP * (1.0 - squash * squash)
        slope_ref[n] = slope
        slopes.append(slope)
        state = state + STEP * squash
        factor = 1.0 + slope * kc
        gain = factor if gain is None else gain * factor
        back_w = jnp.concatenate(
            [turned[t * chans : (t + 1) * chans, mine] for t in reversed(range(TAPS))], axis=1
        )
        back_w_ref[n] = back_w
        backs.append(back_w)
    back = guess
    for n in reversed(range(depth)):
        back = back + convolve(backs[n], (back * slopes[n]).astype(jnp.bfloat16))
    place = lax.axis_index("layer")
    first = jnp.where(place == 0, 0.0, start)
    last = jnp.where(place == lax.axis_size("layer") - 1, 0.0, guess)
    sent_ref[0] = gain
    sent_ref[1] = state - gain * first
    sent_ref[2] = back - gain * last


def patch_kernel(rounded_ref, patch_ref):
    depth, chans, _ = rounded_ref.shape
    perm = permutation(chans)
    for n in range(depth):
        patch = taps_of(rounded_ref[n])
        patch_ref[n] = dot(perm, patch, ((0,), (0,))).astype(jnp.bfloat16)


def joined(bit, total, mine, got):
    gain, fwd, bwd = total
    pre_gain, pre, post_gain, post = mine
    got_gain, got_fwd, got_bwd = got
    total = (
        gain * got_gain,
        jnp.where(bit, gain * got_fwd + fwd, got_gain * fwd + got_fwd),
        jnp.where(bit, got_gain * bwd + got_bwd, gain * got_bwd + bwd),
    )
    mine = (
        jnp.where(bit, pre_gain * got_gain, pre_gain),
        jnp.where(bit, pre_gain * got_fwd + pre, pre),
        jnp.where(bit, post_gain, post_gain * got_gain),
        jnp.where(bit, post, post_gain * got_bwd + post),
    )
    return total, mine


def bit_of(axis, step):
    return lax.rem(lax.div(lax.axis_index(axis), 2**step), 2) == 1


def put_joined(step, final, total, mine, sent_ref, mine_out):
    for k in range(4):
        mine_out[k] = mine[k]
    if final:
        sent_ref[...] = jnp.where(bit_of("layer", step), total[2], total[1])
    else:
        for k in range(3):
            sent_ref[k] = total[k]


def four_kernel(final, own_ref, second_ref, first_ref, third_ref, sent_ref, mine_out):
    low, high = bit_of("layer", 0), bit_of("layer", 1)
    place = lax.rem(lax.axis_index("layer"), 4)
    maps = [
        tuple(ref[k] for k in range(3)) for ref in (own_ref, first_ref, second_ref, third_ref)
    ]
    for bit, mask in ((low, 1), (high, 2)):
        maps = [
            tuple(jnp.where(bit, b, a) for a, b in zip(maps[k], maps[k ^ mask])) for k in range(4)
        ]
    one, zero = jnp.ones_like(maps[0][0]), jnp.zeros_like(maps[0][0])
    gain, fwd, bwd = maps[0]
    pre_gain, pre, post_gain, post = one, zero, one, zero
    for k in range(4):
        here = maps[k]
        before = k < place
        pre = jnp.where(before, here[0] * pre + here[1], pre)
        pre_gain = jnp.where(before, pre_gain * here[0], pre_gain)
        if k:
            bwd = bwd + gain * here[2]
            fwd = here[0] * fwd + here[1]
            gain = gain * here[0]
    for k in reversed(range(4)):
        here = maps[k]
        after = k > place
        post = jnp.where(after, here[0] * post + here[2], post)
        post_gain = jnp.where(after, post_gain * here[0], post_gain)
    mine = (pre_gain, pre, post_gain, post)
    put_joined(2, final, (gain, fwd, bwd), mine, sent_ref, mine_out)


def join_kernel(step, final, total_ref, got_ref, mine_ref, sent_ref, mine_out):
    total, got = (tuple(ref[k] for k in range(3)) for ref in (total_ref, got_ref))
    mine = tuple(mine_ref[k] for k in range(4))
    total, mine = joined(bit_of("layer", step - 1), total, mine, got)
    put_joined(step, final, total, mine, sent_ref, mine_out)


def later_fixed(steps, got_ref, mine_ref):
    got = jnp.where(bit_of("layer", steps - 1), 0.0, mine_ref[2] * got_ref[...])
    return mine_ref[3] + got


def fixed_kernel(steps, _, got_ref, mine_ref, guess_ref, start_ref, adj_ref, state_ref):
    place = lax.axis_index("layer")
    adj = in_order(later_fixed(steps, got_ref, mine_ref))
    got = jnp.where(bit_of("layer", steps - 1), mine_ref[0] * got_ref[...], 0.0)
    state = in_order(mine_ref[1] + got)
    adj_ref[0, 0] = jnp.where(place == lax.axis_size("layer") - 1, guess_ref[0, 0], adj)
    state_ref[0, 0] = jnp.where(place == 0, start_ref[0, 0], state)


def grad_kernel(
    steps,
    got_ref,
    mine_ref,
    guess_ref,
    slope_ref,
    patch_ref,
    back_w_ref,
    *part_refs,
):
    depth, chans, rows = back_w_ref.shape
    shares = len(part_refs)
    own = chans // shares
    last = lax.axis_index("layer") == lax.axis_size("layer") - 1
    adj = jnp.where(last, guess_ref[...], later_fixed(steps, got_ref, mine_ref))
    full = rows // HALF * HALF
    block, base = depth * own, depth * own * (full // HALF)
    odd, high = bit_of("dp", 0), bit_of("dp", 1)

    def layer(n, adj):
        dz = adj * slope_ref[n]
        dzb = dz.astype(jnp.bfloat16)
        grad = dot(dzb, patch_ref[n], ((1,), (1,)))
        bias = jnp.broadcast_to(jnp.sum(dz, axis=1, keepdims=True), (chans, HALF))
        start = pl.multiple_of(n * own, own)
        rest = jnp.concatenate([grad[:, full:]] * depth, axis=1)
        both = jnp.concatenate([grad[:, :full], rest, bias], axis=1)
        parts = [both[k * own : (k + 1) * own] for k in range(shares)]
        parts = [jnp.where(odd, parts[i ^ 1], parts[i]) for i in range(shares)]
        parts = [jnp.where(high, parts[i ^ 2], parts[i]) for i in range(shares)]
        lane = lax.broadcasted_iota(jnp.int32, (own, HALF), 1)
        for part, ref in zip(parts, part_refs):
            for k in range(full // HALF):
                ref[pl.ds(k * block + start, own)] = part[:, k * HALF : (k + 1) * HALF]
            for k, here in ((0, lane // (rows - full) == n), (1, lane % depth == n)):
                tile = slice(base + k * own, base + (k + 1) * own)
                at = full + k * HALF
                ref[tile] = jnp.where(here, part[:, at : at + HALF], ref[tile])
        return dzb

    def behind(i, adj):
        n = depth - 1 - i
        return adj + convolve(back_w_ref[n], layer(n, adj))

    layer(0, lax.fori_loop(0, depth - 1, behind, adj))


def total_kernel(mine_ref, both_ref, chip_ref, core_ref, grad_ref, bias_ref):
    depth, own, width = grad_ref.shape
    total = (mine_ref[...] + core_ref[...]) + (chip_ref[...] + both_ref[...])
    eye = lax.broadcasted_iota(jnp.int32, (own, own), 0) == lax.broadcasted_iota(
        jnp.int32, (own, own), 1
    )
    full = width // HALF
    base, rest = depth * own * full, width - full * HALF
    for n in range(depth):
        pieces = [total[(k * depth + n) * own : (k * depth + n + 1) * own] for k in range(full)]
        pieces.append(total[base : base + own, n * rest : (n + 1) * rest])
        grad_ref[n] = jnp.concatenate(pieces, axis=1)
        column = jnp.broadcast_to(total[base + own : base + 2 * own, n : n + 1], (own, own))
        bias_ref[n : n + 1, :] = jnp.sum(jnp.where(eye, column, 0.0), axis=0, keepdims=True)


def call(kernel, out_shape, args, hbm_in=(), hbm_out=(), scratch=()):
    return pl.pallas_call(
        kernel,
        out_shape=out_shape,
        in_specs=[HBM if k in hbm_in else VMEM for k in range(len(args))],
        out_specs=[HBM if k in hbm_out else VMEM for k in range(len(out_shape))],
        scratch_shapes=list(scratch),
        compiler_params=pltpu.CompilerParams(vmem_limit_bytes=LIMIT),
        cost_estimate=pl.CostEstimate(flops=2**28, bytes_accessed=2**20, transcendentals=0),
    )(*(pltpu.with_memory_space_constraint(a, pltpu.HBM) if k in hbm_in else a for k, a in enumerate(args)))


def f32(*shape):
    return jax.ShapeDtypeStruct(shape, jnp.float32)


def bf16(*shape):
    return jax.ShapeDtypeStruct(shape, jnp.bfloat16)


def exchange(x, axis, mask):
    return lax.ppermute(x, axis, [(i, i ^ mask) for i in range(lax.axis_size(axis))])


def local(state_guess, adjoint_guess, conv_weight, conv_bias):
    depth, chans, width = conv_weight.shape
    shares = lax.axis_size("dp")
    steps = lax.axis_size("layer").bit_length() - 1
    args = (state_guess, adjoint_guess, conv_weight, conv_bias)
    guess, total, slope, rounded, back_w = call(
        relax_kernel,
        (
            f32(chans, HW),
            f32(3, chans, HW),
            f32(depth, chans, HW),
            bf16(depth, chans, HW),
            bf16(depth, chans, width),
        ),
        args,
        hbm_in=range(4),
        scratch=[pltpu.VMEM(a.shape, a.dtype) for a in args] + [pltpu.SemaphoreType.DMA((4,))],
    )
    (patch,) = call(patch_kernel, (bf16(depth, width, HW),), (rounded,))
    one = f32(chans, HW)
    shapes = [(f32(3, chans, HW), f32(4, chans, HW))] * (steps - 3) + [(one, f32(4, chans, HW))]
    total, mine = call(
        functools.partial(four_kernel, steps == 3),
        shapes[0],
        (total, *(exchange(total, "layer", mask) for mask in (2, 1, 3))),
    )
    for step in range(3, steps):
        total, mine = call(
            functools.partial(join_kernel, step, step == steps - 1),
            shapes[step - 2],
            (total, exchange(total, "layer", 1 << (step - 1)), mine),
        )
    got = exchange(total, "layer", 1 << (steps - 1))
    own = chans // shares
    part = (depth * own * (width // HALF) + 2 * own, HALF)
    keep, *sends = call(
        functools.partial(grad_kernel, steps),
        (f32(*part),) * shares,
        (got, mine, guess, slope, patch, back_w),
    )
    adjoint_fixed, state_fixed = call(
        functools.partial(fixed_kernel, steps),
        (f32(*adjoint_guess.shape), f32(*state_guess.shape)),
        (keep, got, mine, adjoint_guess, state_guess),
    )
    both = exchange(sends[2], "dp", 3)
    chip = exchange(sends[1], "dp", 2)
    core = exchange(sends[0], "dp", 1)
    weight_grad, bias_grad = call(
        total_kernel,
        (f32(depth, chans // shares, width), f32(depth, chans // shares)),
        (keep, both, chip, core),
    )
    return (state_fixed, adjoint_fixed, weight_grad, bias_grad)


def solution(mesh):
    placed = (
        P("layer", "dp", None, None),
        P("layer", "dp", None, None),
        P("layer", None, None),
        P("layer", None),
    )
    return jax.shard_map(
        local,
        mesh=mesh,
        in_specs=placed,
        out_specs=(
            P("layer", "dp", None, None),
            P("layer", "dp", None, None),
            P("layer", "dp", None),
            P("layer", "dp"),
        ),
        check_vma=False,
    )
```
